32 devices in a mesh: groups: 1, dp: 32 (over z, y, x, core).
Axes of the slice: x: 2, y: 2, z: 4, core: 2. Of those that a mesh axis runs over, the one named last changes fastest.
Arguments:
- queries: bfloat16 [256, 64, 576], P(('groups', 'dp')), may hold values from -40 to 40
- latent_cache: bfloat16 [256, 96, 576], P(('groups', 'dp')), may hold values from -6 to 6
- new_latent: bfloat16 [256, 576], P(('groups', 'dp')), may hold values from -6 to 6
- parents: int32 [256], P(('groups', 'dp')), may hold values from 0 to 255, as said below
- lengths: int32 [256], P(('groups', 'dp')), may hold values from 2 to 96, as said below
- expert_input: bfloat16 [256, 7168], P(('groups', 'dp')), may hold values from -6 to 6
- routed_experts: int32 [256, 2], P(('groups', 'dp')), may hold values from 0 to 3, all different within a row; in each aligned block of 8 rows (0 to 7, 8 to 15, ...) at most 8 rows name the same one
- route_weights: float32 [256, 2], P(('groups', 'dp')), may hold values from 0.2 to 2
- gate_weight: bfloat16 [32, 7168, 256], P('dp'), may hold values from -0.0625 to 0.0625
- up_weight: bfloat16 [32, 7168, 256], P('dp'), may hold values from -0.0625 to 0.0625
- down_weight: bfloat16 [32, 256, 7168], P('dp'), may hold values from -0.125 to 0.125
Outputs:
- attention: bfloat16 [256, 64, 512], P(('groups', 'dp'))
- expert_output: bfloat16 [256, 7168], P(('groups', 'dp'))
The draws below stay inside these ranges and needn't reach their ends.
Inputs may be any that keep to these rules, and one draw needn't show every extreme that they name: `parents`: the parent of survivor g (g counted within its beam-search group) lies within 8 slots of g in the same group. `lengths`: some survivor has length exactly 96. `routed_experts`: each row names 2 different experts; among the rows of one device no expert is named more than 8 times, and that many is reached.
All inputs are finite; a program needn't handle non-finite values.
Results may differ from the reference program's by a relative error of at most 0.0058.
Values may be sent and summed in bfloat16 or wider, within the bound.
No kernel may reach another device: no remote copies, remote signals or barrier semaphores. Data moves between devices by JAX's collectives and lax.ppermute only.
A program may use at most 128 MiB of HBM per device.

```python
import math
import jax
import jax.numpy as jnp
import numpy as np
from jax import lax

D = 7168
FF_E = 2048
KV = 512
ROPE = 64
H = 64
HID_DEV = 256
TOP = 2
B_DEV = 8
L = 96
SUB = 8
EXPERTS = 4
CAP = 8
BEAMS = 256
N_DP = 32


def draw_queries(key, part):
    key = jax.random.fold_in(key, 21)
    values = jax.random.truncated_normal(key, -6.0, 6.0, (BEAMS, H, KV + ROPE), jnp.float32)
    return values.astype(jnp.bfloat16)


def draw_latent_cache(key, part):
    key = jax.random.fold_in(key, 22)
    values = jax.random.truncated_normal(key, -6.0, 6.0, (BEAMS, L, KV + ROPE), jnp.float32)
    return values.astype(jnp.bfloat16)


def draw_parents(key, part):
    key = jax.random.fold_in(key, 23)
    slots = jnp.arange(BEAMS, dtype=jnp.int32)
    offsets = jax.random.randint(key, (BEAMS,), -B_DEV, B_DEV + 1, dtype=jnp.int32)
    return jnp.clip(slots + offsets, 0, BEAMS - 1).astype(jnp.int32)


def draw_lengths(key, part):
    key = jax.random.fold_in(key, 24)
    first_key, second_key = jax.random.split(key)
    values = jax.random.randint(first_key, (BEAMS,), 2, L + 1, dtype=jnp.int32)
    longest = jax.random.randint(second_key, (), 0, BEAMS, dtype=jnp.int32)
    return values.at[longest].set(L).astype(jnp.int32)


def shard_levels(rng, dims, cuts, low, high):
    def one(dim, parts):
        draws = jax.random.uniform(jax.random.fold_in(jax.random.fold_in(rng, 6), dim), (parts,), jnp.float32, low / len(cuts), high / len(cuts))
        return jnp.repeat(jnp.exp(draws), dims[dim] // parts).reshape((-1,) + (1,) * (len(dims) - dim - 1))

    gain = one(*cuts[0])
    for cut in cuts[1:]:
        gain = gain * one(*cut)
    return gain


def assign_block(rng, own, number, rows, amount, top, most, skew):
    order = jax.random.permutation(rng, amount)
    heavy_load, common = portions_of(amount, rows * top, most, skew, True), portions_of(amount, rows * top, most, skew, False)
    places = jnp.arange(amount)

    def named(sizes, turn):
        used = int((sizes > 0).sum())
        fixed = max(1, used // 4)
        shifted = fixed + (places - fixed + turn * (used - fixed)) % max(1, amount - fixed)
        return jnp.zeros((amount,), jnp.int32).at[order[jnp.where(places < fixed, places, shifted)]].set(jnp.asarray(sizes, jnp.int32))

    sizes = jnp.where(number % 4 == 0, named(heavy_load, number // 4), named(common, number - number // 4 - 1))
    mixed = jax.random.permutation(jax.random.fold_in(own, 3), amount)
    donor, receiver = mixed[0:amount // 2 * 2:2], mixed[1:amount // 2 * 2:2]
    slack = jnp.minimum(sizes[donor] - 1, most - sizes[receiver]) // 2
    slack = jnp.where((donor == order[0]) | (receiver == order[0]) | (sizes[receiver] == 0), 0, jnp.maximum(slack, 0))
    shifted = jax.random.randint(jax.random.fold_in(own, 4), (amount // 2,), 0, 1 << 20) % (slack + 1)
    sizes = sizes.at[donor].add(-shifted).at[receiver].add(shifted)
    labels = jnp.searchsorted(jnp.cumsum(sizes), jnp.arange(rows * top), side="right").astype(jnp.int32)
    listing = labels.reshape(top, rows).T
    listing = listing[jax.random.permutation(jax.random.fold_in(own, 1), rows)]
    turn = jax.random.randint(jax.random.fold_in(own, 2), (rows, 1), 0, top)
    return jnp.take_along_axis(listing, (jnp.arange(top)[None, :] + turn) % top, axis=1)


def portions_of(number_of, total, most, skew, full):
    loads = [(1 << 20) // math.isqrt(rank ** skew) + 1 for rank in range(1, number_of + 1)]
    largest = most if full else min(most, max(-(-total // number_of), total * loads[0] // sum(loads)))
    least = 1 if total - largest >= number_of - 1 else 0
    holding, rest = [largest] + [least] * (number_of - 1), total - largest - least * (number_of - 1)
    while rest > 0:
        free = [i for i in range(1, number_of) if holding[i] < largest] or [i for i in range(1, number_of) if holding[i] < most]
        whole, budget = sum([loads[i] for i in free]), rest
        for i in free:
            extra = min(most - holding[i], max(1, budget * loads[i] // whole), rest)
            holding[i] = holding[i] + extra
            rest = rest - extra
    return np.array(holding)


def noise(stream_key, shape, spread, most, pieces=(), kind=jnp.bfloat16):
    values = spread * jax.random.normal(stream_key, shape, jnp.float32)
    if pieces:
        values = values * shard_levels(stream_key, shape, pieces, -0.22, 0.18)
    return jnp.clip(values, -most, most).astype(kind)


def setup_inputs(seed: int = 0, part: int = 0) -> dict:
    arg_keys = jax.random.split(jax.random.key(seed), 12)
    part_splits = jax.random.split(jax.random.fold_in(arg_keys[11], part), 12)
    queries = draw_queries(jax.random.fold_in(jax.random.fold_in(arg_keys[11], part), 71), part)
    latent_cache = draw_latent_cache(jax.random.fold_in(jax.random.fold_in(arg_keys[11], part), 71), part)
    new_latent = noise(part_splits[2], (BEAMS, KV + ROPE), 1.0, 6.0, ((0, 32),))
    parents = draw_parents(jax.random.fold_in(jax.random.fold_in(arg_keys[11], part), 71), part)
    lengths = draw_lengths(jax.random.fold_in(jax.random.fold_in(arg_keys[11], part), 71), part)
    expert_input = noise(part_splits[5], (BEAMS, D), 1.0, 6.0, ((0, 32),))
    routed_experts_keys = jax.random.split(jax.random.fold_in(part_splits[6], 1), BEAMS // B_DEV)
    routed_experts_turns = jax.random.permutation(jax.random.fold_in(part_splits[6], 3), BEAMS // B_DEV)
    routed_experts = jax.vmap(lambda own, number: assign_block(jax.random.fold_in(part_splits[6], 2), own, number, B_DEV, EXPERTS, TOP, CAP, 2))(routed_experts_keys, routed_experts_turns).reshape((BEAMS, TOP))
    route_weights = jnp.clip(jnp.exp(math.log(2.0) - 2.3025851 * jax.random.uniform(part_splits[7], (BEAMS, TOP), jnp.float32) ** shard_levels(part_splits[7], (BEAMS, TOP), ((0, 32),), -0.2, 0.2)), 0.2, 2.0)
    gate_weight = noise(arg_keys[8], (N_DP, D, HID_DEV), D ** -0.5, 0.0625, ((0, 32),))
    up_weight = noise(arg_keys[9], (N_DP, D, HID_DEV), D ** -0.5, 0.0625, ((0, 32),))
    down_weight = noise(arg_keys[10], (N_DP, HID_DEV, D), FF_E ** -0.5, 0.125, ((0, 32),))
    return dict(queries=queries, latent_cache=latent_cache, new_latent=new_latent, parents=parents, lengths=lengths, expert_input=expert_input, routed_experts=routed_experts, route_weights=route_weights, gate_weight=gate_weight, up_weight=up_weight, down_weight=down_weight)


score_scale = 192.0 ** -0.5


def reference(queries, latent_cache, new_latent, parents, lengths, expert_input, routed_experts, route_weights, gate_weight, up_weight, down_weight):
    positions = jnp.arange(L, dtype=jnp.int32)

    def attend_beam(packed):
        beam_query, parent_slot, newest_row, beam_length = packed
        parent_rows = lax.dynamic_index_in_dim(latent_cache, parent_slot, 0, keepdims=False)
        child_cache = jnp.where((positions < beam_length - 1)[:, None], parent_rows, jnp.zeros_like(parent_rows))
        child_cache = jnp.where((positions == beam_length - 1)[:, None], newest_row[None, :], child_cache)
        scores = jnp.einsum('hc,lc->hl', beam_query.astype(jnp.float32), child_cache.astype(jnp.float32)) * score_scale
        scores = jnp.where((positions < beam_length)[None, :], scores, -jnp.inf)
        row_max = jnp.max(scores, axis=1, keepdims=True)
        expons = jnp.exp(scores - row_max)
        probs = (expons / jnp.sum(expons, axis=1, keepdims=True)).astype(jnp.bfloat16)
        mixed = jnp.einsum('hl,lc->hc', probs.astype(jnp.float32), child_cache[:, :KV].astype(jnp.float32))
        return mixed.astype(jnp.bfloat16)

    attention = lax.map(attend_beam, (queries, parents, new_latent, lengths))

    flat_experts = routed_experts.reshape(-1)
    onehot = (flat_experts[:, None] == jnp.arange(EXPERTS, dtype=jnp.int32)[None, :]).astype(jnp.int32)
    position = jnp.sum((jnp.cumsum(onehot, axis=0) - onehot) * onehot, axis=1).astype(jnp.int32)
    row_count = N_DP * CAP
    token_rows = jnp.repeat(expert_input, TOP, axis=0)
    buffer = jnp.zeros((EXPERTS, row_count, D), jnp.bfloat16).at[flat_experts, position].set(token_rows)

    def run_expert(packed):
        block_rows, gate_blocks, up_blocks, down_blocks = packed
        total = jnp.zeros((row_count, D), jnp.float32)
        for slice_index in range(SUB):
            gate_value = jnp.dot(block_rows, gate_blocks[slice_index], preferred_element_type=jnp.float32)
            up_value = jnp.dot(block_rows, up_blocks[slice_index], preferred_element_type=jnp.float32)
            hidden = (jax.nn.silu(gate_value) * up_value).astype(jnp.bfloat16)
            part = jnp.dot(hidden, down_blocks[slice_index], preferred_element_type=jnp.float32).astype(jnp.bfloat16)
            total = total + part.astype(jnp.float32)
        return total

    expert_value = lax.map(run_expert, (buffer, gate_weight.reshape(EXPERTS, SUB, D, HID_DEV), up_weight.reshape(EXPERTS, SUB, D, HID_DEV), down_weight.reshape(EXPERTS, SUB, HID_DEV, D)))
    picked = expert_value[flat_experts, position].reshape(BEAMS, TOP, D)
    expert_output = jnp.sum(route_weights[:, :, None] * picked, axis=1).astype(jnp.bfloat16)
    return attention, expert_output
```

```python
import jax
import jax.numpy as jnp
from jax import lax
from jax.sharding import PartitionSpec as P

FF_E = 2048
KV = 512


score_scale = 192.0 ** (-0.5)


def padded_2(value, sides, width):
    for axis, dim in sides:
        peers, length = (lax.axis_size(axis), value.shape[dim])
        up = [(i, (i + 1) % peers) for i in range(peers - 1)]
        down = [(j, i) for i, j in up]
        last = lax.slice_in_dim(value, length - width, length, axis=dim)
        first = lax.slice_in_dim(value, 0, width, axis=dim)
        before = lax.ppermute(last, axis, up)
        after = lax.ppermute(first, axis, down)
        value = jnp.concatenate([before, value, after], axis=dim)
    return value


def pair_slots(route_rows, expert_count, capacity):
    flat_experts = route_rows.reshape(-1)
    onehot = (flat_experts[:, None] == jnp.arange(expert_count, dtype=jnp.int32)[None, :]).astype(
        jnp.int32
    )
    position = jnp.sum((jnp.cumsum(onehot, axis=0) - onehot) * onehot, axis=1)
    return (flat_experts * capacity + position).astype(jnp.int32).reshape(route_rows.shape)


def attend(queries, latent_cache, new_latent, parents, lengths):
    beam_count = queries.shape[0]
    my_rank = lax.axis_index("dp")
    positions = jnp.arange(latent_cache.shape[1], dtype=jnp.int32)
    first_slot = (my_rank - 1) * beam_count
    padded = padded_2(latent_cache, (("dp", 0),), beam_count)
    parent_rows = jnp.take(padded, parents - first_slot, axis=0)
    child_cache = jnp.where(
        (positions[None, :] < lengths[:, None] - 1)[:, :, None],
        parent_rows,
        jnp.zeros_like(parent_rows),
    )
    child_cache = jnp.where(
        (positions[None, :] == lengths[:, None] - 1)[:, :, None],
        new_latent[:, None, :],
        child_cache,
    )
    scores = (
        jnp.einsum("bhc,blc->bhl", queries, child_cache, preferred_element_type=jnp.float32)
        * score_scale
    )
    scores = jnp.where((positions[None, :] < lengths[:, None])[:, None, :], scores, -jnp.inf)
    row_max = jnp.max(scores, axis=2, keepdims=True)
    expons = jnp.exp(scores - row_max)
    probs = (expons / jnp.sum(expons, axis=2, keepdims=True)).astype(jnp.bfloat16)
    mixed = jnp.einsum(
        "bhl,blc->bhc", probs, child_cache[:, :, :KV], preferred_element_type=jnp.float32
    )
    return mixed.astype(jnp.bfloat16)


def routed(expert_input, routed_experts, route_weights, gate_weight, up_weight, down_weight):
    beam_count, width = expert_input.shape
    devices = lax.axis_size("dp")
    slices = FF_E // gate_weight.shape[2]
    expert_count = devices // slices
    route_count = routed_experts.shape[1]
    capacity = min(beam_count, max(2, 2 * beam_count * route_count // expert_count))
    planes = [[e * slices + s for s in range(slices)] for e in range(expert_count)]
    columns = [[e * slices + s for e in range(expert_count)] for s in range(slices)]
    slots = (
        pair_slots(routed_experts, expert_count, capacity)
        if capacity < beam_count
        else routed_experts * capacity + jnp.arange(beam_count, dtype=jnp.int32)[:, None]
    )
    matches = (
        slots[:, :, None] == jnp.arange(expert_count * capacity, dtype=jnp.int32)
    ).astype(jnp.float32)
    if capacity < beam_count:
        selector = jnp.sum(matches, axis=1).T.astype(jnp.bfloat16)
        chosen = jnp.dot(selector, expert_input, preferred_element_type=jnp.float32)
        chosen = chosen.astype(jnp.bfloat16).reshape(expert_count, capacity, width)
        column = lax.all_to_all(
            chosen, "dp", split_axis=0, concat_axis=0, axis_index_groups=columns, tiled=True
        ).reshape(expert_count * capacity, width)
    else:
        column = lax.all_gather(
            expert_input, "dp", axis=0, axis_index_groups=columns, tiled=True
        )
    rows = lax.all_gather(column, "dp", axis=0, axis_index_groups=planes, tiled=True)
    gate_value = jnp.dot(rows, gate_weight[0], preferred_element_type=jnp.float32)
    up_value = jnp.dot(rows, up_weight[0], preferred_element_type=jnp.float32)
    hidden = (jax.nn.silu(gate_value) * up_value).astype(jnp.bfloat16)
    part = jnp.dot(hidden, down_weight[0], preferred_element_type=jnp.float32).astype(jnp.bfloat16)
    value = lax.psum_scatter(
        part, "dp", scatter_dimension=0, axis_index_groups=planes, tiled=True
    )
    returned = lax.all_to_all(
        value.reshape(expert_count, capacity, width),
        "dp",
        split_axis=0,
        concat_axis=0,
        axis_index_groups=columns,
        tiled=True,
    ).reshape(expert_count * capacity, width)
    mixing = jnp.sum(route_weights[:, :, None] * matches, axis=1)
    return jnp.dot(
        mixing,
        returned.astype(jnp.float32),
        precision=lax.Precision.HIGHEST,
        preferred_element_type=jnp.float32,
    ).astype(jnp.bfloat16)


def body(
    queries,
    latent_cache,
    new_latent,
    parents,
    lengths,
    expert_input,
    routed_experts,
    route_weights,
    gate_weight,
    up_weight,
    down_weight,
):
    attention = attend(queries, latent_cache, new_latent, parents, lengths)
    expert_output = routed(
        expert_input, routed_experts, route_weights, gate_weight, up_weight, down_weight
    )
    return (attention, expert_output)


def solution(mesh):
    in_specs = (
        P(("groups", "dp"), None, None),
        P(("groups", "dp"), None, None),
        P(("groups", "dp"), None),
        P(("groups", "dp")),
        P(("groups", "dp")),
        P(("groups", "dp"), None),
        P(("groups", "dp"), None),
        P(("groups", "dp"), None),
        P("dp", None, None),
        P("dp", None, None),
        P("dp", None, None),
    )
    out_specs = (P(("groups", "dp"), None, None), P(("groups", "dp"), None))
    return jax.shard_map(body, mesh=mesh, in_specs=in_specs, out_specs=out_specs, check_vma=False)
```

```python
import jax
import jax.numpy as jnp
from jax import lax
from jax.sharding import PartitionSpec as P

FF_E = 2048
KV = 512


score_scale = 192.0 ** (-0.5)


def padded_2(value, sides, width):
    for axis, dim in sides:
        peers, length = (lax.axis_size(axis), value.shape[dim])
        up = [(i, (i + 1) % peers) for i in range(peers - 1)]
        down = [(j, i) for i, j in up]
        last = lax.slice_in_dim(value, length - width, length, axis=dim)
        first = lax.slice_in_dim(value, 0, width, axis=dim)
        before = lax.ppermute(last, axis, up)
        after = lax.ppermute(first, axis, down)
        value = jnp.concatenate([before, value, after], axis=dim)
    return value


def pair_slots(route_rows, expert_count, capacity):
    flat_experts = route_rows.reshape(-1)
    onehot = (flat_experts[:, None] == jnp.arange(expert_count, dtype=jnp.int32)[None, :]).astype(
        jnp.int32
    )
    position = jnp.sum((jnp.cumsum(onehot, axis=0) - onehot) * onehot, axis=1)
    return (flat_experts * capacity + position).astype(jnp.int32).reshape(route_rows.shape)


def attend(queries, latent_cache, new_latent, parents, lengths):
    beam_count = queries.shape[0]
    my_rank = lax.axis_index("dp")
    positions = jnp.arange(latent_cache.shape[1], dtype=jnp.int32)
    first_slot = (my_rank - 1) * beam_count
    padded = padded_2(latent_cache, (("dp", 0),), beam_count)
    parent_rows = jnp.take(padded, parents - first_slot, axis=0)
    child_cache = jnp.where(
        (positions[None, :] < lengths[:, None] - 1)[:, :, None],
        parent_rows,
        jnp.zeros_like(parent_rows),
    )
    child_cache = jnp.where(
        (positions[None, :] == lengths[:, None] - 1)[:, :, None],
        new_latent[:, None, :],
        child_cache,
    )
    scores = (
        jnp.einsum("bhc,blc->bhl", queries, child_cache, preferred_element_type=jnp.float32)
        * score_scale
    )
    scores = jnp.where((positions[None, :] < lengths[:, None])[:, None, :], scores, -jnp.inf)
    row_max = jnp.max(scores, axis=2, keepdims=True)
    expons = jnp.exp(scores - row_max)
    probs = (expons / jnp.sum(expons, axis=2, keepdims=True)).astype(jnp.bfloat16)
    mixed = jnp.einsum(
        "bhl,blc->bhc", probs, child_cache[:, :, :KV], preferred_element_type=jnp.float32
    )
    return mixed.astype(jnp.bfloat16)


def swapped(value, partner):
    peers = lax.axis_size("dp")
    return lax.ppermute(value, "dp", [(i, partner(i)) for i in range(peers)])


def experts(rows, gate_weight, up_weight, down_weight):
    gate_value = jnp.dot(rows, gate_weight[0], preferred_element_type=jnp.float32)
    up_value = jnp.dot(rows, up_weight[0], preferred_element_type=jnp.float32)
    hidden = (jax.nn.silu(gate_value) * up_value).astype(jnp.bfloat16)
    return jnp.dot(hidden, down_weight[0], preferred_element_type=jnp.float32).astype(jnp.bfloat16)


def added(values):
    total = values[0].astype(jnp.float32)
    for value in values[1:]:
        total = total + value.astype(jnp.float32)
    return total


def routed(expert_input, routed_experts, route_weights, gate_weight, up_weight, down_weight):
    beam_count, width = expert_input.shape
    devices = lax.axis_size("dp")
    slices = FF_E // gate_weight.shape[2]
    expert_count = devices // slices
    chips = slices // 2
    route_count = routed_experts.shape[1]
    capacity = min(beam_count, max(2, 2 * beam_count * route_count // expert_count))
    dense = capacity == beam_count
    mine = lax.axis_index("dp") // slices

    turns = jnp.arange(expert_count, dtype=jnp.int32)
    targets = (mine + turns) % expert_count
    if dense:
        slots = routed_experts * capacity + jnp.arange(beam_count, dtype=jnp.int32)[:, None]
    else:
        slots = pair_slots(routed_experts, expert_count, capacity)
    wanted = targets[:, None] * capacity + jnp.arange(capacity, dtype=jnp.int32)
    matches = (slots[:, :, None] == wanted.reshape(-1)).astype(jnp.float32)
    mixing = jnp.sum(route_weights[:, :, None] * matches, axis=1)
    if dense:
        blocks = [expert_input] * expert_count
    else:
        selector = jnp.sum(matches, axis=1).T.astype(jnp.bfloat16)
        chosen = jnp.dot(selector, expert_input, preferred_element_type=jnp.float32)
        blocks = list(chosen.astype(jnp.bfloat16).reshape(expert_count, capacity, width))

    def ahead(r):
        return lambda i: (i + r * slices) % devices

    def beside(j):
        return lambda i: i ^ (2 * j)

    def twin(i):
        return i ^ 1

    near = [blocks[0]]
    far = jnp.concatenate([swapped(blocks[r], ahead(r)) for r in range(1, expert_count)])
    near = jnp.concatenate(near + [swapped(blocks[0], beside(j)) for j in range(1, chips)])
    near_twin = swapped(near, twin)
    far = jnp.concatenate([far] + [swapped(far, beside(j)) for j in range(1, chips)])
    far_twin = swapped(far, twin)
    near_rows, far_rows = near.shape[0], far.shape[0]
    rows = jnp.concatenate([near, near_twin, far, far_twin])
    part = experts(rows, gate_weight, up_weight, down_weight)
    at = 2 * near_rows
    near, near_twin = part[:near_rows], part[near_rows:at]
    far, far_twin = part[at : at + far_rows], part[at + far_rows :]

    def collected(held, twin_rows):
        held = added([held, swapped(twin_rows, twin)]).astype(jnp.bfloat16)
        pieces = held.reshape(chips, held.shape[0] // chips, width)
        return added(
            [pieces[0]] + [swapped(pieces[j], beside(j)) for j in range(1, chips)]
        )

    far = collected(far, far_twin).astype(jnp.bfloat16)
    far = far.reshape(expert_count - 1, capacity, width)
    values = [swapped(far[r - 1], ahead(-r)) for r in range(1, expert_count)]
    values = [collected(near, near_twin)] + values
    if dense:
        total = sum(
            jnp.sum(
                mixing.reshape(beam_count, expert_count, capacity)[:, r], axis=1, keepdims=True
            )
            * values[r].astype(jnp.float32)
            for r in range(expert_count)
        )
    else:
        total = jnp.dot(
            mixing,
            jnp.concatenate(values).astype(jnp.float32),
            precision=lax.Precision.HIGHEST,
            preferred_element_type=jnp.float32,
        )
    return total.astype(jnp.bfloat16)


def body(
    queries,
    latent_cache,
    new_latent,
    parents,
    lengths,
    expert_input,
    routed_experts,
    route_weights,
    gate_weight,
    up_weight,
    down_weight,
):
    attention = attend(queries, latent_cache, new_latent, parents, lengths)
    expert_output = routed(
        expert_input, routed_experts, route_weights, gate_weight, up_weight, down_weight
    )
    return (attention, expert_output)


def solution(mesh):
    in_specs = (
        P(("groups", "dp"), None, None),
        P(("groups", "dp"), None, None),
        P(("groups", "dp"), None),
        P(("groups", "dp")),
        P(("groups", "dp")),
        P(("groups", "dp"), None),
        P(("groups", "dp"), None),
        P(("groups", "dp"), None),
        P("dp", None, None),
        P("dp", None, None),
        P("dp", None, None),
    )
    out_specs = (P(("groups", "dp"), None, None), P(("groups", "dp"), None))
    return jax.shard_map(body, mesh=mesh, in_specs=in_specs, out_specs=out_specs, check_vma=False)
```

```python
import jax
import jax.numpy as jnp
from jax import lax
from jax.experimental import pallas as pl
from jax.experimental.pallas import tpu as pltpu
from jax.sharding import PartitionSpec as P

FF_E = 2048
KV = 512


score_scale = 192.0 ** (-0.5)


def pair_slots(route_rows, expert_count, capacity):
    flat_experts = route_rows.reshape(-1)
    onehot = (flat_experts[:, None] == jnp.arange(expert_count, dtype=jnp.int32)[None, :]).astype(
        jnp.int32
    )
    position = jnp.sum((jnp.cumsum(onehot, axis=0) - onehot) * onehot, axis=1)
    return (flat_experts * capacity + position).astype(jnp.int32).reshape(route_rows.shape)


def attend(queries, before, latent_cache, after, new_latent, parents, lengths):
    beam_count = queries.shape[0]
    my_rank = lax.axis_index("dp")
    positions = jnp.arange(latent_cache.shape[1], dtype=jnp.int32)
    first_slot = (my_rank - 1) * beam_count
    padded = jnp.concatenate([before, latent_cache, after], axis=0)
    parent_rows = jnp.take(padded, parents - first_slot, axis=0)
    child_cache = jnp.where(
        (positions[None, :] < lengths[:, None] - 1)[:, :, None],
        parent_rows,
        jnp.zeros_like(parent_rows),
    )
    child_cache = jnp.where(
        (positions[None, :] == lengths[:, None] - 1)[:, :, None],
        new_latent[:, None, :],
        child_cache,
    )
    scores = (
        jnp.einsum("bhc,blc->bhl", queries, child_cache, preferred_element_type=jnp.float32)
        * score_scale
    )
    scores = jnp.where((positions[None, :] < lengths[:, None])[:, None, :], scores, -jnp.inf)
    row_max = jnp.max(scores, axis=2, keepdims=True)
    expons = jnp.exp(scores - row_max)
    probs = (expons / jnp.sum(expons, axis=2, keepdims=True)).astype(jnp.bfloat16)
    mixed = jnp.einsum(
        "bhl,blc->bhc", probs, child_cache[:, :, :KV], preferred_element_type=jnp.float32
    )
    return mixed.astype(jnp.bfloat16)


def swapped(value, partner):
    peers = lax.axis_size("dp")
    return lax.ppermute(value, "dp", [(i, partner(i)) for i in range(peers)])


def step_width(width):
    return max(w for w in (128, 256, 512, 1024) if width % w == 0)


def expert_kernel(steps, blocks, *refs):
    rows, refs = refs[:blocks], refs[blocks:]
    gate_ref, up_ref, down_ref = refs[:3]
    out_refs, (gate_sum, up_sum, hidden) = refs[3 : 3 + blocks], refs[3 + blocks :]
    height = rows[0].shape[0]
    step = pl.program_id(0)

    @pl.when(step < steps)
    def _():
        value = jnp.concatenate([ref[...] for ref in rows], axis=0)
        gate = jnp.dot(value, gate_ref[0], preferred_element_type=jnp.float32)
        up = jnp.dot(value, up_ref[0], preferred_element_type=jnp.float32)
        first = step == 0
        gate_sum[...] = gate + jnp.where(first, 0.0, gate_sum[...])
        up_sum[...] = up + jnp.where(first, 0.0, up_sum[...])

    @pl.when(step == steps - 1)
    def _():
        gate = gate_sum[...]
        hidden[...] = (gate / (1.0 + jnp.exp(-gate)) * up_sum[...]).astype(hidden.dtype)

    @pl.when(step >= steps)
    def _():
        part = jnp.dot(hidden[...], down_ref[0], preferred_element_type=jnp.float32)
        for i, ref in enumerate(out_refs):
            ref[...] = part[i * height : (i + 1) * height].astype(ref.dtype)


def experts(rows, gate_weight, up_weight, down_weight):
    height, width = rows[0].shape
    units = gate_weight.shape[2]
    wide = step_width(width)
    steps = width // wide
    total = len(rows) * height

    def inward(k):
        return jnp.minimum(k, steps - 1)

    def outward(k):
        return jnp.maximum(k - steps, 0)

    return pl.pallas_call(
        lambda *refs: expert_kernel(steps, len(rows), *refs),
        grid=(2 * steps,),
        in_specs=[pl.BlockSpec((height, wide), lambda k: (0, inward(k)))] * len(rows)
        + [pl.BlockSpec((1, wide, units), lambda k: (0, inward(k), 0))] * 2
        + [pl.BlockSpec((1, units, wide), lambda k: (0, 0, outward(k)))],
        out_specs=[pl.BlockSpec((height, wide), lambda k: (0, outward(k)))] * len(rows),
        out_shape=[jax.ShapeDtypeStruct((height, width), jnp.bfloat16)] * len(rows),
        scratch_shapes=[
            pltpu.VMEM((total, units), jnp.float32),
            pltpu.VMEM((total, units), jnp.float32),
            pltpu.VMEM((total, units), jnp.bfloat16),
        ],
        compiler_params=pltpu.CompilerParams(vmem_limit_bytes=24 * 2**20),
        cost_estimate=pl.CostEstimate(
            flops=6 * total * width * units,
            bytes_accessed=6 * width * units + 4 * total * width,
            transcendentals=total * units,
        ),
    )(*rows, gate_weight, up_weight, down_weight)


def added(values):
    total = values[0].astype(jnp.float32)
    for value in values[1:]:
        total = total + value.astype(jnp.float32)
    return total


def body(
    queries,
    latent_cache,
    new_latent,
    parents,
    lengths,
    expert_input,
    routed_experts,
    route_weights,
    gate_weight,
    up_weight,
    down_weight,
):
    beam_count, width = expert_input.shape
    devices = lax.axis_size("dp")
    slices = FF_E // gate_weight.shape[2]
    expert_count = devices // slices
    chips = slices // 2
    route_count = routed_experts.shape[1]
    capacity = min(beam_count, max(2, 2 * beam_count * route_count // expert_count))
    dense = capacity == beam_count
    mine = lax.axis_index("dp") // slices

    turns = jnp.arange(expert_count, dtype=jnp.int32)
    targets = (mine + turns) % expert_count
    if dense:
        slots = routed_experts * capacity + jnp.arange(beam_count, dtype=jnp.int32)[:, None]
    else:
        slots = pair_slots(routed_experts, expert_count, capacity)
    wanted = targets[:, None] * capacity + jnp.arange(capacity, dtype=jnp.int32)
    matches = (slots[:, :, None] == wanted.reshape(-1)).astype(jnp.float32)
    mixing = jnp.sum(route_weights[:, :, None] * matches, axis=1)
    if dense:
        blocks = [expert_input] * expert_count
    else:
        selector = jnp.sum(matches, axis=1).T.astype(jnp.bfloat16)
        chosen = jnp.dot(selector, expert_input, preferred_element_type=jnp.float32)
        blocks = list(chosen.astype(jnp.bfloat16).reshape(expert_count, capacity, width))

    def ahead(r):
        return lambda i: (i + r * slices) % devices

    def beside(j):
        return lambda i: i ^ (2 * j)

    def twin(i):
        return i ^ 1

    column = jnp.concatenate(
        [blocks[0]] + [swapped(blocks[r], ahead(r)) for r in range(1, expert_count)]
    )
    before = lax.ppermute(latent_cache, "dp", [(i, i + 1) for i in range(devices - 1)])
    held = [column] + [swapped(column, beside(j)) for j in range(1, chips)]
    *held, latent_again = lax.optimization_barrier((*held, latent_cache))
    after = lax.ppermute(latent_again, "dp", [(i + 1, i) for i in range(devices - 1)])
    held = held + [swapped(value, twin) for value in held]
    parts = experts(held, gate_weight, up_weight, down_weight)

    own, others = parts[:chips], parts[chips:]
    joined = {}
    for j in list(range(1, chips)) + [0]:
        joined[j] = added([own[j], swapped(others[j], twin)]).astype(jnp.bfloat16)
    arrived = [swapped(joined[j], beside(j)) for j in range(1, chips)]
    value = added([joined[0]] + arrived).reshape(expert_count, capacity, width)
    values = [value[0]] + [
        swapped(value[r].astype(jnp.bfloat16), ahead(-r)) for r in range(1, expert_count)
    ]
    if dense:
        weights = jnp.sum(mixing.reshape(beam_count, expert_count, capacity), axis=2)
        total = sum(
            weights[:, r : r + 1] * values[r].astype(jnp.float32) for r in range(expert_count)
        )
    else:
        total = jnp.dot(
            mixing,
            jnp.concatenate([v.astype(jnp.float32) for v in values]),
            precision=lax.Precision.HIGHEST,
            preferred_element_type=jnp.float32,
        )
    attention = attend(queries, before, latent_cache, after, new_latent, parents, lengths)
    return (attention, total.astype(jnp.bfloat16))


def solution(mesh):
    in_specs = (
        P(("groups", "dp"), None, None),
        P(("groups", "dp"), None, None),
        P(("groups", "dp"), None),
        P(("groups", "dp")),
        P(("groups", "dp")),
        P(("groups", "dp"), None),
        P(("groups", "dp"), None),
        P(("groups", "dp"), None),
        P("dp", None, None),
        P("dp", None, None),
        P("dp", None, None),
    )
    out_specs = (P(("groups", "dp"), None, None), P(("groups", "dp"), None))
    return jax.shard_map(body, mesh=mesh, in_specs=in_specs, out_specs=out_specs, check_vma=False)
```

```python
import jax
import jax.numpy as jnp
from jax import lax
from jax.experimental import pallas as pl
from jax.experimental.pallas import tpu as pltpu
from jax.sharding import PartitionSpec as P

FF_E = 2048
KV = 512


score_scale = 192.0 ** (-0.5)


def pair_slots(route_rows, expert_count, capacity):
    flat_experts = route_rows.reshape(-1)
    onehot = (flat_experts[:, None] == jnp.arange(expert_count, dtype=jnp.int32)[None, :]).astype(
        jnp.int32
    )
    position = jnp.sum((jnp.cumsum(onehot, axis=0) - onehot) * onehot, axis=1)
    return (flat_experts * capacity + position).astype(jnp.int32).reshape(route_rows.shape)


def attend(queries, before, latent_cache, after, new_latent, parents, lengths):
    beam_count = queries.shape[0]
    my_rank = lax.axis_index("dp")
    positions = jnp.arange(latent_cache.shape[1], dtype=jnp.int32)
    first_slot = (my_rank - 1) * beam_count
    padded = jnp.concatenate([before, latent_cache, after], axis=0)
    parent_rows = jnp.take(padded, parents - first_slot, axis=0)
    child_cache = jnp.where(
        (positions[None, :] < lengths[:, None] - 1)[:, :, None],
        parent_rows,
        jnp.zeros_like(parent_rows),
    )
    child_cache = jnp.where(
        (positions[None, :] == lengths[:, None] - 1)[:, :, None],
        new_latent[:, None, :],
        child_cache,
    )
    scores = (
        jnp.einsum("bhc,blc->bhl", queries, child_cache, preferred_element_type=jnp.float32)
        * score_scale
    )
    scores = jnp.where((positions[None, :] < lengths[:, None])[:, None, :], scores, -jnp.inf)
    row_max = jnp.max(scores, axis=2, keepdims=True)
    expons = jnp.exp(scores - row_max)
    probs = (expons / jnp.sum(expons, axis=2, keepdims=True)).astype(jnp.bfloat16)
    mixed = jnp.einsum(
        "bhl,blc->bhc", probs, child_cache[:, :, :KV], preferred_element_type=jnp.float32
    )
    return mixed.astype(jnp.bfloat16)


def swapped(value, partner):
    peers = lax.axis_size("dp")
    return lax.ppermute(value, "dp", [(i, partner(i)) for i in range(peers)])


def step_width(width):
    return max(w for w in (128, 256, 512, 1024) if width % w == 0)


def expert_kernel(steps, blocks, *refs):
    rows, refs = refs[:blocks], refs[blocks:]
    gate_ref, up_ref, down_ref = refs[:3]
    out_refs, (gate_sum, up_sum, hidden) = refs[3 : 3 + blocks], refs[3 + blocks :]
    height = rows[0].shape[0]
    step = pl.program_id(0)

    @pl.when(step < steps)
    def _():
        value = jnp.concatenate([ref[...] for ref in rows], axis=0)
        gate = jnp.dot(value, gate_ref[0], preferred_element_type=jnp.float32)
        up = jnp.dot(value, up_ref[0], preferred_element_type=jnp.float32)
        first = step == 0
        gate_sum[...] = gate + jnp.where(first, 0.0, gate_sum[...])
        up_sum[...] = up + jnp.where(first, 0.0, up_sum[...])

    @pl.when(step == steps - 1)
    def _():
        gate = gate_sum[...]
        hidden[...] = (gate / (1.0 + jnp.exp(-gate)) * up_sum[...]).astype(hidden.dtype)

    @pl.when(step >= steps)
    def _():
        part = jnp.dot(hidden[...], down_ref[0], preferred_element_type=jnp.float32)
        for i, ref in enumerate(out_refs):
            ref[...] = part[i * height : (i + 1) * height].astype(ref.dtype)


def experts(rows, gate_weight, up_weight, down_weight):
    height, width = rows[0].shape
    units = gate_weight.shape[2]
    wide = step_width(width)
    steps = width // wide
    total = len(rows) * height

    def inward(k):
        return jnp.minimum(k, steps - 1)

    def outward(k):
        return jnp.maximum(k - steps, 0)

    return pl.pallas_call(
        lambda *refs: expert_kernel(steps, len(rows), *refs),
        grid=(2 * steps,),
        in_specs=[pl.BlockSpec((height, wide), lambda k: (0, inward(k)))] * len(rows)
        + [pl.BlockSpec((1, wide, units), lambda k: (0, inward(k), 0))] * 2
        + [pl.BlockSpec((1, units, wide), lambda k: (0, 0, outward(k)))],
        out_specs=[pl.BlockSpec((height, wide), lambda k: (0, outward(k)))] * len(rows),
        out_shape=[jax.ShapeDtypeStruct((height, width), jnp.bfloat16)] * len(rows),
        scratch_shapes=[
            pltpu.VMEM((total, units), jnp.float32),
            pltpu.VMEM((total, units), jnp.float32),
            pltpu.VMEM((total, units), jnp.bfloat16),
        ],
        compiler_params=pltpu.CompilerParams(vmem_limit_bytes=60 * 2**20),
        cost_estimate=pl.CostEstimate(
            flops=6 * total * width * units,
            bytes_accessed=6 * width * units + 4 * total * width,
            transcendentals=total * units,
        ),
    )(*rows, gate_weight, up_weight, down_weight)


def added(values):
    total = values[0].astype(jnp.float32)
    for value in values[1:]:
        total = total + value.astype(jnp.float32)
    return total


def body(
    queries,
    latent_cache,
    new_latent,
    parents,
    lengths,
    expert_input,
    routed_experts,
    route_weights,
    gate_weight,
    up_weight,
    down_weight,
):
    beam_count, width = expert_input.shape
    devices = lax.axis_size("dp")
    slices = FF_E // gate_weight.shape[2]
    expert_count = devices // slices
    route_count = routed_experts.shape[1]
    capacity = min(beam_count, max(2, 2 * beam_count * route_count // expert_count))
    dense = capacity == beam_count
    mine = lax.axis_index("dp") // slices
    assert slices == 8

    turns = jnp.arange(expert_count, dtype=jnp.int32)
    targets = (mine + turns) % expert_count
    if dense:
        slots = routed_experts * capacity + jnp.arange(beam_count, dtype=jnp.int32)[:, None]
    else:
        slots = pair_slots(routed_experts, expert_count, capacity)
    wanted = targets[:, None] * capacity + jnp.arange(capacity, dtype=jnp.int32)
    matches = (slots[:, :, None] == wanted.reshape(-1)).astype(jnp.float32)
    mixing = jnp.sum(route_weights[:, :, None] * matches, axis=1)
    if dense:
        blocks = [expert_input] * expert_count
    else:
        selector = jnp.sum(matches, axis=1).T.astype(jnp.bfloat16)
        chosen = jnp.dot(selector, expert_input, preferred_element_type=jnp.float32)
        blocks = list(chosen.astype(jnp.bfloat16).reshape(expert_count, capacity, width))

    def ahead(r):
        return lambda i: (i + r * slices) % devices

    def twin(i):
        return i ^ 1

    def first(i):
        return i ^ (2 if i & 1 else 4)

    def second(i):
        return i ^ (4 if i & 1 else 2)

    column = jnp.concatenate(
        [blocks[0]] + [swapped(blocks[r], ahead(r)) for r in range(1, expert_count)]
    )
    before = lax.ppermute(latent_cache, "dp", [(i, i + 1) for i in range(devices - 1)])
    near = swapped(column, first)
    side = swapped(column, second)
    across = swapped(near, second)
    held = [column, near, side, across]
    *held, latent_cache, mixing = lax.optimization_barrier((*held, latent_cache, mixing))
    after = lax.ppermute(latent_cache, "dp", [(i + 1, i) for i in range(devices - 1)])
    held = held + [swapped(value, twin) for value in held]
    parts = experts(held, gate_weight, up_weight, down_weight)

    own, others = parts[:4], parts[4:]

    def joined(j):
        return added([own[j], swapped(others[j], twin)]).astype(jnp.bfloat16)

    across = swapped(joined(3), second)
    side = swapped(joined(2), second)
    near = added([own[1], swapped(others[1], twin), across]).astype(jnp.bfloat16)
    near, before, after = lax.optimization_barrier((near, before, after))
    near = swapped(near, first)
    value = added([joined(0), side, near]).reshape(expert_count, capacity, width)
    values = [value[0]] + [
        swapped(value[r].astype(jnp.bfloat16), ahead(-r)) for r in range(1, expert_count)
    ]
    if dense:
        weights = jnp.sum(mixing.reshape(beam_count, expert_count, capacity), axis=2)
        total = sum(
            weights[:, r : r + 1] * values[r].astype(jnp.float32) for r in range(expert_count)
        )
    else:
        total = jnp.dot(
            mixing,
            jnp.concatenate([v.astype(jnp.float32) for v in values]),
            precision=lax.Precision.HIGHEST,
            preferred_element_type=jnp.float32,
        )
    attention = attend(queries, before, latent_cache, after, new_latent, parents, lengths)
    return (attention, total.astype(jnp.bfloat16))


def solution(mesh):
    in_specs = (
        P(("groups", "dp"), None, None),
        P(("groups", "dp"), None, None),
        P(("groups", "dp"), None),
        P(("groups", "dp")),
        P(("groups", "dp")),
        P(("groups", "dp"), None),
        P(("groups", "dp"), None),
        P(("groups", "dp"), None),
        P("dp", None, None),
        P("dp", None, None),
        P("dp", None, None),
    )
    out_specs = (P(("groups", "dp"), None, None), P(("groups", "dp"), None))
    return jax.shard_map(body, mesh=mesh, in_specs=in_specs, out_specs=out_specs, check_vma=False)
```

```python
import jax
import jax.numpy as jnp
from jax import lax
from jax.experimental import pallas as pl
from jax.experimental.pallas import tpu as pltpu
from jax.sharding import PartitionSpec as P

FF_E = 2048
KV = 512


score_scale = 192.0 ** (-0.5)


def pair_slots(route_rows, expert_count, capacity):
    flat_experts = route_rows.reshape(-1)
    onehot = (flat_experts[:, None] == jnp.arange(expert_count, dtype=jnp.int32)[None, :]).astype(
        jnp.int32
    )
    position = jnp.sum((jnp.cumsum(onehot, axis=0) - onehot) * onehot, axis=1)
    return (flat_experts * capacity + position).astype(jnp.int32).reshape(route_rows.shape)


def swapped(value, partner):
    peers = lax.axis_size("dp")
    return lax.ppermute(value, "dp", [(i, partner(i)) for i in range(peers)])


def added(values):
    total = values[0].astype(jnp.float32)
    for value in values[1:]:
        total = total + value.astype(jnp.float32)
    return total


EARLY = ((1, 2), (3, 4), (5, 6), (6, 5))
LATE = ((2, 1), (4, 3), (7, 8), (8, 7))


def neighbours(value, moves, slices):
    peers = lax.axis_size("dp")
    pairs = [(base + i, base + j) for base in range(0, peers, slices) for i, j in moves]
    return lax.ppermute(value, "dp", [p for p in pairs if max(p) < peers])


def attend_kernel(parents, lengths, query, own, twin, early, late, newest, out):
    beam_count = parents.shape[0]
    beam = pl.program_id(0)
    rank = lax.axis_index("dp")
    holder = parents[beam] // beam_count
    length = lengths[beam]
    place = rank % 8
    arrives_early = (place == 2) | (place == 4) | (place == 5) | (place == 6)
    rows = jnp.where(arrives_early, early[0], late[0])
    rows = jnp.where(holder == (rank ^ 1), twin[0], rows)
    rows = jnp.where(holder == rank, own[0], rows)
    at = lax.broadcasted_iota(jnp.int32, rows.shape, 0)
    rows = jnp.where(at < length - 1, rows, jnp.zeros_like(rows))
    rows = jnp.where(at == length - 1, newest[0], rows)
    scores = lax.dot_general(
        query[0], rows, (((1,), (1,)), ((), ())), preferred_element_type=jnp.float32
    )
    scores = scores * score_scale
    at = lax.broadcasted_iota(jnp.int32, scores.shape, 1)
    scores = jnp.where(at < length, scores, -jnp.inf)
    expons = jnp.exp(scores - jnp.max(scores, axis=1, keepdims=True))
    probs = (expons / jnp.sum(expons, axis=1, keepdims=True)).astype(jnp.bfloat16)
    mixed = jnp.dot(probs, rows[:, :KV], preferred_element_type=jnp.float32)
    out[0] = mixed.astype(out.dtype)


def attend(queries, own, twin, early, late, new_latent, parents, lengths):
    beam_count, heads, width = queries.shape
    positions = own.shape[1]

    def chosen(b, parents, lengths):
        return (parents[b] % beam_count, 0, 0)

    def each(b, parents, lengths):
        return (b, 0, 0)

    return pl.pallas_call(
        attend_kernel,
        grid_spec=pltpu.PrefetchScalarGridSpec(
            num_scalar_prefetch=2,
            grid=(beam_count,),
            in_specs=[pl.BlockSpec((1, heads, width), each)]
            + [pl.BlockSpec((1, positions, width), chosen)] * 4
            + [pl.BlockSpec((1, 1, width), each)],
            out_specs=pl.BlockSpec((1, heads, KV), each),
        ),
        out_shape=jax.ShapeDtypeStruct((beam_count, heads, KV), jnp.bfloat16),
        cost_estimate=pl.CostEstimate(
            flops=2 * beam_count * heads * positions * (width + KV),
            bytes_accessed=2 * beam_count * (4 * positions * width + heads * (width + KV)),
            transcendentals=beam_count * heads * positions,
        ),
    )(parents, lengths, queries, own, twin, early, late, new_latent[:, None, :])


def expert_kernel(wide, *refs):
    rows, refs = refs[:8], refs[8:]
    gate_hbm, up_hbm, down_hbm, own_hbm, high_hbm, low_hbm = refs[:6]
    value, gate, up, down, part, gate_sum, up_sum, row_sem, weight_sem, out_sem = refs[6:]
    height, width = rows[0].shape
    steps = width // wide
    half = 4 * height

    def row_copy(i):
        return pltpu.make_async_copy(
            rows[i], value.at[pl.ds(i * height, height), :], row_sem.at[i]
        )

    def span(k):
        return pl.ds(pl.multiple_of(k * wide, wide), wide)

    def inward(which, k):
        hbm, ref = ((gate_hbm, gate), (up_hbm, up))[which]
        return pltpu.make_async_copy(
            hbm.at[0, span(k), :], ref.at[span(k), :], weight_sem.at[which, k]
        )

    def onward(k):
        return pltpu.make_async_copy(
            down_hbm.at[0, :, span(k)], down.at[:, span(k)], weight_sem.at[2, k]
        )

    def outward(which, k):
        hbm, first, count = (
            (own_hbm, 0, half),
            (high_hbm, half + 2 * height, 2 * height),
            (low_hbm, half, 2 * height),
        )[which]
        return pltpu.make_async_copy(
            part.at[pl.ds(first, count), span(k)], hbm.at[:, span(k)], out_sem.at[which, k]
        )

    for i in range(8):
        row_copy(i).start()
    for k in range(steps):
        inward(0, k).start()
        inward(1, k).start()
    for k in range(steps):
        onward(k).start()
    for i in range(8):
        row_copy(i).wait()
    gate_sum[...] = jnp.zeros_like(gate_sum)
    up_sum[...] = jnp.zeros_like(up_sum)

    @pl.loop(0, steps)
    def _(k):
        inward(0, k).wait()
        inward(1, k).wait()
        piece = value[:, span(k)]
        gate_sum[...] += jnp.dot(piece, gate[span(k), :], preferred_element_type=jnp.float32)
        up_sum[...] += jnp.dot(piece, up[span(k), :], preferred_element_type=jnp.float32)

    total = gate_sum[...]
    hidden = (total / (1.0 + jnp.exp(-total)) * up_sum[...]).astype(jnp.bfloat16)

    @pl.loop(0, steps)
    def _(k):
        onward(k).wait()
        product = jnp.dot(hidden, down[:, span(k)], preferred_element_type=jnp.float32)
        part[:, span(k)] = product.astype(part.dtype)
        for which in range(3):
            outward(which, k).start()

    @pl.loop(0, steps)
    def _(k):
        for which in range(3):
            outward(which, k).wait()


def experts(rows, gate_weight, up_weight, down_weight):
    height, width = rows[0].shape
    units = gate_weight.shape[2]
    wide = max(w for w in (128, 256, 512, 1024) if width % w == 0)
    total = len(rows) * height
    return pl.pallas_call(
        lambda *refs: expert_kernel(wide, *refs),
        in_specs=[pl.BlockSpec(memory_space=pl.ANY)] * (len(rows) + 3),
        out_specs=[pl.BlockSpec(memory_space=pl.ANY)] * 3,
        out_shape=[
            jax.ShapeDtypeStruct((count * height, width), jnp.bfloat16) for count in (4, 2, 2)
        ],
        scratch_shapes=[
            pltpu.VMEM((total, width), jnp.bfloat16),
            pltpu.VMEM((width, units), jnp.bfloat16),
            pltpu.VMEM((width, units), jnp.bfloat16),
            pltpu.VMEM((units, width), jnp.bfloat16),
            pltpu.VMEM((total, width), jnp.bfloat16),
            pltpu.VMEM((total, units), jnp.float32),
            pltpu.VMEM((total, units), jnp.float32),
            pltpu.SemaphoreType.DMA((len(rows),)),
            pltpu.SemaphoreType.DMA((3, width // wide)),
            pltpu.SemaphoreType.DMA((3, width // wide)),
        ],
        compiler_params=pltpu.CompilerParams(vmem_limit_bytes=60 * 2**20),
        cost_estimate=pl.CostEstimate(
            flops=6 * total * width * units,
            bytes_accessed=6 * width * units + 4 * total * width,
            transcendentals=total * units,
        ),
    )(*rows, gate_weight, up_weight, down_weight)


def mix_kernel(expert_count, slices, routes, scales, *refs):
    values, out = refs[:-1], refs[-1]
    top, beam_count = routes.shape
    mine = lax.axis_index("dp") // slices
    at = lax.broadcasted_iota(jnp.int32, (beam_count, 1), 0)
    total = jnp.zeros(out.shape, jnp.float32)
    for r, value in enumerate(values):
        expert = (mine + r) % expert_count
        column = jnp.zeros((beam_count, 1), jnp.float32)
        for b in range(beam_count):
            scale = 0.0
            for k in range(top):
                scale = scale + jnp.where(routes[k, b] == expert, scales[k, b], 0.0)
            column = jnp.where(at == b, scale, column)
        total = total + column * value[...].astype(jnp.float32)
    out[...] = total.astype(out.dtype)


def mixed_rows(values, routed_experts, route_weights, expert_count, slices):
    scalars = pl.BlockSpec(memory_space=pltpu.SMEM)
    whole = pl.BlockSpec(memory_space=pltpu.VMEM)
    return pl.pallas_call(
        lambda *refs: mix_kernel(expert_count, slices, *refs),
        in_specs=[scalars, scalars] + [whole] * len(values),
        out_specs=whole,
        out_shape=jax.ShapeDtypeStruct(values[0].shape, jnp.bfloat16),
        cost_estimate=pl.CostEstimate(
            flops=2 * len(values) * values[0].size,
            bytes_accessed=2 * (len(values) + 2) * values[0].size,
            transcendentals=0,
        ),
    )(routed_experts.T, route_weights.T, *values)


def body(
    queries,
    latent_cache,
    new_latent,
    parents,
    lengths,
    expert_input,
    routed_experts,
    route_weights,
    gate_weight,
    up_weight,
    down_weight,
):
    beam_count, width = expert_input.shape
    devices = lax.axis_size("dp")
    slices = FF_E // gate_weight.shape[2]
    expert_count = devices // slices
    route_count = routed_experts.shape[1]
    capacity = min(beam_count, max(2, 2 * beam_count * route_count // expert_count))
    dense = capacity == beam_count
    assert slices == 8

    if dense:
        blocks = [expert_input] * expert_count
    else:
        mine = lax.axis_index("dp") // slices
        turns = jnp.arange(expert_count, dtype=jnp.int32)
        targets = (mine + turns) % expert_count
        slots = pair_slots(routed_experts, expert_count, capacity)
        wanted = targets[:, None] * capacity + jnp.arange(capacity, dtype=jnp.int32)
        matches = (slots[:, :, None] == wanted.reshape(-1)).astype(jnp.float32)
        mixing = jnp.sum(route_weights[:, :, None] * matches, axis=1)
        selector = jnp.sum(matches, axis=1).T.astype(jnp.bfloat16)
        chosen = jnp.dot(selector, expert_input, preferred_element_type=jnp.float32)
        blocks = list(chosen.astype(jnp.bfloat16).reshape(expert_count, capacity, width))

    def ahead(r):
        return lambda i: (i + r * slices) % devices

    def twin(i):
        return i ^ 1

    def first(i):
        return i ^ (2 if i & 1 else 4)

    def second(i):
        return i ^ (4 if i & 1 else 2)

    blocks = blocks[:1] + [swapped(blocks[r], ahead(r)) for r in range(1, expert_count)]
    early = neighbours(latent_cache, EARLY, slices)
    *blocks, early = lax.optimization_barrier((*blocks, early))
    column = jnp.concatenate(blocks)
    near = swapped(column, first)
    side = swapped(column, second)
    across = swapped(near, second)
    beside = swapped(latent_cache, twin)
    held = [column, near, side, across]
    *held, latent_cache = lax.optimization_barrier((*held, latent_cache))
    late = neighbours(latent_cache, LATE, slices)
    held = held + [swapped(value, twin) for value in held]
    own, high, low = experts(held, gate_weight, up_weight, down_weight)

    high, low = swapped(high, twin), swapped(low, twin)
    height = expert_count * capacity

    def block(value, j):
        return lax.slice_in_dim(value, j * height, (j + 1) * height)

    across = swapped(added([block(own, 3), block(high, 1)]).astype(jnp.bfloat16), second)
    side = swapped(added([block(own, 2), block(high, 0)]).astype(jnp.bfloat16), second)
    near = added([block(own, 1), block(low, 1), across]).astype(jnp.bfloat16)
    near, early, late = lax.optimization_barrier((near, early, late))
    near = swapped(near, first)
    here = [own, low, side, near]

    def share(r):
        return added([v[r * capacity : (r + 1) * capacity] for v in here])

    values = [swapped(share(r).astype(jnp.bfloat16), ahead(-r)) for r in range(1, expert_count)]
    values = [share(0)] + values
    if dense:
        expert_output = mixed_rows(values, routed_experts, route_weights, expert_count, slices)
    else:
        expert_output = jnp.dot(
            mixing,
            jnp.concatenate([v.astype(jnp.float32) for v in values]),
            precision=lax.Precision.HIGHEST,
            preferred_element_type=jnp.float32,
        ).astype(jnp.bfloat16)
    attention = attend(
        queries, latent_cache, beside, early, late, new_latent, parents, lengths
    )
    return (attention, expert_output)


def solution(mesh):
    in_specs = (
        P(("groups", "dp"), None, None),
        P(("groups", "dp"), None, None),
        P(("groups", "dp"), None),
        P(("groups", "dp")),
        P(("groups", "dp")),
        P(("groups", "dp"), None),
        P(("groups", "dp"), None),
        P(("groups", "dp"), None),
        P("dp", None, None),
        P("dp", None, None),
        P("dp", None, None),
    )
    out_specs = (P(("groups", "dp"), None, None), P(("groups", "dp"), None))
    return jax.shard_map(body, mesh=mesh, in_specs=in_specs, out_specs=out_specs, check_vma=False)
```

```python
import jax
import jax.numpy as jnp
from jax import lax
from jax.experimental import pallas as pl
from jax.experimental.pallas import tpu as pltpu
from jax.sharding import PartitionSpec as P

FF_E = 2048
KV = 512


score_scale = 192.0 ** (-0.5)


def pair_slots(route_rows, expert_count, capacity):
    flat_experts = route_rows.reshape(-1)
    onehot = (flat_experts[:, None] == jnp.arange(expert_count, dtype=jnp.int32)[None, :]).astype(
        jnp.int32
    )
    position = jnp.sum((jnp.cumsum(onehot, axis=0) - onehot) * onehot, axis=1)
    return (flat_experts * capacity + position).astype(jnp.int32).reshape(route_rows.shape)


def swapped(value, partner):
    peers = lax.axis_size("dp")
    return lax.ppermute(value, "dp", [(i, partner(i)) for i in range(peers)])


def added(values):
    total = values[0].astype(jnp.float32)
    for value in values[1:]:
        total = total + value.astype(jnp.float32)
    return total


EARLY = ((1, 2), (3, 4), (5, 6), (6, 5))
LATE = ((2, 1), (4, 3), (7, 8), (8, 7))


def neighbours(value, moves, slices):
    peers = lax.axis_size("dp")
    pairs = [(base + i, base + j) for base in range(0, peers, slices) for i, j in moves]
    return lax.ppermute(value, "dp", [p for p in pairs if max(p) < peers])


def attend_kernel(parents, lengths, query, own, twin, early, late, newest, out):
    beam_count = parents.shape[0]
    beam = pl.program_id(0)
    rank = lax.axis_index("dp")
    holder = parents[beam] // beam_count
    length = lengths[beam]
    place = rank % 8
    arrives_early = (place == 2) | (place == 4) | (place == 5) | (place == 6)
    rows = jnp.where(arrives_early, early[0], late[0])
    rows = jnp.where(holder == (rank ^ 1), twin[0], rows)
    rows = jnp.where(holder == rank, own[0], rows)
    at = lax.broadcasted_iota(jnp.int32, rows.shape, 0)
    rows = jnp.where(at < length - 1, rows, jnp.zeros_like(rows))
    rows = jnp.where(at == length - 1, newest[0], rows)
    scores = lax.dot_general(
        query[0], rows, (((1,), (1,)), ((), ())), preferred_element_type=jnp.float32
    )
    scores = scores * score_scale
    at = lax.broadcasted_iota(jnp.int32, scores.shape, 1)
    scores = jnp.where(at < length, scores, -jnp.inf)
    expons = jnp.exp(scores - jnp.max(scores, axis=1, keepdims=True))
    probs = (expons / jnp.sum(expons, axis=1, keepdims=True)).astype(jnp.bfloat16)
    mixed = jnp.dot(probs, rows[:, :KV], preferred_element_type=jnp.float32)
    out[0] = mixed.astype(out.dtype)


def attend(queries, own, twin, early, late, newest, parents, lengths):
    beam_count, heads, width = queries.shape
    positions = own.shape[1]

    def chosen(b, parents, lengths):
        return (parents[b] % beam_count, 0, 0)

    def each(b, parents, lengths):
        return (b, 0, 0)

    return pl.pallas_call(
        attend_kernel,
        grid_spec=pltpu.PrefetchScalarGridSpec(
            num_scalar_prefetch=2,
            grid=(beam_count,),
            in_specs=[pl.BlockSpec((1, heads, width), each)]
            + [pl.BlockSpec((1, positions, width), chosen)] * 4
            + [pl.BlockSpec((1, 1, width), each)],
            out_specs=pl.BlockSpec((1, heads, KV), each),
        ),
        out_shape=jax.ShapeDtypeStruct((beam_count, heads, KV), jnp.bfloat16),
        cost_estimate=pl.CostEstimate(
            flops=2 * beam_count * heads * positions * (width + KV),
            bytes_accessed=2 * beam_count * (4 * positions * width + heads * (width + KV)),
            transcendentals=beam_count * heads * positions,
        ),
    )(parents, lengths, queries, own, twin, early, late, newest)


def fetch_kernel(*refs):
    count = len(refs) // 2
    sources, targets, sems = refs[:count], refs[count:-1], refs[-1]
    copies = [
        pltpu.make_async_copy(source, target, sems.at[i])
        for i, (source, target) in enumerate(zip(sources, targets))
    ]
    for copy in copies:
        copy.start()
    for copy in copies:
        copy.wait()


def fetched(weights):
    return pl.pallas_call(
        fetch_kernel,
        in_specs=[pl.BlockSpec(memory_space=pl.ANY)] * len(weights),
        out_specs=[pl.BlockSpec(memory_space=pltpu.VMEM)] * len(weights),
        out_shape=[pltpu.VMEM(w.shape, w.dtype) for w in weights],
        scratch_shapes=[pltpu.SemaphoreType.DMA((len(weights),))],
        compiler_params=pltpu.CompilerParams(vmem_limit_bytes=16 * 2**20),
        cost_estimate=pl.CostEstimate(
            flops=0,
            bytes_accessed=2 * sum(w.size * w.dtype.itemsize for w in weights),
            transcendentals=0,
        ),
    )(*weights)


def expert_kernel(wide, *refs):
    rows, refs = refs[:8], refs[8:]
    gate, up, down, own, high, low, gate_sum, up_sum = refs
    height, width = rows[0].shape
    half = 4 * height

    def span(k):
        return pl.ds(pl.multiple_of(k * wide, wide), wide)

    gate_sum[...] = jnp.zeros_like(gate_sum)
    up_sum[...] = jnp.zeros_like(up_sum)

    @pl.loop(0, width // wide)
    def _(k):
        piece = jnp.concatenate([ref[:, span(k)] for ref in rows], axis=0)
        gate_sum[...] += jnp.dot(piece, gate[0, span(k), :], preferred_element_type=jnp.float32)
        up_sum[...] += jnp.dot(piece, up[0, span(k), :], preferred_element_type=jnp.float32)

    total = gate_sum[...]
    hidden = (total / (1.0 + jnp.exp(-total)) * up_sum[...]).astype(jnp.bfloat16)

    @pl.loop(0, width // wide)
    def _(k):
        product = jnp.dot(hidden, down[0, :, span(k)], preferred_element_type=jnp.float32)
        product = product.astype(jnp.bfloat16)
        own[:, span(k)] = product[:half]
        low[:, span(k)] = product[half : half + 2 * height]
        high[:, span(k)] = product[half + 2 * height :]


def experts(rows, weights):
    height, width = rows[0].shape
    units = weights[0].shape[2]
    wide = max(w for w in (128, 256, 512, 1024) if width % w == 0)
    total = len(rows) * height
    whole = pl.BlockSpec(memory_space=pltpu.VMEM)
    inputs = [pltpu.with_memory_space_constraint(v, pltpu.VMEM) for v in (*rows, *weights)]
    return pl.pallas_call(
        lambda *refs: expert_kernel(wide, *refs),
        in_specs=[whole] * len(inputs),
        out_specs=[whole] * 3,
        out_shape=[pltpu.VMEM((count * height, width), jnp.bfloat16) for count in (4, 2, 2)],
        scratch_shapes=[
            pltpu.VMEM((total, units), jnp.float32),
            pltpu.VMEM((total, units), jnp.float32),
        ],
        compiler_params=pltpu.CompilerParams(vmem_limit_bytes=28 * 2**20),
        cost_estimate=pl.CostEstimate(
            flops=6 * total * width * units,
            bytes_accessed=6 * width * units + 4 * total * width,
            transcendentals=total * units,
        ),
    )(*inputs)


def body(
    queries,
    latent_cache,
    new_latent,
    parents,
    lengths,
    expert_input,
    routed_experts,
    route_weights,
    gate_weight,
    up_weight,
    down_weight,
):
    beam_count, width = expert_input.shape
    devices = lax.axis_size("dp")
    slices = FF_E // gate_weight.shape[2]
    expert_count = devices // slices
    route_count = routed_experts.shape[1]
    capacity = min(beam_count, max(2, 2 * beam_count * route_count // expert_count))
    dense = capacity == beam_count
    assert slices == 8

    mine = lax.axis_index("dp") // slices
    turns = jnp.arange(expert_count, dtype=jnp.int32)
    targets = (mine + turns) % expert_count
    if dense:
        blocks = [expert_input] * expert_count
        mixing = [
            jnp.sum(jnp.where(routed_experts == targets[r], route_weights, 0.0), axis=1)
            for r in range(expert_count)
        ]
    else:
        slots = pair_slots(routed_experts, expert_count, capacity)
        wanted = targets[:, None] * capacity + jnp.arange(capacity, dtype=jnp.int32)
        matches = (slots[:, :, None] == wanted.reshape(-1)).astype(jnp.float32)
        mixing = jnp.sum(route_weights[:, :, None] * matches, axis=1)
        selector = jnp.sum(matches, axis=1).T.astype(jnp.bfloat16)
        chosen = jnp.dot(selector, expert_input, preferred_element_type=jnp.float32)
        blocks = list(chosen.astype(jnp.bfloat16).reshape(expert_count, capacity, width))

    def ahead(r):
        return lambda i: (i + r * slices) % devices

    def twin(i):
        return i ^ 1

    def first(i):
        return i ^ (2 if i & 1 else 4)

    def second(i):
        return i ^ (4 if i & 1 else 2)

    blocks = blocks[:1] + [swapped(blocks[r], ahead(r)) for r in range(1, expert_count)]
    early = neighbours(latent_cache, EARLY, slices)
    newest = new_latent[:, None, :]
    *blocks, early, newest, mixing = lax.optimization_barrier((*blocks, early, newest, mixing))
    column = jnp.concatenate(blocks)
    near = swapped(column, first)
    side = swapped(column, second)
    across = swapped(near, second)
    beside = swapped(latent_cache, twin)
    held = [column, near, side, across]
    *held, beside, latent_cache = lax.optimization_barrier((*held, beside, latent_cache))
    late = neighbours(latent_cache, LATE, slices)
    held = held + [swapped(value, twin) for value in held]
    own, high, low = experts(held, fetched([gate_weight, up_weight, down_weight]))

    high, low = swapped(high, twin), swapped(low, twin)
    height = expert_count * capacity

    def block(value, j):
        return lax.slice_in_dim(value, j * height, (j + 1) * height)

    across = added([block(own, 3), block(high, 1)]).astype(jnp.bfloat16)
    across, late = lax.optimization_barrier((across, late))
    across = swapped(across, second)
    side = swapped(added([block(own, 2), block(high, 0)]).astype(jnp.bfloat16), second)
    attention = attend(queries, latent_cache, beside, early, late, newest, parents, lengths)
    near = added([block(own, 1), block(low, 1), across]).astype(jnp.bfloat16)
    near, attention = lax.optimization_barrier((near, attention))
    near = swapped(near, first)
    here = [own, low, side, near]

    def share(r):
        return added([v[r * capacity : (r + 1) * capacity] for v in here])

    values = [swapped(share(r).astype(jnp.bfloat16), ahead(-r)) for r in range(1, expert_count)]
    values = [share(0)] + values
    values = [v.astype(jnp.float32) for v in values]
    if dense:
        expert_output = sum(mixing[r][:, None] * values[r] for r in range(expert_count))
    else:
        expert_output = jnp.dot(
            mixing,
            jnp.concatenate(values),
            precision=lax.Precision.HIGHEST,
            preferred_element_type=jnp.float32,
        )
    return (attention, expert_output.astype(jnp.bfloat16))


def solution(mesh):
    in_specs = (
        P(("groups", "dp"), None, None),
        P(("groups", "dp"), None, None),
        P(("groups", "dp"), None),
        P(("groups", "dp")),
        P(("groups", "dp")),
        P(("groups", "dp"), None),
        P(("groups", "dp"), None),
        P(("groups", "dp"), None),
        P("dp", None, None),
        P("dp", None, None),
        P("dp", None, None),
    )
    out_specs = (P(("groups", "dp"), None, None), P(("groups", "dp"), None))
    return jax.shard_map(body, mesh=mesh, in_specs=in_specs, out_specs=out_specs, check_vma=False)
```

```python
import jax
import jax.numpy as jnp
from jax import lax
from jax.experimental import pallas as pl
from jax.experimental.pallas import tpu as pltpu
from jax.sharding import PartitionSpec as P

FF_E = 2048
KV = 512


score_scale = 192.0 ** (-0.5)


def pair_slots(route_rows, expert_count, capacity):
    flat_experts = route_rows.reshape(-1)
    onehot = (flat_experts[:, None] == jnp.arange(expert_count, dtype=jnp.int32)[None, :]).astype(
        jnp.int32
    )
    position = jnp.sum((jnp.cumsum(onehot, axis=0) - onehot) * onehot, axis=1)
    return (flat_experts * capacity + position).astype(jnp.int32).reshape(route_rows.shape)


def swapped(value, partner):
    peers = lax.axis_size("dp")
    return lax.ppermute(value, "dp", [(i, partner(i)) for i in range(peers)])


def added(values):
    total = values[0].astype(jnp.float32)
    for value in values[1:]:
        total = total + value.astype(jnp.float32)
    return total


EARLY = ((1, 2), (3, 4), (5, 6), (6, 5))
LATE = ((2, 1), (4, 3), (7, 8), (8, 7))


def neighbours(value, moves, slices):
    peers = lax.axis_size("dp")
    pairs = [(base + i, base + j) for base in range(0, peers, slices) for i, j in moves]
    return lax.ppermute(value, "dp", [p for p in pairs if max(p) < peers])


def attend_kernel(parents, lengths, query, own, twin, early, late, newest, out):
    beam_count = parents.shape[0]
    beam = pl.program_id(0)
    rank = lax.axis_index("dp")
    holder = parents[beam] // beam_count
    length = lengths[beam]
    place = rank % 8
    arrives_early = (place == 2) | (place == 4) | (place == 5) | (place == 6)
    rows = jnp.where(arrives_early, early[0], late[0])
    rows = jnp.where(holder == (rank ^ 1), twin[0], rows)
    rows = jnp.where(holder == rank, own[0], rows)
    at = lax.broadcasted_iota(jnp.int32, rows.shape, 0)
    rows = jnp.where(at < length - 1, rows, jnp.zeros_like(rows))
    rows = jnp.where(at == length - 1, newest[0], rows)
    scores = lax.dot_general(
        query[0], rows, (((1,), (1,)), ((), ())), preferred_element_type=jnp.float32
    )
    scores = scores * score_scale
    at = lax.broadcasted_iota(jnp.int32, scores.shape, 1)
    scores = jnp.where(at < length, scores, -jnp.inf)
    expons = jnp.exp(scores - jnp.max(scores, axis=1, keepdims=True))
    probs = (expons / jnp.sum(expons, axis=1, keepdims=True)).astype(jnp.bfloat16)
    mixed = jnp.dot(probs, rows[:, :KV], preferred_element_type=jnp.float32)
    out[0] = mixed.astype(out.dtype)


def attend(queries, own, twin, early, late, newest, parents, lengths):
    beam_count, heads, width = queries.shape
    positions = own.shape[1]

    def chosen(b, parents, lengths):
        return (parents[b] % beam_count, 0, 0)

    def each(b, parents, lengths):
        return (b, 0, 0)

    return pl.pallas_call(
        attend_kernel,
        grid_spec=pltpu.PrefetchScalarGridSpec(
            num_scalar_prefetch=2,
            grid=(beam_count,),
            in_specs=[pl.BlockSpec((1, heads, width), each)]
            + [pl.BlockSpec((1, positions, width), chosen)] * 4
            + [pl.BlockSpec((1, 1, width), each)],
            out_specs=pl.BlockSpec((1, heads, KV), each),
        ),
        out_shape=jax.ShapeDtypeStruct((beam_count, heads, KV), jnp.bfloat16),
        cost_estimate=pl.CostEstimate(
            flops=2 * beam_count * heads * positions * (width + KV),
            bytes_accessed=2 * beam_count * (4 * positions * width + heads * (width + KV)),
            transcendentals=beam_count * heads * positions,
        ),
    )(parents, lengths, queries, own, twin, early, late, newest)


def fetch_kernel(*refs):
    count = len(refs) // 2
    sources, targets, sems = refs[:count], refs[count:-1], refs[-1]
    copies = [
        pltpu.make_async_copy(source, target, sems.at[i])
        for i, (source, target) in enumerate(zip(sources, targets))
    ]
    for copy in copies:
        copy.start()
    for copy in copies:
        copy.wait()


def fetched(weights):
    return pl.pallas_call(
        fetch_kernel,
        in_specs=[pl.BlockSpec(memory_space=pltpu.HBM)] * len(weights),
        out_specs=[pl.BlockSpec(memory_space=pltpu.VMEM)] * len(weights),
        out_shape=[pltpu.VMEM(w.shape, w.dtype) for w in weights],
        scratch_shapes=[pltpu.SemaphoreType.DMA((len(weights),))],
        compiler_params=pltpu.CompilerParams(vmem_limit_bytes=16 * 2**20),
        cost_estimate=pl.CostEstimate(
            flops=0,
            bytes_accessed=2 * sum(w.size * w.dtype.itemsize for w in weights),
            transcendentals=0,
        ),
    )(*[pltpu.with_memory_space_constraint(w, pltpu.HBM) for w in weights])


def expert_kernel(wide, *refs):
    rows, refs = refs[:8], refs[8:]
    gate, up, down, own, high, low, gate_sum, up_sum = refs
    height, width = rows[0].shape
    half = 4 * height

    def span(k):
        return pl.ds(pl.multiple_of(k * wide, wide), wide)

    gate_sum[...] = jnp.zeros_like(gate_sum)
    up_sum[...] = jnp.zeros_like(up_sum)

    @pl.loop(0, width // wide)
    def _(k):
        piece = jnp.concatenate([ref[:, span(k)] for ref in rows], axis=0)
        gate_sum[...] += jnp.dot(piece, gate[0, span(k), :], preferred_element_type=jnp.float32)
        up_sum[...] += jnp.dot(piece, up[0, span(k), :], preferred_element_type=jnp.float32)

    total = gate_sum[...]
    hidden = (total / (1.0 + jnp.exp(-total)) * up_sum[...]).astype(jnp.bfloat16)

    @pl.loop(0, width // wide)
    def _(k):
        product = jnp.dot(hidden, down[0, :, span(k)], preferred_element_type=jnp.float32)
        product = product.astype(jnp.bfloat16)
        own[:, span(k)] = product[:half]
        low[:, span(k)] = product[half : half + 2 * height]
        high[:, span(k)] = product[half + 2 * height :]


def experts(rows, weights):
    height, width = rows[0].shape
    units = weights[0].shape[2]
    wide = max(w for w in (128, 256, 512, 1024) if width % w == 0)
    total = len(rows) * height
    whole = pl.BlockSpec(memory_space=pltpu.VMEM)
    inputs = [pltpu.with_memory_space_constraint(v, pltpu.VMEM) for v in (*rows, *weights)]
    return pl.pallas_call(
        lambda *refs: expert_kernel(wide, *refs),
        in_specs=[whole] * len(inputs),
        out_specs=[whole] * 3,
        out_shape=[pltpu.VMEM((count * height, width), jnp.bfloat16) for count in (4, 2, 2)],
        scratch_shapes=[
            pltpu.VMEM((total, units), jnp.float32),
            pltpu.VMEM((total, units), jnp.float32),
        ],
        compiler_params=pltpu.CompilerParams(vmem_limit_bytes=28 * 2**20),
        cost_estimate=pl.CostEstimate(
            flops=6 * total * width * units,
            bytes_accessed=6 * width * units + 4 * total * width,
            transcendentals=total * units,
        ),
    )(*inputs)


def body(
    queries,
    latent_cache,
    new_latent,
    parents,
    lengths,
    expert_input,
    routed_experts,
    route_weights,
    gate_weight,
    up_weight,
    down_weight,
):
    beam_count, width = expert_input.shape
    devices = lax.axis_size("dp")
    slices = FF_E // gate_weight.shape[2]
    expert_count = devices // slices
    route_count = routed_experts.shape[1]
    capacity = min(beam_count, max(2, 2 * beam_count * route_count // expert_count))
    dense = capacity == beam_count
    assert slices == 8

    mine = lax.axis_index("dp") // slices
    turns = jnp.arange(expert_count, dtype=jnp.int32)
    targets = (mine + turns) % expert_count
    if dense:
        blocks = [expert_input] * expert_count
        mixing = [
            jnp.sum(jnp.where(routed_experts == targets[r], route_weights, 0.0), axis=1)
            for r in range(expert_count)
        ]
    else:
        slots = pair_slots(routed_experts, expert_count, capacity)
        wanted = targets[:, None] * capacity + jnp.arange(capacity, dtype=jnp.int32)
        matches = (slots[:, :, None] == wanted.reshape(-1)).astype(jnp.float32)
        mixing = jnp.sum(route_weights[:, :, None] * matches, axis=1)
        selector = jnp.sum(matches, axis=1).T.astype(jnp.bfloat16)
        chosen = jnp.dot(selector, expert_input, preferred_element_type=jnp.float32)
        blocks = list(chosen.astype(jnp.bfloat16).reshape(expert_count, capacity, width))

    def ahead(r):
        return lambda i: (i + r * slices) % devices

    def twin(i):
        return i ^ 1

    def first(i):
        return i ^ (2 if i & 1 else 4)

    def second(i):
        return i ^ (4 if i & 1 else 2)

    blocks = blocks[:1] + [swapped(blocks[r], ahead(r)) for r in range(1, expert_count)]
    early = neighbours(latent_cache, EARLY, slices)
    newest = new_latent[:, None, :]
    *blocks, early, newest, mixing = lax.optimization_barrier((*blocks, early, newest, mixing))
    column = jnp.concatenate(blocks)
    near = swapped(column, first)
    side = swapped(column, second)
    across = swapped(near, second)
    beside = swapped(latent_cache, twin)
    held = [column, near, side, across]
    weights = fetched([gate_weight, up_weight, down_weight])
    held, weights, beside, latent_cache = lax.optimization_barrier(
        (held, weights, beside, latent_cache)
    )
    late = neighbours(latent_cache, LATE, slices)
    held = held + [swapped(value, twin) for value in held]
    own, high, low = experts(held, weights)
    high, late = lax.optimization_barrier((high, late))

    high, low = swapped(high, twin), swapped(low, twin)
    height = expert_count * capacity

    def block(value, j):
        return lax.slice_in_dim(value, j * height, (j + 1) * height)

    across = added([block(own, 3), block(high, 1)]).astype(jnp.bfloat16)
    across = swapped(across, second)
    side = swapped(added([block(own, 2), block(high, 0)]).astype(jnp.bfloat16), second)
    attention = attend(queries, latent_cache, beside, early, late, newest, parents, lengths)
    near = added([block(own, 1), block(low, 1), across]).astype(jnp.bfloat16)
    near, attention = lax.optimization_barrier((near, attention))
    near = swapped(near, first)
    here = [own, low, side, near]

    def share(r):
        return added([v[r * capacity : (r + 1) * capacity] for v in here])

    values = [swapped(share(r).astype(jnp.bfloat16), ahead(-r)) for r in range(1, expert_count)]
    values = [share(0)] + values
    values = [v.astype(jnp.float32) for v in values]
    if dense:
        expert_output = sum(mixing[r][:, None] * values[r] for r in range(expert_count))
    else:
        expert_output = jnp.dot(
            mixing,
            jnp.concatenate(values),
            precision=lax.Precision.HIGHEST,
            preferred_element_type=jnp.float32,
        )
    return (attention, expert_output.astype(jnp.bfloat16))


def solution(mesh):
    in_specs = (
        P(("groups", "dp"), None, None),
        P(("groups", "dp"), None, None),
        P(("groups", "dp"), None),
        P(("groups", "dp")),
        P(("groups", "dp")),
        P(("groups", "dp"), None),
        P(("groups", "dp"), None),
        P(("groups", "dp"), None),
        P("dp", None, None),
        P("dp", None, None),
        P("dp", None, None),
    )
    out_specs = (P(("groups", "dp"), None, None), P(("groups", "dp"), None))
    return jax.shard_map(body, mesh=mesh, in_specs=in_specs, out_specs=out_specs, check_vma=False)
```

```python
import jax
import jax.numpy as jnp
from jax import lax
from jax.experimental import pallas as pl
from jax.experimental.pallas import tpu as pltpu
from jax.sharding import PartitionSpec as P

FF_E = 2048
KV = 512


score_scale = 192.0 ** (-0.5)


def pair_slots(route_rows, expert_count, capacity):
    flat_experts = route_rows.reshape(-1)
    onehot = (flat_experts[:, None] == jnp.arange(expert_count, dtype=jnp.int32)[None, :]).astype(
        jnp.int32
    )
    position = jnp.sum((jnp.cumsum(onehot, axis=0) - onehot) * onehot, axis=1)
    return (flat_experts * capacity + position).astype(jnp.int32).reshape(route_rows.shape)


def swapped(value, partner):
    peers = lax.axis_size("dp")
    return lax.ppermute(value, "dp", [(i, partner(i)) for i in range(peers)])


def after(value, other):
    return lax.optimization_barrier((value, other))[0]


def added(values):
    total = values[0].astype(jnp.float32)
    for value in values[1:]:
        total = total + value.astype(jnp.float32)
    return total


EARLY = ((1, 2), (3, 4), (5, 6), (6, 5))
LATE = ((2, 1), (4, 3), (7, 8), (8, 7))


def neighbours(value, moves, slices):
    peers = lax.axis_size("dp")
    pairs = [(base + i, base + j) for base in range(0, peers, slices) for i, j in moves]
    return lax.ppermute(value, "dp", [p for p in pairs if max(p) < peers])


def attend_kernel(parents, lengths, query, own, twin, early, late, newest, out):
    beams = range(query.shape[0])
    rank = lax.axis_index("dp")
    place = rank % 8
    arrives_early = (place == 2) | (place == 4) | (place == 5) | (place == 6)
    latest = newest[...].astype(jnp.float32)
    at = lax.broadcasted_iota(jnp.int32, own.shape[1:], 0)
    rows, scores, probs = [], [], []
    for b in beams:
        slot, holder = parents[b] % len(beams), parents[b] // len(beams)
        value = jnp.where(arrives_early, early[slot], late[slot])
        value = jnp.where(holder == (rank ^ 1), twin[slot], value)
        value = jnp.where(holder == rank, own[slot], value)
        value = jnp.where(at < lengths[b] - 1, value, jnp.zeros_like(value))
        row = jnp.broadcast_to(latest[b : b + 1], value.shape).astype(value.dtype)
        rows.append(jnp.where(at == lengths[b] - 1, row, value))
    for b in beams:
        product = lax.dot_general(
            query[b], rows[b], (((1,), (1,)), ((), ())), preferred_element_type=jnp.float32
        )
        scores.append(product * score_scale)
    at = lax.broadcasted_iota(jnp.int32, scores[0].shape, 1)
    for b in beams:
        value = jnp.where(at < lengths[b], scores[b], -jnp.inf)
        expons = jnp.exp(value - jnp.max(value, axis=1, keepdims=True))
        total = jnp.sum(expons, axis=1, keepdims=True)
        probs.append((expons / total).astype(jnp.bfloat16))
    for b in beams:
        mixed = jnp.dot(probs[b], rows[b][:, :KV], preferred_element_type=jnp.float32)
        out[b] = mixed.astype(out.dtype)


def attend(queries, own, twin, early, late, newest, parents, lengths):
    beam_count, heads, width = queries.shape
    positions = own.shape[1]
    scalars = pl.BlockSpec(memory_space=pltpu.SMEM)
    whole = pl.BlockSpec(memory_space=pltpu.VMEM)
    arrays = [
        pltpu.with_memory_space_constraint(v, pltpu.VMEM)
        for v in (queries, own, twin, early, late, newest)
    ]
    return pl.pallas_call(
        attend_kernel,
        in_specs=[scalars] * 2 + [whole] * len(arrays),
        out_specs=whole,
        out_shape=jax.ShapeDtypeStruct((beam_count, heads, KV), jnp.bfloat16),
        compiler_params=pltpu.CompilerParams(vmem_limit_bytes=16 * 2**20),
        cost_estimate=pl.CostEstimate(
            flops=2 * beam_count * heads * positions * (width + KV),
            bytes_accessed=2 * beam_count * (4 * positions * width + heads * (width + KV)),
            transcendentals=beam_count * heads * positions,
        ),
    )(parents, lengths, *arrays)


def fetch_kernel(*refs):
    count = len(refs) // 2
    sources, targets, sems = refs[:count], refs[count:-1], refs[-1]
    copies = [
        pltpu.make_async_copy(source, target, sems.at[i])
        for i, (source, target) in enumerate(zip(sources, targets))
    ]
    for copy in copies:
        copy.start()
    for copy in copies:
        copy.wait()


def fetched(weights):
    return pl.pallas_call(
        fetch_kernel,
        in_specs=[pl.BlockSpec(memory_space=pltpu.HBM)] * len(weights),
        out_specs=[pl.BlockSpec(memory_space=pltpu.VMEM)] * len(weights),
        out_shape=[pltpu.VMEM(w.shape, w.dtype) for w in weights],
        scratch_shapes=[pltpu.SemaphoreType.DMA((len(weights),))],
        compiler_params=pltpu.CompilerParams(vmem_limit_bytes=16 * 2**20),
        cost_estimate=pl.CostEstimate(
            flops=0,
            bytes_accessed=2 * sum(w.size * w.dtype.itemsize for w in weights),
            transcendentals=0,
        ),
    )(*[pltpu.with_memory_space_constraint(w, pltpu.HBM) for w in weights])


def expert_kernel(wide, *refs):
    rows, refs = refs[:8], refs[8:]
    gate, up, down, own, high, low, gate_sum, up_sum = refs
    height, width = rows[0].shape
    half = 4 * height

    def span(k):
        return pl.ds(pl.multiple_of(k * wide, wide), wide)

    gate_sum[...] = jnp.zeros_like(gate_sum)
    up_sum[...] = jnp.zeros_like(up_sum)

    @pl.loop(0, width // wide)
    def _(k):
        piece = jnp.concatenate([ref[:, span(k)] for ref in rows], axis=0)
        gate_sum[...] += jnp.dot(piece, gate[0, span(k), :], preferred_element_type=jnp.float32)
        up_sum[...] += jnp.dot(piece, up[0, span(k), :], preferred_element_type=jnp.float32)

    total = gate_sum[...]
    hidden = (total / (1.0 + jnp.exp(-total)) * up_sum[...]).astype(jnp.bfloat16)

    @pl.loop(0, width // wide)
    def _(k):
        product = jnp.dot(hidden, down[0, :, span(k)], preferred_element_type=jnp.float32)
        product = product.astype(jnp.bfloat16)
        own[:, span(k)] = product[:half]
        low[:, span(k)] = product[half : half + 2 * height]
        high[:, span(k)] = product[half + 2 * height :]


def experts(rows, weights):
    height, width = rows[0].shape
    units = weights[0].shape[2]
    wide = max(w for w in (128, 256, 512, 1024) if width % w == 0)
    total = len(rows) * height
    whole = pl.BlockSpec(memory_space=pltpu.VMEM)
    inputs = [pltpu.with_memory_space_constraint(v, pltpu.VMEM) for v in (*rows, *weights)]
    return pl.pallas_call(
        lambda *refs: expert_kernel(wide, *refs),
        in_specs=[whole] * len(inputs),
        out_specs=[whole] * 3,
        out_shape=[pltpu.VMEM((count * height, width), jnp.bfloat16) for count in (4, 2, 2)],
        scratch_shapes=[
            pltpu.VMEM((total, units), jnp.float32),
            pltpu.VMEM((total, units), jnp.float32),
        ],
        compiler_params=pltpu.CompilerParams(vmem_limit_bytes=28 * 2**20),
        cost_estimate=pl.CostEstimate(
            flops=6 * total * width * units,
            bytes_accessed=6 * width * units + 4 * total * width,
            transcendentals=total * units,
        ),
    )(*inputs)


def body(
    queries,
    latent_cache,
    new_latent,
    parents,
    lengths,
    expert_input,
    routed_experts,
    route_weights,
    gate_weight,
    up_weight,
    down_weight,
):
    beam_count, width = expert_input.shape
    devices = lax.axis_size("dp")
    slices = FF_E // gate_weight.shape[2]
    expert_count = devices // slices
    route_count = routed_experts.shape[1]
    capacity = min(beam_count, max(2, 2 * beam_count * route_count // expert_count))
    dense = capacity == beam_count
    assert slices == 8

    mine = lax.axis_index("dp") // slices
    turns = jnp.arange(expert_count, dtype=jnp.int32)
    targets = (mine + turns) % expert_count
    if dense:
        blocks = [expert_input] * expert_count
        mixing = [
            jnp.sum(jnp.where(routed_experts == targets[r], route_weights, 0.0), axis=1)
            for r in range(expert_count)
        ]
    else:
        slots = pair_slots(routed_experts, expert_count, capacity)
        wanted = targets[:, None] * capacity + jnp.arange(capacity, dtype=jnp.int32)
        matches = (slots[:, :, None] == wanted.reshape(-1)).astype(jnp.float32)
        mixing = jnp.sum(route_weights[:, :, None] * matches, axis=1)
        selector = jnp.sum(matches, axis=1).T.astype(jnp.bfloat16)
        chosen = jnp.dot(selector, expert_input, preferred_element_type=jnp.float32)
        blocks = list(chosen.astype(jnp.bfloat16).reshape(expert_count, capacity, width))

    def ahead(r):
        return lambda i: (i + r * slices) % devices

    def twin(i):
        return i ^ 1

    def first(i):
        return i ^ (2 if i & 1 else 4)

    def second(i):
        return i ^ (4 if i & 1 else 2)

    blocks = blocks[:1] + [swapped(blocks[r], ahead(r)) for r in range(1, expert_count)]
    early = neighbours(latent_cache, EARLY, slices)
    *blocks, early, mixing = lax.optimization_barrier((*blocks, early, mixing))
    column = jnp.concatenate(blocks)
    near = swapped(column, first)
    side = swapped(column, second)
    across = swapped(near, second)
    beside = swapped(latent_cache, twin)
    twin_column, twin_near = swapped(column, twin), swapped(near, twin)
    weights = fetched([gate_weight, up_weight, down_weight])
    across, twin_column, twin_near, weights, beside, latent_cache = lax.optimization_barrier(
        (across, twin_column, twin_near, weights, beside, latent_cache)
    )
    late = neighbours(latent_cache, LATE, slices)
    held = [column, near, side, across, twin_column, twin_near]
    held = held + [swapped(side, twin), swapped(across, twin)]
    own, high, low = experts(held, weights)
    high, late = lax.optimization_barrier((high, late))

    high, low = swapped(high, twin), swapped(low, twin)
    height = expert_count * capacity
    halves = [(0, width // 2), (width // 2, width)]

    def block(value, j, half):
        return value[j * height : (j + 1) * height, half[0] : half[1]]

    attention = attend(queries, latent_cache, beside, early, late, new_latent, parents, lengths)
    totals, done, token = [], None, None
    for half in halves:
        across = added([block(own, 3, half), block(high, 1, half)]).astype(jnp.bfloat16)
        across = across if token is None else after(across, token)
        later = after(high, across)
        across = swapped(across, second)
        if done is not None:
            across, later = after((across, later), done)
        side = added([block(own, 2, half), block(later, 0, half)]).astype(jnp.bfloat16)
        near = added([block(own, 1, half), block(low, 1, half), across]).astype(jnp.bfloat16)
        if done is not None:
            near, attention = lax.optimization_barrier((near, attention))
        token = near
        near, side = swapped(near, first), swapped(side, second)
        here = [block(own, 0, half), block(low, 0, half), side, near]
        shares = [
            added([v[r * capacity : (r + 1) * capacity] for v in here])
            for r in range(expert_count)
        ]
        done = shares
        values = [
            swapped(shares[r].astype(jnp.bfloat16), ahead(-r)) for r in range(1, expert_count)
        ]
        values = [v.astype(jnp.float32) for v in values]
        if dense:
            weighted = lax.optimization_barrier(mixing[0][:, None] * shares[0])
            total = weighted + sum(
                mixing[r][:, None] * values[r - 1] for r in range(1, expert_count)
            )
        else:
            total = jnp.dot(
                mixing,
                jnp.concatenate([shares[0]] + values),
                precision=lax.Precision.HIGHEST,
                preferred_element_type=jnp.float32,
            )
        totals.append(total.astype(jnp.bfloat16))
    expert_output = jnp.concatenate(totals, axis=1)
    return (attention, expert_output)


def solution(mesh):
    in_specs = (
        P(("groups", "dp"), None, None),
        P(("groups", "dp"), None, None),
        P(("groups", "dp"), None),
        P(("groups", "dp")),
        P(("groups", "dp")),
        P(("groups", "dp"), None),
        P(("groups", "dp"), None),
        P(("groups", "dp"), None),
        P("dp", None, None),
        P("dp", None, None),
        P("dp", None, None),
    )
    out_specs = (P(("groups", "dp"), None, None), P(("groups", "dp"), None))
    return jax.shard_map(body, mesh=mesh, in_specs=in_specs, out_specs=out_specs, check_vma=False)
```

```python
import jax
import jax.numpy as jnp
from jax import lax
from jax.experimental import pallas as pl
from jax.experimental.pallas import tpu as pltpu
from jax.sharding import PartitionSpec as P

FF_E = 2048
KV = 512


score_scale = 192.0 ** (-0.5)


def pair_slots(route_rows, expert_count, capacity):
    flat_experts = route_rows.reshape(-1)
    onehot = (flat_experts[:, None] == jnp.arange(expert_count, dtype=jnp.int32)[None, :]).astype(
        jnp.int32
    )
    position = jnp.sum((jnp.cumsum(onehot, axis=0) - onehot) * onehot, axis=1)
    return (flat_experts * capacity + position).astype(jnp.int32).reshape(route_rows.shape)


def swapped(value, partner):
    peers = lax.axis_size("dp")
    return lax.ppermute(value, "dp", [(i, partner(i)) for i in range(peers)])


def tied(*values):
    return lax.optimization_barrier(values)


def added(values):
    total = values[0].astype(jnp.float32)
    for value in values[1:]:
        total = total + value.astype(jnp.float32)
    return total


EARLY = ((1, 2), (3, 4), (5, 6), (6, 5))
LATE = ((2, 1), (4, 3), (7, 8), (8, 7))


def neighbours(value, moves, slices):
    peers = lax.axis_size("dp")
    pairs = [(base + i, base + j) for base in range(0, peers, slices) for i, j in moves]
    return lax.ppermute(value, "dp", [p for p in pairs if max(p) < peers])


def attend_kernel(spans, parents, lengths, query, own, twin, newest, *refs):
    pieces, out = refs[:-1], refs[-1]
    beams = range(query.shape[0])
    rank = lax.axis_index("dp")
    place = rank % 8
    arrives_early = (place == 2) | (place == 4) | (place == 5) | (place == 6)
    latest = newest[...].astype(jnp.float32)
    at = lax.broadcasted_iota(jnp.int32, own.shape[1:], 0)
    rows, scores, probs = [], [], []
    for b in beams:
        slot, holder = parents[b] % len(beams), parents[b] // len(beams)
        value = own[slot]
        value = jnp.where(holder == (rank ^ 1), twin[slot], value)
        far = (holder != rank) & (holder != (rank ^ 1))
        for (kind, low, high), piece in zip(spans, pieces):
            here = far & (slot >= low) & (slot < high)
            if kind == "early":
                here = here & arrives_early
            if kind == "late":
                here = here & jnp.logical_not(arrives_early)
            value = jnp.where(here, piece[jnp.clip(slot - low, 0, high - low - 1)], value)
        value = jnp.where(at < lengths[b] - 1, value, jnp.zeros_like(value))
        row = jnp.broadcast_to(latest[b : b + 1], value.shape).astype(value.dtype)
        rows.append(jnp.where(at == lengths[b] - 1, row, value))
    for b in beams:
        product = lax.dot_general(
            query[b], rows[b], (((1,), (1,)), ((), ())), preferred_element_type=jnp.float32
        )
        scores.append(product * score_scale)
    at = lax.broadcasted_iota(jnp.int32, scores[0].shape, 1)
    for b in beams:
        value = jnp.where(at < lengths[b], scores[b], -jnp.inf)
        expons = jnp.exp(value - jnp.max(value, axis=1, keepdims=True))
        total = jnp.sum(expons, axis=1, keepdims=True)
        probs.append((expons / total).astype(jnp.bfloat16))
    for b in beams:
        mixed = jnp.dot(probs[b], rows[b][:, :KV], preferred_element_type=jnp.float32)
        out[b] = mixed.astype(out.dtype)


def attend(queries, own, twin, newest, spans, pieces, parents, lengths):
    beam_count, heads, width = queries.shape
    positions = own.shape[1]
    scalars = pl.BlockSpec(memory_space=pltpu.SMEM)
    whole = pl.BlockSpec(memory_space=pltpu.VMEM)
    arrays = [
        pltpu.with_memory_space_constraint(v, pltpu.VMEM)
        for v in (queries, own, twin, newest, *pieces)
    ]
    return pl.pallas_call(
        lambda *refs: attend_kernel(spans, *refs),
        in_specs=[scalars] * 2 + [whole] * len(arrays),
        out_specs=whole,
        out_shape=jax.ShapeDtypeStruct((beam_count, heads, KV), jnp.bfloat16),
        compiler_params=pltpu.CompilerParams(vmem_limit_bytes=16 * 2**20),
        cost_estimate=pl.CostEstimate(
            flops=2 * beam_count * heads * positions * (width + KV),
            bytes_accessed=2 * beam_count * (4 * positions * width + heads * (width + KV)),
            transcendentals=beam_count * heads * positions,
        ),
    )(parents, lengths, *arrays)


def fetch_kernel(*refs):
    count = len(refs) // 2
    sources, targets, sems = refs[:count], refs[count:-1], refs[-1]
    copies = [
        pltpu.make_async_copy(source, target, sems.at[i])
        for i, (source, target) in enumerate(zip(sources, targets))
    ]
    for copy in copies:
        copy.start()
    for copy in copies:
        copy.wait()


def fetched(weights):
    return pl.pallas_call(
        fetch_kernel,
        in_specs=[pl.BlockSpec(memory_space=pltpu.HBM)] * len(weights),
        out_specs=[pl.BlockSpec(memory_space=pltpu.VMEM)] * len(weights),
        out_shape=[pltpu.VMEM(w.shape, w.dtype) for w in weights],
        scratch_shapes=[pltpu.SemaphoreType.DMA((len(weights),))],
        compiler_params=pltpu.CompilerParams(vmem_limit_bytes=16 * 2**20),
        cost_estimate=pl.CostEstimate(
            flops=0,
            bytes_accessed=2 * sum(w.size * w.dtype.itemsize for w in weights),
            transcendentals=0,
        ),
    )(*[pltpu.with_memory_space_constraint(w, pltpu.HBM) for w in weights])


def span(k, wide, begin=0):
    return pl.ds(pl.multiple_of(begin + k * wide, wide), wide)


def sum_products(begin, wide, rows, gate, up, gate_sum, up_sum):
    @pl.loop(0, rows[0].shape[1] // wide)
    def _(k):
        piece = jnp.concatenate([ref[:, span(k, wide)] for ref in rows], axis=0)
        depth = span(k, wide, begin)
        gate_sum[...] += jnp.dot(piece, gate[0, depth, :], preferred_element_type=jnp.float32)
        up_sum[...] += jnp.dot(piece, up[0, depth, :], preferred_element_type=jnp.float32)


def first_kernel(wide, *refs):
    rows, (gate, up, gate_sum, up_sum) = refs[:8], refs[8:]
    gate_sum[...] = jnp.zeros_like(gate_sum)
    up_sum[...] = jnp.zeros_like(up_sum)
    sum_products(0, wide, rows, gate, up, gate_sum, up_sum)


def second_kernel(wide, *refs):
    rows, refs = refs[:8], refs[8:]
    gate, up, down, gate_part, up_part, own, high, low, gate_sum, up_sum = refs
    height = rows[0].shape[0]
    half = 4 * height
    gate_sum[...] = gate_part[...]
    up_sum[...] = up_part[...]
    sum_products(rows[0].shape[1], wide, rows, gate, up, gate_sum, up_sum)
    total = gate_sum[...]
    hidden = (total / (1.0 + jnp.exp(-total)) * up_sum[...]).astype(jnp.bfloat16)

    @pl.loop(0, own.shape[1] // wide)
    def _(k):
        at = span(k, wide)
        product = jnp.dot(hidden, down[0, :, at], preferred_element_type=jnp.float32)
        product = product.astype(jnp.bfloat16)
        own[:, at] = product[:half]
        low[:, at] = product[half : half + 2 * height]
        high[:, at] = product[half + 2 * height :]


def step_width(width):
    return max(w for w in (128, 256, 512, 896) if width % w == 0)


def first_half(rows, weights):
    height, width = rows[0].shape
    units = weights[0].shape[2]
    total = len(rows) * height
    whole = pl.BlockSpec(memory_space=pltpu.VMEM)
    inputs = [pltpu.with_memory_space_constraint(v, pltpu.VMEM) for v in (*rows, *weights[:2])]
    return pl.pallas_call(
        lambda *refs: first_kernel(step_width(width), *refs),
        in_specs=[whole] * len(inputs),
        out_specs=[whole] * 2,
        out_shape=[pltpu.VMEM((total, units), jnp.float32)] * 2,
        compiler_params=pltpu.CompilerParams(vmem_limit_bytes=24 * 2**20),
        cost_estimate=pl.CostEstimate(
            flops=4 * total * width * units,
            bytes_accessed=4 * width * units + 2 * total * width,
            transcendentals=0,
        ),
    )(*inputs)


def second_half(rows, weights, sums):
    height, width = rows[0].shape
    units = weights[0].shape[2]
    total = len(rows) * height
    whole = pl.BlockSpec(memory_space=pltpu.VMEM)
    inputs = [
        pltpu.with_memory_space_constraint(v, pltpu.VMEM) for v in (*rows, *weights, *sums)
    ]
    return pl.pallas_call(
        lambda *refs: second_kernel(step_width(width), *refs),
        in_specs=[whole] * len(inputs),
        out_specs=[whole] * 3,
        out_shape=[pltpu.VMEM((count * height, 2 * width), jnp.bfloat16) for count in (4, 2, 2)],
        scratch_shapes=[
            pltpu.VMEM((total, units), jnp.float32),
            pltpu.VMEM((total, units), jnp.float32),
        ],
        compiler_params=pltpu.CompilerParams(vmem_limit_bytes=24 * 2**20),
        cost_estimate=pl.CostEstimate(
            flops=8 * total * width * units,
            bytes_accessed=8 * width * units + 6 * total * width,
            transcendentals=total * units,
        ),
    )(*inputs)


def body(
    queries,
    latent_cache,
    new_latent,
    parents,
    lengths,
    expert_input,
    routed_experts,
    route_weights,
    gate_weight,
    up_weight,
    down_weight,
):
    beam_count, width = expert_input.shape
    devices = lax.axis_size("dp")
    slices = FF_E // gate_weight.shape[2]
    expert_count = devices // slices
    route_count = routed_experts.shape[1]
    capacity = min(beam_count, max(2, 2 * beam_count * route_count // expert_count))
    dense = capacity == beam_count
    assert slices == 8

    mine = lax.axis_index("dp") // slices
    turns = jnp.arange(expert_count, dtype=jnp.int32)
    targets = (mine + turns) % expert_count
    if dense:
        blocks = [expert_input] * expert_count
        mixing = [
            jnp.sum(jnp.where(routed_experts == targets[r], route_weights, 0.0), axis=1)
            for r in range(expert_count)
        ]
    else:
        slots = pair_slots(routed_experts, expert_count, capacity)
        wanted = targets[:, None] * capacity + jnp.arange(capacity, dtype=jnp.int32)
        matches = (slots[:, :, None] == wanted.reshape(-1)).astype(jnp.float32)
        mixing = jnp.sum(route_weights[:, :, None] * matches, axis=1)
        selector = jnp.sum(matches, axis=1).T.astype(jnp.bfloat16)
        chosen = jnp.dot(selector, expert_input, preferred_element_type=jnp.float32)
        blocks = list(chosen.astype(jnp.bfloat16).reshape(expert_count, capacity, width))

    def ahead(r):
        return lambda i: (i + r * slices) % devices

    def twin(i):
        return i ^ 1

    def first(i):
        return i ^ (2 if i & 1 else 4)

    def second(i):
        return i ^ (4 if i & 1 else 2)

    halves = [(0, width // 2), (width // 2, width)]
    last = 3 * beam_count // 4
    middle = beam_count // 2
    spans, pieces = [], []

    def cache_rows(kind, begin, end, ready=None):
        moves = {"early": EARLY, "late": LATE, "both": EARLY + LATE}[kind]
        source = latent_cache[begin:end]
        if ready is not None:
            source, ready = tied(source, ready)
        spans.append((kind, begin, end))
        return neighbours(source, moves, slices), ready

    def cut(half):
        return [block[:, half[0] : half[1]] for block in blocks]

    def to_column(cuts):
        return cuts[:1] + [swapped(cuts[r], ahead(r)) for r in range(1, expert_count)]

    def to_plane(column):
        near = swapped(column, first)
        return [column, near, swapped(column, second), swapped(near, second)]

    column = to_column(cut(halves[0]))
    column[1], later = tied(column[1], cut(halves[1]))
    early, _ = cache_rows("early", 0, last)
    weights = fetched([gate_weight, up_weight, down_weight])
    column, early, mixing, weights = tied(column, early, mixing, weights)
    pieces.append(early)
    held = to_plane(jnp.concatenate(column))
    later = to_column(later)
    later, held = tied(later, held)
    held_later = to_plane(jnp.concatenate(later))
    beside = swapped(latent_cache, twin)
    held = held + [swapped(value, twin) for value in held]
    held, held_later[2] = tied(held, held_later[2])
    sums = first_half(held, weights)
    held_later[3], sums, beside = tied(held_later[3], sums, beside)
    late, held_later[3] = cache_rows("late", 0, middle, held_later[3])
    held_later = held_later + [swapped(value, twin) for value in held_later]
    own, high, low = second_half(held_later, weights, sums)
    high, late = tied(high, late)
    pieces.append(late)
    late, own = cache_rows("late", middle, last, own)

    high, low = swapped(high, twin), swapped(low, twin)
    height = expert_count * capacity

    def block(value, j, half):
        return value[j * height : (j + 1) * height, half[0] : half[1]]

    def to_second(half):
        return added([block(own, 3, half), block(high, 1, half)]).astype(jnp.bfloat16)

    def to_first(half, across):
        return added([block(own, 1, half), block(low, 1, half), across]).astype(jnp.bfloat16)

    def to_side(half):
        return added([block(own, 2, half), block(high, 0, half)]).astype(jnp.bfloat16)

    def shares(half, side, near):
        here = [block(own, 0, half), block(low, 0, half), side, near]
        return [
            added([v[r * capacity : (r + 1) * capacity] for v in here])
            for r in range(expert_count)
        ]

    def back(share):
        return [
            swapped(share[r].astype(jnp.bfloat16), ahead(-r)) for r in range(1, expert_count)
        ]

    across, late = tied(to_second(halves[0]), late)
    pieces.append(late)
    across, high = tied(across, high)
    across = swapped(across, second)
    near, side = to_first(halves[0], across), to_side(halves[0])
    near, across = tied(near, to_second(halves[1]))
    near, side, across = swapped(near, first), swapped(side, second), swapped(across, second)
    share = shares(halves[0], side, near)
    share, across, high = tied(share, across, high)
    values = [[share[0]] + back(share)]
    near, side = to_first(halves[1], across), to_side(halves[1])
    near, side = swapped(near, first), swapped(side, second)
    near, side, values[0] = tied(near, side, values[0])
    share = shares(halves[1], side, near)
    rest, share = cache_rows("both", last, beam_count, share)
    pieces.append(rest)
    values.append([share[0]] + back(share))
    attention = attend(
        queries, latent_cache, beside, new_latent, spans, pieces, parents, lengths
    )
    values, attention = tied(values, attention)
    totals = []
    for value in values:
        value = [v.astype(jnp.float32) for v in value]
        if dense:
            total = sum(mixing[r][:, None] * value[r] for r in range(expert_count))
        else:
            total = jnp.dot(
                mixing,
                jnp.concatenate(value),
                precision=lax.Precision.HIGHEST,
                preferred_element_type=jnp.float32,
            )
        totals.append(total.astype(jnp.bfloat16))
    expert_output = jnp.concatenate(totals, axis=1)
    return (attention, expert_output)


def solution(mesh):
    in_specs = (
        P(("groups", "dp"), None, None),
        P(("groups", "dp"), None, None),
        P(("groups", "dp"), None),
        P(("groups", "dp")),
        P(("groups", "dp")),
        P(("groups", "dp"), None),
        P(("groups", "dp"), None),
        P(("groups", "dp"), None),
        P("dp", None, None),
        P("dp", None, None),
        P("dp", None, None),
    )
    out_specs = (P(("groups", "dp"), None, None), P(("groups", "dp"), None))
    return jax.shard_map(body, mesh=mesh, in_specs=in_specs, out_specs=out_specs, check_vma=False)
```

```python
import jax
import jax.numpy as jnp
from jax import lax
from jax.experimental import pallas as pl
from jax.experimental.pallas import tpu as pltpu
from jax.sharding import PartitionSpec as P

FF_E = 2048
KV = 512


score_scale = 192.0 ** (-0.5)


def pair_slots(route_rows, expert_count, capacity):
    flat_experts = route_rows.reshape(-1)
    onehot = (flat_experts[:, None] == jnp.arange(expert_count, dtype=jnp.int32)[None, :]).astype(
        jnp.int32
    )
    position = jnp.sum((jnp.cumsum(onehot, axis=0) - onehot) * onehot, axis=1)
    return (flat_experts * capacity + position).astype(jnp.int32).reshape(route_rows.shape)


def swapped(value, partner):
    peers = lax.axis_size("dp")
    return lax.ppermute(value, "dp", [(i, partner(i)) for i in range(peers)])


def tied(*values):
    return lax.optimization_barrier(values)


def added(values):
    total = values[0].astype(jnp.float32)
    for value in values[1:]:
        total = total + value.astype(jnp.float32)
    return total


EARLY = ((1, 2), (3, 4), (5, 6), (6, 5))
LATE = ((2, 1), (4, 3), (7, 8), (8, 7))


def neighbours(value, moves, slices):
    peers = lax.axis_size("dp")
    pairs = [(base + i, base + j) for base in range(0, peers, slices) for i, j in moves]
    return lax.ppermute(value, "dp", [p for p in pairs if max(p) < peers])


def attend_kernel(spans, parents, lengths, query, own, twin, newest, *refs):
    pieces, out = refs[:-1], refs[-1]
    beams = range(query.shape[0])
    rank = lax.axis_index("dp")
    place = rank % 8
    arrives_early = (place == 2) | (place == 4) | (place == 5) | (place == 6)
    latest = newest[...].astype(jnp.float32)
    at = lax.broadcasted_iota(jnp.int32, own.shape[1:], 0)
    rows, scores, probs = [], [], []
    for b in beams:
        slot, holder = parents[b] % len(beams), parents[b] // len(beams)
        value = own[slot]
        value = jnp.where(holder == (rank ^ 1), twin[slot], value)
        far = (holder != rank) & (holder != (rank ^ 1))
        for (kind, low, high), piece in zip(spans, pieces):
            here = far & (slot >= low) & (slot < high)
            if kind == "early":
                here = here & arrives_early
            if kind == "late":
                here = here & jnp.logical_not(arrives_early)
            value = jnp.where(here, piece[jnp.clip(slot - low, 0, high - low - 1)], value)
        value = jnp.where(at < lengths[b] - 1, value, jnp.zeros_like(value))
        row = jnp.broadcast_to(latest[b : b + 1], value.shape).astype(value.dtype)
        rows.append(jnp.where(at == lengths[b] - 1, row, value))
    for b in beams:
        product = lax.dot_general(
            query[b], rows[b], (((1,), (1,)), ((), ())), preferred_element_type=jnp.float32
        )
        scores.append(product * score_scale)
    at = lax.broadcasted_iota(jnp.int32, scores[0].shape, 1)
    for b in beams:
        value = jnp.where(at < lengths[b], scores[b], -jnp.inf)
        expons = jnp.exp(value - jnp.max(value, axis=1, keepdims=True))
        total = jnp.sum(expons, axis=1, keepdims=True)
        probs.append((expons / total).astype(jnp.bfloat16))
    for b in beams:
        mixed = jnp.dot(probs[b], rows[b][:, :KV], preferred_element_type=jnp.float32)
        out[b] = mixed.astype(out.dtype)


def attend(queries, own, twin, newest, spans, pieces, parents, lengths):
    beam_count, heads, width = queries.shape
    positions = own.shape[1]
    scalars = pl.BlockSpec(memory_space=pltpu.SMEM)
    whole = pl.BlockSpec(memory_space=pltpu.VMEM)
    arrays = [
        pltpu.with_memory_space_constraint(v, pltpu.VMEM)
        for v in (queries, own, twin, newest, *pieces)
    ]
    return pl.pallas_call(
        lambda *refs: attend_kernel(spans, *refs),
        in_specs=[scalars] * 2 + [whole] * len(arrays),
        out_specs=whole,
        out_shape=jax.ShapeDtypeStruct((beam_count, heads, KV), jnp.bfloat16),
        compiler_params=pltpu.CompilerParams(vmem_limit_bytes=16 * 2**20),
        cost_estimate=pl.CostEstimate(
            flops=2 * beam_count * heads * positions * (width + KV),
            bytes_accessed=2 * beam_count * (4 * positions * width + heads * (width + KV)),
            transcendentals=beam_count * heads * positions,
        ),
    )(parents, lengths, *arrays)


def fetch_kernel(*refs):
    count = len(refs) // 2
    sources, targets, sems = refs[:count], refs[count:-1], refs[-1]
    copies = [
        pltpu.make_async_copy(source, target, sems.at[i])
        for i, (source, target) in enumerate(zip(sources, targets))
    ]
    for copy in copies:
        copy.start()
    for copy in copies:
        copy.wait()


def fetched(weights):
    return pl.pallas_call(
        fetch_kernel,
        in_specs=[pl.BlockSpec(memory_space=pltpu.HBM)] * len(weights),
        out_specs=[pl.BlockSpec(memory_space=pltpu.VMEM)] * len(weights),
        out_shape=[pltpu.VMEM(w.shape, w.dtype) for w in weights],
        scratch_shapes=[pltpu.SemaphoreType.DMA((len(weights),))],
        compiler_params=pltpu.CompilerParams(vmem_limit_bytes=16 * 2**20),
        cost_estimate=pl.CostEstimate(
            flops=0,
            bytes_accessed=2 * sum(w.size * w.dtype.itemsize for w in weights),
            transcendentals=0,
        ),
    )(*[pltpu.with_memory_space_constraint(w, pltpu.HBM) for w in weights])


def expert_kernel(wide, *refs):
    rows, refs = refs[:8], refs[8:]
    gate, up, down, own, high, low, gate_sum, up_sum = refs
    height, width = rows[0].shape
    half = 4 * height

    def span(k):
        return pl.ds(pl.multiple_of(k * wide, wide), wide)

    gate_sum[...] = jnp.zeros_like(gate_sum)
    up_sum[...] = jnp.zeros_like(up_sum)

    @pl.loop(0, width // wide)
    def _(k):
        piece = jnp.concatenate([ref[:, span(k)] for ref in rows], axis=0)
        gate_sum[...] += jnp.dot(piece, gate[0, span(k), :], preferred_element_type=jnp.float32)
        up_sum[...] += jnp.dot(piece, up[0, span(k), :], preferred_element_type=jnp.float32)

    total = gate_sum[...]
    hidden = (total / (1.0 + jnp.exp(-total)) * up_sum[...]).astype(jnp.bfloat16)

    @pl.loop(0, width // wide)
    def _(k):
        product = jnp.dot(hidden, down[0, :, span(k)], preferred_element_type=jnp.float32)
        product = product.astype(jnp.bfloat16)
        own[:, span(k)] = product[:half]
        low[:, span(k)] = product[half : half + 2 * height]
        high[:, span(k)] = product[half + 2 * height :]


def experts(rows, weights):
    height, width = rows[0].shape
    units = weights[0].shape[2]
    wide = max(w for w in (128, 256, 512, 1024) if width % w == 0)
    total = len(rows) * height
    whole = pl.BlockSpec(memory_space=pltpu.VMEM)
    inputs = [pltpu.with_memory_space_constraint(v, pltpu.VMEM) for v in (*rows, *weights)]
    return pl.pallas_call(
        lambda *refs: expert_kernel(wide, *refs),
        in_specs=[whole] * len(inputs),
        out_specs=[whole] * 3,
        out_shape=[pltpu.VMEM((count * height, width), jnp.bfloat16) for count in (4, 2, 2)],
        scratch_shapes=[
            pltpu.VMEM((total, units), jnp.float32),
            pltpu.VMEM((total, units), jnp.float32),
        ],
        compiler_params=pltpu.CompilerParams(vmem_limit_bytes=28 * 2**20),
        cost_estimate=pl.CostEstimate(
            flops=6 * total * width * units,
            bytes_accessed=6 * width * units + 4 * total * width,
            transcendentals=total * units,
        ),
    )(*inputs)


def body(
    queries,
    latent_cache,
    new_latent,
    parents,
    lengths,
    expert_input,
    routed_experts,
    route_weights,
    gate_weight,
    up_weight,
    down_weight,
):
    beam_count, width = expert_input.shape
    devices = lax.axis_size("dp")
    slices = FF_E // gate_weight.shape[2]
    expert_count = devices // slices
    route_count = routed_experts.shape[1]
    capacity = min(beam_count, max(2, 2 * beam_count * route_count // expert_count))
    dense = capacity == beam_count
    assert slices == 8 and expert_count & (expert_count - 1) == 0

    mine = lax.axis_index("dp") // slices
    turns = jnp.arange(expert_count, dtype=jnp.int32)
    targets = mine ^ turns
    if dense:
        blocks = [expert_input] * expert_count
        mixing = [
            jnp.sum(jnp.where(routed_experts == targets[r], route_weights, 0.0), axis=1)
            for r in range(expert_count)
        ]
    else:
        slots = pair_slots(routed_experts, expert_count, capacity)
        wanted = targets[:, None] * capacity + jnp.arange(capacity, dtype=jnp.int32)
        matches = (slots[:, :, None] == wanted.reshape(-1)).astype(jnp.float32)
        mixing = jnp.sum(route_weights[:, :, None] * matches, axis=1)
        selector = jnp.sum(matches, axis=1).T.astype(jnp.bfloat16)
        chosen = jnp.dot(selector, expert_input, preferred_element_type=jnp.float32)
        blocks = list(chosen.astype(jnp.bfloat16).reshape(expert_count, capacity, width))

    def ahead(r):
        return lambda i: i ^ (r * slices)

    def twin(i):
        return i ^ 1

    def first(i):
        return i ^ (2 if i & 1 else 4)

    def second(i):
        return i ^ (4 if i & 1 else 2)

    spans, pieces = [], []

    def cache_rows(kind, begin, end, ready=None):
        moves = {"early": EARLY, "late": LATE}[kind]
        source = latent_cache[begin:end]
        if ready is not None:
            source, ready = tied(source, ready)
        spans.append((kind, begin, end))
        return neighbours(source, moves, slices), ready

    column = blocks[:1] + [swapped(blocks[r], ahead(r)) for r in range(1, expert_count)]
    early, _ = cache_rows("early", 0, beam_count)
    weights = fetched([gate_weight, up_weight, down_weight])
    column, early, weights = tied(column, early, weights)
    pieces.append(early)
    column = jnp.concatenate(column)
    near = swapped(column, first)
    side = swapped(column, second)
    across = swapped(near, second)
    beside = swapped(latent_cache, twin)
    twin_column, twin_near = swapped(column, twin), swapped(near, twin)
    across, twin_column, twin_near, beside, mixing = tied(
        across, twin_column, twin_near, beside, mixing
    )
    late, across = cache_rows("late", 0, beam_count, across)
    twin_across, side = tied(swapped(across, twin), side)
    held = [column, near, side, across, twin_column, twin_near, swapped(side, twin), twin_across]
    own, high, low = experts(held, weights)
    high, late = tied(high, late)
    pieces.append(late)

    high, low = swapped(high, twin), swapped(low, twin)
    height = expert_count * capacity

    cut = 128 * (5 * width // 1024)
    halves = [(0, cut), (cut, width)]

    def block(value, j, half):
        return value[j * height : (j + 1) * height, half[0] : half[1]]

    def to_second(half):
        return added([block(own, 3, half), block(high, 1, half)]).astype(jnp.bfloat16)

    def to_first(half, across):
        return added([block(own, 1, half), block(low, 1, half), across]).astype(jnp.bfloat16)

    def to_side(half):
        return added([block(own, 2, half), block(high, 0, half)]).astype(jnp.bfloat16)

    def shares(half, side, near):
        here = [block(own, 0, half), block(low, 0, half), side, near]
        return [
            added([v[r * capacity : (r + 1) * capacity] for v in here])
            for r in range(expert_count)
        ]

    def back(share):
        return [
            swapped(share[r].astype(jnp.bfloat16), ahead(r)) for r in range(1, expert_count)
        ]

    across, high = tied(to_second(halves[0]), high)
    across = swapped(across, second)
    near, side = to_first(halves[0], across), to_side(halves[0])
    near, across = tied(near, to_second(halves[1]))
    near, side, across = swapped(near, first), swapped(side, second), swapped(across, second)
    share = shares(halves[0], side, near)
    share, across, high = tied(share, across, high)
    values = [[share[0]] + back(share)]
    near, side = to_first(halves[1], across), to_side(halves[1])
    attention = attend(
        queries, latent_cache, beside, new_latent, spans, pieces, parents, lengths
    )
    near, attention = tied(near, attention)
    near, side = swapped(near, first), swapped(side, second)
    share = shares(halves[1], side, near)
    values.append([share[0]] + back(share))
    totals = []
    for value in values:
        value = [v.astype(jnp.float32) for v in value]
        if dense:
            total = sum(mixing[r][:, None] * value[r] for r in range(expert_count))
        else:
            total = jnp.dot(
                mixing,
                jnp.concatenate(value),
                precision=lax.Precision.HIGHEST,
                preferred_element_type=jnp.float32,
            )
        totals.append(total.astype(jnp.bfloat16))
    expert_output = jnp.concatenate(totals, axis=1)
    return (attention, expert_output)


def solution(mesh):
    in_specs = (
        P(("groups", "dp"), None, None),
        P(("groups", "dp"), None, None),
        P(("groups", "dp"), None),
        P(("groups", "dp")),
        P(("groups", "dp")),
        P(("groups", "dp"), None),
        P(("groups", "dp"), None),
        P(("groups", "dp"), None),
        P("dp", None, None),
        P("dp", None, None),
        P("dp", None, None),
    )
    out_specs = (P(("groups", "dp"), None, None), P(("groups", "dp"), None))
    return jax.shard_map(body, mesh=mesh, in_specs=in_specs, out_specs=out_specs, check_vma=False)
```

```python
import jax
import jax.numpy as jnp
from jax import lax
from jax.experimental import pallas as pl
from jax.experimental.pallas import tpu as pltpu
from jax.sharding import PartitionSpec as P

FF_E = 2048
KV = 512


score_scale = 192.0 ** (-0.5)


def pair_slots(route_rows, expert_count, capacity):
    flat_experts = route_rows.reshape(-1)
    onehot = (flat_experts[:, None] == jnp.arange(expert_count, dtype=jnp.int32)[None, :]).astype(
        jnp.int32
    )
    position = jnp.sum((jnp.cumsum(onehot, axis=0) - onehot) * onehot, axis=1)
    return (flat_experts * capacity + position).astype(jnp.int32).reshape(route_rows.shape)


def swapped(value, partner):
    peers = lax.axis_size("dp")
    return lax.ppermute(value, "dp", [(i, partner(i)) for i in range(peers)])


def tied(*values):
    return lax.optimization_barrier(values)


def added(values):
    total = values[0].astype(jnp.float32)
    for value in values[1:]:
        total = total + value.astype(jnp.float32)
    return total


EARLY = ((1, 2), (3, 4), (5, 6), (6, 5))
LATE = ((2, 1), (4, 3), (7, 8), (8, 7))


def neighbours(value, moves, slices):
    peers = lax.axis_size("dp")
    pairs = [(base + i, base + j) for base in range(0, peers, slices) for i, j in moves]
    return lax.ppermute(value, "dp", [p for p in pairs if max(p) < peers])


def attend_kernel(spans, parents, lengths, query, own, twin, newest, *refs):
    pieces, out = refs[:-1], refs[-1]
    beams = range(query.shape[0])
    rank = lax.axis_index("dp")
    place = rank % 8
    arrives_early = (place == 2) | (place == 4) | (place == 5) | (place == 6)
    latest = newest[...].astype(jnp.float32)
    at = lax.broadcasted_iota(jnp.int32, own.shape[1:], 0)
    rows, scores, probs = [], [], []
    for b in beams:
        slot, holder = parents[b] % len(beams), parents[b] // len(beams)
        value = own[slot]
        value = jnp.where(holder == (rank ^ 1), twin[slot], value)
        far = (holder != rank) & (holder != (rank ^ 1))
        for (kind, low, high), piece in zip(spans, pieces):
            here = far & (slot >= low) & (slot < high)
            if kind == "early":
                here = here & arrives_early
            if kind == "late":
                here = here & jnp.logical_not(arrives_early)
            value = jnp.where(here, piece[jnp.clip(slot - low, 0, high - low - 1)], value)
        value = jnp.where(at < lengths[b] - 1, value, jnp.zeros_like(value))
        row = jnp.broadcast_to(latest[b : b + 1], value.shape).astype(value.dtype)
        rows.append(jnp.where(at == lengths[b] - 1, row, value))
    for b in beams:
        product = lax.dot_general(
            query[b], rows[b], (((1,), (1,)), ((), ())), preferred_element_type=jnp.float32
        )
        scores.append(product * score_scale)
    at = lax.broadcasted_iota(jnp.int32, scores[0].shape, 1)
    for b in beams:
        value = jnp.where(at < lengths[b], scores[b], -jnp.inf)
        expons = jnp.exp(value - jnp.max(value, axis=1, keepdims=True))
        total = jnp.sum(expons, axis=1, keepdims=True)
        probs.append((expons / total).astype(jnp.bfloat16))
    for b in beams:
        mixed = jnp.dot(probs[b], rows[b][:, :KV], preferred_element_type=jnp.float32)
        out[b] = mixed.astype(out.dtype)


def attend(queries, own, twin, newest, spans, pieces, parents, lengths):
    beam_count, heads, width = queries.shape
    positions = own.shape[1]
    scalars = pl.BlockSpec(memory_space=pltpu.SMEM)
    whole = pl.BlockSpec(memory_space=pltpu.VMEM)
    arrays = [
        pltpu.with_memory_space_constraint(v, pltpu.VMEM)
        for v in (queries, own, twin, newest, *pieces)
    ]
    return pl.pallas_call(
        lambda *refs: attend_kernel(spans, *refs),
        in_specs=[scalars] * 2 + [whole] * len(arrays),
        out_specs=whole,
        out_shape=jax.ShapeDtypeStruct((beam_count, heads, KV), jnp.bfloat16),
        compiler_params=pltpu.CompilerParams(vmem_limit_bytes=16 * 2**20),
        cost_estimate=pl.CostEstimate(
            flops=2 * beam_count * heads * positions * (width + KV),
            bytes_accessed=2 * beam_count * (4 * positions * width + heads * (width + KV)),
            transcendentals=beam_count * heads * positions,
        ),
    )(parents, lengths, *arrays)


def fetch_kernel(*refs):
    count = len(refs) // 2
    sources, targets, sems = refs[:count], refs[count:-1], refs[-1]
    copies = [
        pltpu.make_async_copy(source, target, sems.at[i])
        for i, (source, target) in enumerate(zip(sources, targets))
    ]
    for copy in copies:
        copy.start()
    for copy in copies:
        copy.wait()


def fetched(weights):
    return pl.pallas_call(
        fetch_kernel,
        in_specs=[pl.BlockSpec(memory_space=pltpu.HBM)] * len(weights),
        out_specs=[pl.BlockSpec(memory_space=pltpu.VMEM)] * len(weights),
        out_shape=[pltpu.VMEM(w.shape, w.dtype) for w in weights],
        scratch_shapes=[pltpu.SemaphoreType.DMA((len(weights),))],
        compiler_params=pltpu.CompilerParams(vmem_limit_bytes=16 * 2**20),
        cost_estimate=pl.CostEstimate(
            flops=0,
            bytes_accessed=2 * sum(w.size * w.dtype.itemsize for w in weights),
            transcendentals=0,
        ),
    )(*[pltpu.with_memory_space_constraint(w, pltpu.HBM) for w in weights])


def expert_kernel(wide, *refs):
    rows, refs = refs[:8], refs[8:]
    gate, up, down, own, high, low, gate_sum, up_sum = refs
    height, width = rows[0].shape
    half = 4 * height

    def span(k):
        return pl.ds(pl.multiple_of(k * wide, wide), wide)

    gate_sum[...] = jnp.zeros_like(gate_sum)
    up_sum[...] = jnp.zeros_like(up_sum)

    @pl.loop(0, width // wide)
    def _(k):
        piece = jnp.concatenate([ref[:, span(k)] for ref in rows], axis=0)
        gate_sum[...] += jnp.dot(piece, gate[0, span(k), :], preferred_element_type=jnp.float32)
        up_sum[...] += jnp.dot(piece, up[0, span(k), :], preferred_element_type=jnp.float32)

    total = gate_sum[...]
    hidden = (total / (1.0 + jnp.exp(-total)) * up_sum[...]).astype(jnp.bfloat16)

    @pl.loop(0, width // wide)
    def _(k):
        product = jnp.dot(hidden, down[0, :, span(k)], preferred_element_type=jnp.float32)
        product = product.astype(jnp.bfloat16)
        own[:, span(k)] = product[:half]
        low[:, span(k)] = product[half : half + 2 * height]
        high[:, span(k)] = product[half + 2 * height :]


def experts(rows, weights):
    height, width = rows[0].shape
    units = weights[0].shape[2]
    wide = max(w for w in (128, 256, 512, 1024) if width % w == 0)
    total = len(rows) * height
    whole = pl.BlockSpec(memory_space=pltpu.VMEM)
    inputs = [pltpu.with_memory_space_constraint(v, pltpu.VMEM) for v in (*rows, *weights)]
    return pl.pallas_call(
        lambda *refs: expert_kernel(wide, *refs),
        in_specs=[whole] * len(inputs),
        out_specs=[whole] * 3,
        out_shape=[pltpu.VMEM((count * height, width), jnp.bfloat16) for count in (4, 2, 2)],
        scratch_shapes=[
            pltpu.VMEM((total, units), jnp.float32),
            pltpu.VMEM((total, units), jnp.float32),
        ],
        compiler_params=pltpu.CompilerParams(vmem_limit_bytes=28 * 2**20),
        cost_estimate=pl.CostEstimate(
            flops=6 * total * width * units,
            bytes_accessed=6 * width * units + 4 * total * width,
            transcendentals=total * units,
        ),
    )(*inputs)


def body(
    queries,
    latent_cache,
    new_latent,
    parents,
    lengths,
    expert_input,
    routed_experts,
    route_weights,
    gate_weight,
    up_weight,
    down_weight,
):
    beam_count, width = expert_input.shape
    devices = lax.axis_size("dp")
    slices = FF_E // gate_weight.shape[2]
    expert_count = devices // slices
    route_count = routed_experts.shape[1]
    capacity = min(beam_count, max(2, 2 * beam_count * route_count // expert_count))
    dense = capacity == beam_count
    assert slices == 8 and expert_count & (expert_count - 1) == 0

    mine = lax.axis_index("dp") // slices
    turns = jnp.arange(expert_count, dtype=jnp.int32)
    targets = mine ^ turns
    if dense:
        blocks = [expert_input] * expert_count
        mixing = [
            jnp.sum(jnp.where(routed_experts == targets[r], route_weights, 0.0), axis=1)
            for r in range(expert_count)
        ]
    else:
        slots = pair_slots(routed_experts, expert_count, capacity)
        wanted = targets[:, None] * capacity + jnp.arange(capacity, dtype=jnp.int32)
        matches = (slots[:, :, None] == wanted.reshape(-1)).astype(jnp.float32)
        mixing = jnp.sum(route_weights[:, :, None] * matches, axis=1)
        selector = jnp.sum(matches, axis=1).T.astype(jnp.bfloat16)
        chosen = jnp.dot(selector, expert_input, preferred_element_type=jnp.float32)
        blocks = list(chosen.astype(jnp.bfloat16).reshape(expert_count, capacity, width))

    def ahead(r):
        return lambda i: i ^ (r * slices)

    def twin(i):
        return i ^ 1

    def first(i):
        return i ^ (2 if i & 1 else 4)

    def second(i):
        return i ^ (4 if i & 1 else 2)

    spans, pieces = [], []

    def cache_rows(kind, begin, end, ready=None):
        moves = {"early": EARLY, "late": LATE}[kind]
        source = latent_cache[begin:end]
        if ready is not None:
            source, ready = tied(source, ready)
        spans.append((kind, begin, end))
        return neighbours(source, moves, slices), ready

    column = blocks[:1] + [swapped(blocks[r], ahead(r)) for r in range(1, expert_count)]
    early, _ = cache_rows("early", 0, beam_count)
    column, early, mixing = tied(column, early, mixing)
    pieces.append(early)
    column = jnp.concatenate(column)
    near = swapped(column, first)
    side = swapped(column, second)
    across = swapped(near, second)
    beside = swapped(latent_cache, twin)
    twin_column, twin_near = swapped(column, twin), swapped(near, twin)
    weights = fetched([gate_weight, up_weight, down_weight])
    across, twin_column, twin_near, weights, beside = tied(
        across, twin_column, twin_near, weights, beside
    )
    middle = 5 * beam_count // 8
    late, across = cache_rows("late", 0, middle, across)
    held = [column, near, side, across, twin_column, twin_near]
    held = held + [swapped(side, twin), swapped(across, twin)]
    own, high, low = experts(held, weights)
    high, late = tied(high, late)
    pieces.append(late)

    high, low = swapped(high, twin), swapped(low, twin)
    height = expert_count * capacity

    cut = 128 * (5 * width // 1024)
    halves = [(0, cut), (cut, width)]

    def block(value, j, half):
        return value[j * height : (j + 1) * height, half[0] : half[1]]

    def to_second(half):
        return added([block(own, 3, half), block(high, 1, half)]).astype(jnp.bfloat16)

    def to_first(half, across):
        return added([block(own, 1, half), block(low, 1, half), across]).astype(jnp.bfloat16)

    def to_side(half):
        return added([block(own, 2, half), block(high, 0, half)]).astype(jnp.bfloat16)

    def shares(half, side, near):
        here = [block(own, 0, half), block(low, 0, half), side, near]
        return [
            added([v[r * capacity : (r + 1) * capacity] for v in here])
            for r in range(expert_count)
        ]

    def back(share):
        return [
            swapped(share[r].astype(jnp.bfloat16), ahead(r)) for r in range(1, expert_count)
        ]

    across, high = tied(to_second(halves[0]), high)
    late, across = cache_rows("late", middle, beam_count, across)
    across = swapped(across, second)
    across, late = tied(across, late)
    pieces.append(late)
    near, side = to_first(halves[0], across), to_side(halves[0])
    near, across = tied(near, to_second(halves[1]))
    near, side, across = swapped(near, first), swapped(side, second), swapped(across, second)
    share = shares(halves[0], side, near)
    share, across, high = tied(share, across, high)
    values = [[share[0]] + back(share)]
    near, side = to_first(halves[1], across), to_side(halves[1])
    attention = attend(
        queries, latent_cache, beside, new_latent, spans, pieces, parents, lengths
    )
    near, attention = tied(near, attention)
    near, side = swapped(near, first), swapped(side, second)
    share = shares(halves[1], side, near)
    values.append([share[0]] + back(share))
    totals = []
    for value in values:
        value = [v.astype(jnp.float32) for v in value]
        if dense:
            total = sum(mixing[r][:, None] * value[r] for r in range(expert_count))
        else:
            total = jnp.dot(
                mixing,
                jnp.concatenate(value),
                precision=lax.Precision.HIGHEST,
                preferred_element_type=jnp.float32,
            )
        totals.append(total.astype(jnp.bfloat16))
    expert_output = jnp.concatenate(totals, axis=1)
    return (attention, expert_output)


def solution(mesh):
    in_specs = (
        P(("groups", "dp"), None, None),
        P(("groups", "dp"), None, None),
        P(("groups", "dp"), None),
        P(("groups", "dp")),
        P(("groups", "dp")),
        P(("groups", "dp"), None),
        P(("groups", "dp"), None),
        P(("groups", "dp"), None),
        P("dp", None, None),
        P("dp", None, None),
        P("dp", None, None),
    )
    out_specs = (P(("groups", "dp"), None, None), P(("groups", "dp"), None))
    return jax.shard_map(body, mesh=mesh, in_specs=in_specs, out_specs=out_specs, check_vma=False)
```

```python
import jax
import jax.numpy as jnp
from jax import lax
from jax.experimental import pallas as pl
from jax.experimental.pallas import tpu as pltpu
from jax.sharding import PartitionSpec as P

FF_E = 2048
KV = 512


score_scale = 192.0 ** (-0.5)


def pair_slots(route_rows, expert_count, capacity):
    flat_experts = route_rows.reshape(-1)
    onehot = (flat_experts[:, None] == jnp.arange(expert_count, dtype=jnp.int32)[None, :]).astype(
        jnp.int32
    )
    position = jnp.sum((jnp.cumsum(onehot, axis=0) - onehot) * onehot, axis=1)
    return (flat_experts * capacity + position).astype(jnp.int32).reshape(route_rows.shape)


def swapped(value, partner):
    peers = lax.axis_size("dp")
    return lax.ppermute(value, "dp", [(i, partner(i)) for i in range(peers)])


def tied(*values):
    return lax.optimization_barrier(values)


def added(values):
    total = values[0].astype(jnp.float32)
    for value in values[1:]:
        total = total + value.astype(jnp.float32)
    return total


EARLY = ((1, 2), (3, 4), (5, 6), (6, 5))
LATE = ((2, 1), (4, 3), (7, 8), (8, 7))


def neighbours(value, moves, slices):
    peers = lax.axis_size("dp")
    pairs = [(base + i, base + j) for base in range(0, peers, slices) for i, j in moves]
    return lax.ppermute(value, "dp", [p for p in pairs if max(p) < peers])


def attend_kernel(spans, parents, lengths, query, own, twin, newest, *refs):
    pieces, out = refs[:-1], refs[-1]
    beams = range(query.shape[0])
    rank = lax.axis_index("dp")
    place = rank % 8
    arrives_early = (place == 2) | (place == 4) | (place == 5) | (place == 6)
    latest = newest[...].astype(jnp.float32)
    at = lax.broadcasted_iota(jnp.int32, own.shape[1:], 0)
    rows, scores, probs = [], [], []
    for b in beams:
        slot, holder = parents[b] % len(beams), parents[b] // len(beams)
        value = own[slot]
        value = jnp.where(holder == (rank ^ 1), twin[slot], value)
        far = (holder != rank) & (holder != (rank ^ 1))
        for (kind, low, high), piece in zip(spans, pieces):
            here = far & (slot >= low) & (slot < high)
            if kind == "early":
                here = here & arrives_early
            if kind == "late":
                here = here & jnp.logical_not(arrives_early)
            value = jnp.where(here, piece[jnp.clip(slot - low, 0, high - low - 1)], value)
        value = jnp.where(at < lengths[b] - 1, value, jnp.zeros_like(value))
        row = jnp.broadcast_to(latest[b : b + 1], value.shape).astype(value.dtype)
        rows.append(jnp.where(at == lengths[b] - 1, row, value))
    for b in beams:
        product = lax.dot_general(
            query[b], rows[b], (((1,), (1,)), ((), ())), preferred_element_type=jnp.float32
        )
        scores.append(product * score_scale)
    at = lax.broadcasted_iota(jnp.int32, scores[0].shape, 1)
    for b in beams:
        value = jnp.where(at < lengths[b], scores[b], -jnp.inf)
        expons = jnp.exp(value - jnp.max(value, axis=1, keepdims=True))
        total = jnp.sum(expons, axis=1, keepdims=True)
        probs.append((expons / total).astype(jnp.bfloat16))
    for b in beams:
        mixed = jnp.dot(probs[b], rows[b][:, :KV], preferred_element_type=jnp.float32)
        out[b] = mixed.astype(out.dtype)


def attend(queries, own, twin, newest, spans, pieces, parents, lengths):
    beam_count, heads, width = queries.shape
    positions = own.shape[1]
    scalars = pl.BlockSpec(memory_space=pltpu.SMEM)
    whole = pl.BlockSpec(memory_space=pltpu.VMEM)
    arrays = [
        pltpu.with_memory_space_constraint(v, pltpu.VMEM)
        for v in (queries, own, twin, newest, *pieces)
    ]
    return pl.pallas_call(
        lambda *refs: attend_kernel(spans, *refs),
        in_specs=[scalars] * 2 + [whole] * len(arrays),
        out_specs=whole,
        out_shape=jax.ShapeDtypeStruct((beam_count, heads, KV), jnp.bfloat16),
        compiler_params=pltpu.CompilerParams(vmem_limit_bytes=16 * 2**20),
        cost_estimate=pl.CostEstimate(
            flops=2 * beam_count * heads * positions * (width + KV),
            bytes_accessed=2 * beam_count * (4 * positions * width + heads * (width + KV)),
            transcendentals=beam_count * heads * positions,
        ),
    )(parents, lengths, *arrays)


def fetch_kernel(*refs):
    count = len(refs) // 2
    sources, targets, sems = refs[:count], refs[count:-1], refs[-1]
    copies = [
        pltpu.make_async_copy(source, target, sems.at[i])
        for i, (source, target) in enumerate(zip(sources, targets))
    ]
    for copy in copies:
        copy.start()
    for copy in copies:
        copy.wait()


def fetched(weights):
    return pl.pallas_call(
        fetch_kernel,
        in_specs=[pl.BlockSpec(memory_space=pltpu.HBM)] * len(weights),
        out_specs=[pl.BlockSpec(memory_space=pltpu.VMEM)] * len(weights),
        out_shape=[pltpu.VMEM(w.shape, w.dtype) for w in weights],
        scratch_shapes=[pltpu.SemaphoreType.DMA((len(weights),))],
        compiler_params=pltpu.CompilerParams(vmem_limit_bytes=16 * 2**20),
        cost_estimate=pl.CostEstimate(
            flops=0,
            bytes_accessed=2 * sum(w.size * w.dtype.itemsize for w in weights),
            transcendentals=0,
        ),
    )(*[pltpu.with_memory_space_constraint(w, pltpu.HBM) for w in weights])


def expert_kernel(wide, *refs):
    rows, refs = refs[:8], refs[8:]
    gate, up, down, own, high, low, gate_sum, up_sum = refs
    height, width = rows[0].shape
    half = 4 * height

    def span(k):
        return pl.ds(pl.multiple_of(k * wide, wide), wide)

    gate_sum[...] = jnp.zeros_like(gate_sum)
    up_sum[...] = jnp.zeros_like(up_sum)

    @pl.loop(0, width // wide)
    def _(k):
        piece = jnp.concatenate([ref[:, span(k)] for ref in rows], axis=0)
        gate_sum[...] += jnp.dot(piece, gate[0, span(k), :], preferred_element_type=jnp.float32)
        up_sum[...] += jnp.dot(piece, up[0, span(k), :], preferred_element_type=jnp.float32)

    total = gate_sum[...]
    hidden = (total / (1.0 + jnp.exp(-total)) * up_sum[...]).astype(jnp.bfloat16)

    @pl.loop(0, width // wide)
    def _(k):
        product = jnp.dot(hidden, down[0, :, span(k)], preferred_element_type=jnp.float32)
        product = product.astype(jnp.bfloat16)
        own[:, span(k)] = product[:half]
        low[:, span(k)] = product[half : half + 2 * height]
        high[:, span(k)] = product[half + 2 * height :]


def experts(rows, weights):
    height, width = rows[0].shape
    units = weights[0].shape[2]
    wide = max(w for w in (128, 256, 512, 1024) if width % w == 0)
    total = len(rows) * height
    whole = pl.BlockSpec(memory_space=pltpu.VMEM)
    inputs = [pltpu.with_memory_space_constraint(v, pltpu.VMEM) for v in (*rows, *weights)]
    return pl.pallas_call(
        lambda *refs: expert_kernel(wide, *refs),
        in_specs=[whole] * len(inputs),
        out_specs=[whole] * 3,
        out_shape=[pltpu.VMEM((count * height, width), jnp.bfloat16) for count in (4, 2, 2)],
        scratch_shapes=[
            pltpu.VMEM((total, units), jnp.float32),
            pltpu.VMEM((total, units), jnp.float32),
        ],
        compiler_params=pltpu.CompilerParams(vmem_limit_bytes=28 * 2**20),
        cost_estimate=pl.CostEstimate(
            flops=6 * total * width * units,
            bytes_accessed=6 * width * units + 4 * total * width,
            transcendentals=total * units,
        ),
    )(*inputs)


def body(
    queries,
    latent_cache,
    new_latent,
    parents,
    lengths,
    expert_input,
    routed_experts,
    route_weights,
    gate_weight,
    up_weight,
    down_weight,
):
    beam_count, width = expert_input.shape
    devices = lax.axis_size("dp")
    slices = FF_E // gate_weight.shape[2]
    expert_count = devices // slices
    route_count = routed_experts.shape[1]
    capacity = min(beam_count, max(2, 2 * beam_count * route_count // expert_count))
    dense = capacity == beam_count
    assert slices == 8 and expert_count & (expert_count - 1) == 0

    mine = lax.axis_index("dp") // slices
    turns = jnp.arange(expert_count, dtype=jnp.int32)
    targets = mine ^ turns
    if dense:
        blocks = [expert_input] * expert_count
        mixing = [
            jnp.sum(jnp.where(routed_experts == targets[r], route_weights, 0.0), axis=1)
            for r in range(expert_count)
        ]
    else:
        slots = pair_slots(routed_experts, expert_count, capacity)
        wanted = targets[:, None] * capacity + jnp.arange(capacity, dtype=jnp.int32)
        matches = (slots[:, :, None] == wanted.reshape(-1)).astype(jnp.float32)
        mixing = jnp.sum(route_weights[:, :, None] * matches, axis=1)
        selector = jnp.sum(matches, axis=1).T.astype(jnp.bfloat16)
        chosen = jnp.dot(selector, expert_input, preferred_element_type=jnp.float32)
        blocks = list(chosen.astype(jnp.bfloat16).reshape(expert_count, capacity, width))

    def ahead(r):
        return lambda i: i ^ (r * slices)

    def twin(i):
        return i ^ 1

    def first(i):
        return i ^ (2 if i & 1 else 4)

    def second(i):
        return i ^ (4 if i & 1 else 2)

    spans, pieces = [], []

    def cache_rows(kind, begin, end, ready=None):
        moves = {"early": EARLY, "late": LATE}[kind]
        source = latent_cache[begin:end]
        if ready is not None:
            source, ready = tied(source, ready)
        spans.append((kind, begin, end))
        return neighbours(source, moves, slices), ready

    column = blocks[:1] + [swapped(blocks[r], ahead(r)) for r in range(1, expert_count)]
    early, _ = cache_rows("early", 0, beam_count)
    column, early, mixing = tied(column, early, mixing)
    pieces.append(early)
    column = jnp.concatenate(column)
    near = swapped(column, first)
    again, near = tied(column, near)
    across = swapped(near, second)
    side = swapped(again, second)
    beside = swapped(latent_cache, twin)
    twin_column, twin_near = swapped(column, twin), swapped(near, twin)
    weights = fetched([gate_weight, up_weight, down_weight])
    across, twin_column, twin_near, weights, beside = tied(
        across, twin_column, twin_near, weights, beside
    )
    late, across = cache_rows("late", 0, beam_count, across)
    held = [column, near, side, across, twin_column, twin_near]
    held = held + [swapped(side, twin), swapped(across, twin)]
    own, high, low = experts(held, weights)
    high, late = tied(high, late)
    pieces.append(late)

    high, low = swapped(high, twin), swapped(low, twin)
    height = expert_count * capacity

    cut = 128 * (5 * width // 1024)
    halves = [(0, cut), (cut, width)]

    def block(value, j, half):
        return value[j * height : (j + 1) * height, half[0] : half[1]]

    def to_second(half):
        return added([block(own, 3, half), block(high, 1, half)]).astype(jnp.bfloat16)

    def to_first(half, across):
        return added([block(own, 1, half), block(low, 1, half), across]).astype(jnp.bfloat16)

    def to_side(half):
        return added([block(own, 2, half), block(high, 0, half)]).astype(jnp.bfloat16)

    def shares(half, side, near):
        here = [block(own, 0, half), block(low, 0, half), side, near]
        return [
            added([v[r * capacity : (r + 1) * capacity] for v in here])
            for r in range(expert_count)
        ]

    def back(share):
        return [
            swapped(share[r].astype(jnp.bfloat16), ahead(r)) for r in range(1, expert_count)
        ]

    across, high = tied(to_second(halves[0]), high)
    across = swapped(across, second)
    near, side = to_first(halves[0], across), to_side(halves[0])
    near, across = tied(near, to_second(halves[1]))
    near, side, across = swapped(near, first), swapped(side, second), swapped(across, second)
    share = shares(halves[0], side, near)
    share, across, high = tied(share, across, high)
    values = [[share[0]] + back(share)]
    near, side = to_first(halves[1], across), to_side(halves[1])
    attention = attend(
        queries, latent_cache, beside, new_latent, spans, pieces, parents, lengths
    )
    near, attention = tied(near, attention)
    near, side = swapped(near, first), swapped(side, second)
    share = shares(halves[1], side, near)
    values.append([share[0]] + back(share))
    totals = []
    for value in values:
        value = [v.astype(jnp.float32) for v in value]
        if dense:
            total = sum(mixing[r][:, None] * value[r] for r in range(expert_count))
        else:
            total = jnp.dot(
                mixing,
                jnp.concatenate(value),
                precision=lax.Precision.HIGHEST,
                preferred_element_type=jnp.float32,
            )
        totals.append(total.astype(jnp.bfloat16))
    expert_output = jnp.concatenate(totals, axis=1)
    return (attention, expert_output)


def solution(mesh):
    in_specs = (
        P(("groups", "dp"), None, None),
        P(("groups", "dp"), None, None),
        P(("groups", "dp"), None),
        P(("groups", "dp")),
        P(("groups", "dp")),
        P(("groups", "dp"), None),
        P(("groups", "dp"), None),
        P(("groups", "dp"), None),
        P("dp", None, None),
        P("dp", None, None),
        P("dp", None, None),
    )
    out_specs = (P(("groups", "dp"), None, None), P(("groups", "dp"), None))
    return jax.shard_map(body, mesh=mesh, in_specs=in_specs, out_specs=out_specs, check_vma=False)
```

```python
import jax
import jax.numpy as jnp
from jax import lax
from jax.experimental import pallas as pl
from jax.experimental.pallas import tpu as pltpu
from jax.sharding import PartitionSpec as P

FF_E = 2048
KV = 512


score_scale = 192.0 ** (-0.5)


def pair_slots(route_rows, expert_count, capacity):
    flat_experts = route_rows.reshape(-1)
    onehot = (flat_experts[:, None] == jnp.arange(expert_count, dtype=jnp.int32)[None, :]).astype(
        jnp.int32
    )
    position = jnp.sum((jnp.cumsum(onehot, axis=0) - onehot) * onehot, axis=1)
    return (flat_experts * capacity + position).astype(jnp.int32).reshape(route_rows.shape)


def swapped(value, partner):
    peers = lax.axis_size("dp")
    return lax.ppermute(value, "dp", [(i, partner(i)) for i in range(peers)])


def tied(*values):
    return lax.optimization_barrier(values)


def added(values):
    total = values[0].astype(jnp.float32)
    for value in values[1:]:
        total = total + value.astype(jnp.float32)
    return total


EARLY = ((1, 2), (3, 4), (5, 6), (6, 5))
LATE = ((2, 1), (4, 3), (7, 8), (8, 7))


def neighbours(value, moves, slices):
    peers = lax.axis_size("dp")
    pairs = [(base + i, base + j) for base in range(0, peers, slices) for i, j in moves]
    return lax.ppermute(value, "dp", [p for p in pairs if max(p) < peers])


def attend_kernel(spans, parents, lengths, query, own, twin, newest, *refs):
    pieces, out = refs[:-1], refs[-1]
    beams = range(query.shape[0])
    rank = lax.axis_index("dp")
    place = rank % 8
    arrives_early = (place == 2) | (place == 4) | (place == 5) | (place == 6)
    latest = newest[...].astype(jnp.float32)
    at = lax.broadcasted_iota(jnp.int32, own.shape[1:], 0)
    rows, scores, probs = [], [], []
    for b in beams:
        slot, holder = parents[b] % len(beams), parents[b] // len(beams)
        value = own[slot]
        value = jnp.where(holder == (rank ^ 1), twin[slot], value)
        far = (holder != rank) & (holder != (rank ^ 1))
        for (kind, low, high), piece in zip(spans, pieces):
            here = far & (slot >= low) & (slot < high)
            if kind == "early":
                here = here & arrives_early
            if kind == "late":
                here = here & jnp.logical_not(arrives_early)
            value = jnp.where(here, piece[jnp.clip(slot - low, 0, high - low - 1)], value)
        value = jnp.where(at < lengths[b] - 1, value, jnp.zeros_like(value))
        row = jnp.broadcast_to(latest[b : b + 1], value.shape).astype(value.dtype)
        rows.append(jnp.where(at == lengths[b] - 1, row, value))
    for b in beams:
        product = lax.dot_general(
            query[b], rows[b], (((1,), (1,)), ((), ())), preferred_element_type=jnp.float32
        )
        scores.append(product * score_scale)
    at = lax.broadcasted_iota(jnp.int32, scores[0].shape, 1)
    for b in beams:
        value = jnp.where(at < lengths[b], scores[b], -jnp.inf)
        expons = jnp.exp(value - jnp.max(value, axis=1, keepdims=True))
        total = jnp.sum(expons, axis=1, keepdims=True)
        probs.append((expons / total).astype(jnp.bfloat16))
    for b in beams:
        mixed = jnp.dot(probs[b], rows[b][:, :KV], preferred_element_type=jnp.float32)
        out[b] = mixed.astype(out.dtype)


def attend(queries, own, twin, newest, spans, pieces, parents, lengths):
    beam_count, heads, width = queries.shape
    positions = own.shape[1]
    scalars = pl.BlockSpec(memory_space=pltpu.SMEM)
    whole = pl.BlockSpec(memory_space=pltpu.VMEM)
    arrays = [
        pltpu.with_memory_space_constraint(v, pltpu.VMEM)
        for v in (queries, own, twin, newest, *pieces)
    ]
    return pl.pallas_call(
        lambda *refs: attend_kernel(spans, *refs),
        in_specs=[scalars] * 2 + [whole] * len(arrays),
        out_specs=whole,
        out_shape=jax.ShapeDtypeStruct((beam_count, heads, KV), jnp.bfloat16),
        compiler_params=pltpu.CompilerParams(vmem_limit_bytes=16 * 2**20),
        cost_estimate=pl.CostEstimate(
            flops=2 * beam_count * heads * positions * (width + KV),
            bytes_accessed=2 * beam_count * (4 * positions * width + heads * (width + KV)),
            transcendentals=beam_count * heads * positions,
        ),
    )(parents, lengths, *arrays)


def fetch_kernel(*refs):
    count = len(refs) // 2
    sources, targets, sems = refs[:count], refs[count:-1], refs[-1]
    copies = [
        pltpu.make_async_copy(source, target, sems.at[i])
        for i, (source, target) in enumerate(zip(sources, targets))
    ]
    for copy in copies:
        copy.start()
    for copy in copies:
        copy.wait()


def fetched(weights):
    return pl.pallas_call(
        fetch_kernel,
        in_specs=[pl.BlockSpec(memory_space=pltpu.HBM)] * len(weights),
        out_specs=[pl.BlockSpec(memory_space=pltpu.VMEM)] * len(weights),
        out_shape=[pltpu.VMEM(w.shape, w.dtype) for w in weights],
        scratch_shapes=[pltpu.SemaphoreType.DMA((len(weights),))],
        compiler_params=pltpu.CompilerParams(vmem_limit_bytes=16 * 2**20),
        cost_estimate=pl.CostEstimate(
            flops=0,
            bytes_accessed=2 * sum(w.size * w.dtype.itemsize for w in weights),
            transcendentals=0,
        ),
    )(*[pltpu.with_memory_space_constraint(w, pltpu.HBM) for w in weights])


def expert_kernel(wide, *refs):
    rows, refs = refs[:8], refs[8:]
    gate, up, down, own, low, far_side, far_across, gate_sum, up_sum = refs
    height, width = rows[0].shape
    half = 4 * height

    def span(k):
        return pl.ds(pl.multiple_of(k * wide, wide), wide)

    gate_sum[...] = jnp.zeros_like(gate_sum)
    up_sum[...] = jnp.zeros_like(up_sum)

    @pl.loop(0, width // wide)
    def _(k):
        piece = jnp.concatenate([ref[:, span(k)] for ref in rows], axis=0)
        gate_sum[...] += jnp.dot(piece, gate[0, span(k), :], preferred_element_type=jnp.float32)
        up_sum[...] += jnp.dot(piece, up[0, span(k), :], preferred_element_type=jnp.float32)

    total = gate_sum[...]
    hidden = (total / (1.0 + jnp.exp(-total)) * up_sum[...]).astype(jnp.bfloat16)

    @pl.loop(0, width // wide)
    def _(k):
        product = jnp.dot(hidden, down[0, :, span(k)], preferred_element_type=jnp.float32)
        product = product.astype(jnp.bfloat16)
        own[:, span(k)] = product[:half]
        low[:, span(k)] = product[half : half + 2 * height]
        far_side[:, span(k)] = product[half + 2 * height : half + 3 * height]
        far_across[:, span(k)] = product[half + 3 * height :]


def experts(rows, weights):
    height, width = rows[0].shape
    units = weights[0].shape[2]
    wide = max(w for w in (128, 256, 512, 1024) if width % w == 0)
    total = len(rows) * height
    whole = pl.BlockSpec(memory_space=pltpu.VMEM)
    inputs = [pltpu.with_memory_space_constraint(v, pltpu.VMEM) for v in (*rows, *weights)]
    return pl.pallas_call(
        lambda *refs: expert_kernel(wide, *refs),
        in_specs=[whole] * len(inputs),
        out_specs=[whole] * 4,
        out_shape=[pltpu.VMEM((count * height, width), jnp.bfloat16) for count in (4, 2, 1, 1)],
        scratch_shapes=[
            pltpu.VMEM((total, units), jnp.float32),
            pltpu.VMEM((total, units), jnp.float32),
        ],
        compiler_params=pltpu.CompilerParams(vmem_limit_bytes=28 * 2**20),
        cost_estimate=pl.CostEstimate(
            flops=6 * total * width * units,
            bytes_accessed=6 * width * units + 4 * total * width,
            transcendentals=total * units,
        ),
    )(*inputs)


def body(
    queries,
    latent_cache,
    new_latent,
    parents,
    lengths,
    expert_input,
    routed_experts,
    route_weights,
    gate_weight,
    up_weight,
    down_weight,
):
    beam_count, width = expert_input.shape
    devices = lax.axis_size("dp")
    slices = FF_E // gate_weight.shape[2]
    expert_count = devices // slices
    route_count = routed_experts.shape[1]
    capacity = min(beam_count, max(2, 2 * beam_count * route_count // expert_count))
    dense = capacity == beam_count
    assert slices == 8 and expert_count & (expert_count - 1) == 0

    mine = lax.axis_index("dp") // slices
    turns = jnp.arange(expert_count, dtype=jnp.int32)
    targets = mine ^ turns
    if dense:
        blocks = [expert_input] * expert_count
        mixing = [
            jnp.sum(jnp.where(routed_experts == targets[r], route_weights, 0.0), axis=1)
            for r in range(expert_count)
        ]
    else:
        slots = pair_slots(routed_experts, expert_count, capacity)
        wanted = targets[:, None] * capacity + jnp.arange(capacity, dtype=jnp.int32)
        matches = (slots[:, :, None] == wanted.reshape(-1)).astype(jnp.float32)
        mixing = jnp.sum(route_weights[:, :, None] * matches, axis=1)
        selector = jnp.sum(matches, axis=1).T.astype(jnp.bfloat16)
        chosen = jnp.dot(selector, expert_input, preferred_element_type=jnp.float32)
        blocks = list(chosen.astype(jnp.bfloat16).reshape(expert_count, capacity, width))

    def ahead(r):
        return lambda i: i ^ (r * slices)

    def twin(i):
        return i ^ 1

    def first(i):
        return i ^ (2 if i & 1 else 4)

    def second(i):
        return i ^ (4 if i & 1 else 2)

    spans, pieces = [], []

    def cache_rows(kind, begin, end, ready=None):
        moves = {"early": EARLY, "late": LATE}[kind]
        source = latent_cache[begin:end]
        if ready is not None:
            source, ready = tied(source, ready)
        spans.append((kind, begin, end))
        return neighbours(source, moves, slices), ready

    column = blocks[:1] + [swapped(blocks[r], ahead(r)) for r in range(1, expert_count)]
    early, _ = cache_rows("early", 0, beam_count)
    height = expert_count * capacity
    rows = jnp.pad(column[0], ((0, height - capacity), (0, 0)))
    rows, column, early, mixing = tied(rows, column, early, mixing)
    pieces.append(early)
    for r in range(1, expert_count):
        rows = lax.dynamic_update_slice(rows, column[r], (r * capacity, 0))
    column = rows
    near = swapped(column, first)
    again, near = tied(column, near)
    across = swapped(near, second)
    side = swapped(again, second)
    beside = swapped(latent_cache, twin)
    twin_column, twin_near = swapped(column, twin), swapped(near, twin)
    weights = fetched([gate_weight, up_weight, down_weight])
    across, twin_column, twin_near, weights, beside = tied(
        across, twin_column, twin_near, weights, beside
    )
    late, across = cache_rows("late", 0, beam_count, across)
    held = [column, near, side, across, twin_column, twin_near]
    held = held + [swapped(side, twin), swapped(across, twin)]
    own, low, far_side, far_across = experts(held, weights)
    far_across, late = tied(far_across, late)
    pieces.append(late)

    far_across, far_side = swapped(far_across, twin), swapped(far_side, twin)
    low = swapped(low, twin)
    height = expert_count * capacity

    cut = 128 * (5 * width // 1024)
    halves = [(0, cut), (cut, width)]

    def block(value, j, half):
        return value[j * height : (j + 1) * height, half[0] : half[1]]

    def to_second(half):
        return added([block(own, 3, half), block(far_across, 0, half)]).astype(jnp.bfloat16)

    def to_first(half, across):
        return added([block(own, 1, half), block(low, 1, half), across]).astype(jnp.bfloat16)

    def to_side(half):
        return added([block(own, 2, half), block(far_side, 0, half)]).astype(jnp.bfloat16)

    def shares(half, side, near):
        here = [block(own, 0, half), block(low, 0, half), side, near]
        return [
            added([v[r * capacity : (r + 1) * capacity] for v in here])
            for r in range(expert_count)
        ]

    def back(share):
        return [
            swapped(share[r].astype(jnp.bfloat16), ahead(r)) for r in range(1, expert_count)
        ]

    across, pieces[1] = tied(to_second(halves[0]), pieces[1])
    across = swapped(across, second)
    attention = attend(
        queries, latent_cache, beside, new_latent, spans, pieces, parents, lengths
    )
    across, attention = tied(across, attention)
    near, side = to_first(halves[0], across), to_side(halves[0])
    near, across = tied(near, to_second(halves[1]))
    near, side, across = swapped(near, first), swapped(side, second), swapped(across, second)
    share = shares(halves[0], side, near)
    share, across, far_side = tied(share, across, far_side)
    values = [[share[0]] + back(share)]
    near, side = to_first(halves[1], across), to_side(halves[1])
    near, side = swapped(near, first), swapped(side, second)
    share = shares(halves[1], side, near)
    values.append([share[0]] + back(share))
    totals = []
    for value in values:
        value = [v.astype(jnp.float32) for v in value]
        if dense:
            total = sum(mixing[r][:, None] * value[r] for r in range(expert_count))
        else:
            total = jnp.dot(
                mixing,
                jnp.concatenate(value),
                precision=lax.Precision.HIGHEST,
                preferred_element_type=jnp.float32,
            )
        totals.append(total.astype(jnp.bfloat16))
    expert_output = jnp.concatenate(totals, axis=1)
    return (attention, expert_output)


def solution(mesh):
    in_specs = (
        P(("groups", "dp"), None, None),
        P(("groups", "dp"), None, None),
        P(("groups", "dp"), None),
        P(("groups", "dp")),
        P(("groups", "dp")),
        P(("groups", "dp"), None),
        P(("groups", "dp"), None),
        P(("groups", "dp"), None),
        P("dp", None, None),
        P("dp", None, None),
        P("dp", None, None),
    )
    out_specs = (P(("groups", "dp"), None, None), P(("groups", "dp"), None))
    return jax.shard_map(body, mesh=mesh, in_specs=in_specs, out_specs=out_specs, check_vma=False)
```

```python
import jax
import jax.numpy as jnp
from jax import lax
from jax.experimental import pallas as pl
from jax.experimental.pallas import tpu as pltpu
from jax.sharding import PartitionSpec as P

FF_E = 2048
KV = 512


score_scale = 192.0 ** (-0.5)


def pair_slots(route_rows, expert_count, capacity):
    flat_experts = route_rows.reshape(-1)
    onehot = (flat_experts[:, None] == jnp.arange(expert_count, dtype=jnp.int32)[None, :]).astype(
        jnp.int32
    )
    position = jnp.sum((jnp.cumsum(onehot, axis=0) - onehot) * onehot, axis=1)
    return (flat_experts * capacity + position).astype(jnp.int32).reshape(route_rows.shape)


def swapped(value, partner):
    peers = lax.axis_size("dp")
    return lax.ppermute(value, "dp", [(i, partner(i)) for i in range(peers)])


def tied(*values):
    return lax.optimization_barrier(values)


def added(values):
    total = values[0].astype(jnp.float32)
    for value in values[1:]:
        total = total + value.astype(jnp.float32)
    return total


EARLY = ((1, 2), (3, 4), (5, 6), (6, 5))
LATE = ((2, 1), (4, 3), (7, 8), (8, 7))


def neighbours(value, moves, slices):
    peers = lax.axis_size("dp")
    pairs = [(base + i, base + j) for base in range(0, peers, slices) for i, j in moves]
    return lax.ppermute(value, "dp", [p for p in pairs if max(p) < peers])


def attend_kernel(spans, parents, lengths, query, own, twin, newest, *refs):
    pieces, out = refs[:-1], refs[-1]
    beams = range(query.shape[0])
    rank = lax.axis_index("dp")
    place = rank % 8
    arrives_early = (place == 2) | (place == 4) | (place == 5) | (place == 6)
    latest = newest[...].astype(jnp.float32)
    at = lax.broadcasted_iota(jnp.int32, own.shape[1:], 0)
    rows, scores, probs = [], [], []
    for b in beams:
        slot, holder = parents[b] % len(beams), parents[b] // len(beams)
        value = own[slot]
        value = jnp.where(holder == (rank ^ 1), twin[slot], value)
        far = (holder != rank) & (holder != (rank ^ 1))
        for (kind, low, high), piece in zip(spans, pieces):
            here = far & (slot >= low) & (slot < high)
            if kind == "early":
                here = here & arrives_early
            if kind == "late":
                here = here & jnp.logical_not(arrives_early)
            value = jnp.where(here, piece[jnp.clip(slot - low, 0, high - low - 1)], value)
        value = jnp.where(at < lengths[b] - 1, value, jnp.zeros_like(value))
        row = jnp.broadcast_to(latest[b : b + 1], value.shape).astype(value.dtype)
        rows.append(jnp.where(at == lengths[b] - 1, row, value))
    for b in beams:
        product = lax.dot_general(
            query[b], rows[b], (((1,), (1,)), ((), ())), preferred_element_type=jnp.float32
        )
        scores.append(product * score_scale)
    at = lax.broadcasted_iota(jnp.int32, scores[0].shape, 1)
    for b in beams:
        value = jnp.where(at < lengths[b], scores[b], -jnp.inf)
        expons = jnp.exp(value - jnp.max(value, axis=1, keepdims=True))
        total = jnp.sum(expons, axis=1, keepdims=True)
        probs.append((expons / total).astype(jnp.bfloat16))
    for b in beams:
        mixed = jnp.dot(probs[b], rows[b][:, :KV], preferred_element_type=jnp.float32)
        out[b] = mixed.astype(out.dtype)


def attend(queries, own, twin, newest, spans, pieces, parents, lengths):
    beam_count, heads, width = queries.shape
    positions = own.shape[1]
    scalars = pl.BlockSpec(memory_space=pltpu.SMEM)
    whole = pl.BlockSpec(memory_space=pltpu.VMEM)
    arrays = [
        pltpu.with_memory_space_constraint(v, pltpu.VMEM)
        for v in (queries, own, twin, newest, *pieces)
    ]
    return pl.pallas_call(
        lambda *refs: attend_kernel(spans, *refs),
        in_specs=[scalars] * 2 + [whole] * len(arrays),
        out_specs=whole,
        out_shape=jax.ShapeDtypeStruct((beam_count, heads, KV), jnp.bfloat16),
        compiler_params=pltpu.CompilerParams(vmem_limit_bytes=16 * 2**20),
        cost_estimate=pl.CostEstimate(
            flops=2 * beam_count * heads * positions * (width + KV),
            bytes_accessed=2 * beam_count * (4 * positions * width + heads * (width + KV)),
            transcendentals=beam_count * heads * positions,
        ),
    )(parents, lengths, *arrays)


def fetch_kernel(*refs):
    count = len(refs) // 2
    sources, targets, sems = refs[:count], refs[count:-1], refs[-1]
    copies = [
        pltpu.make_async_copy(source, target, sems.at[i])
        for i, (source, target) in enumerate(zip(sources, targets))
    ]
    for copy in copies:
        copy.start()
    for copy in copies:
        copy.wait()


def fetched(weights):
    return pl.pallas_call(
        fetch_kernel,
        in_specs=[pl.BlockSpec(memory_space=pltpu.HBM)] * len(weights),
        out_specs=[pl.BlockSpec(memory_space=pltpu.VMEM)] * len(weights),
        out_shape=[pltpu.VMEM(w.shape, w.dtype) for w in weights],
        scratch_shapes=[pltpu.SemaphoreType.DMA((len(weights),))],
        compiler_params=pltpu.CompilerParams(vmem_limit_bytes=16 * 2**20),
        cost_estimate=pl.CostEstimate(
            flops=0,
            bytes_accessed=2 * sum(w.size * w.dtype.itemsize for w in weights),
            transcendentals=0,
        ),
    )(*[pltpu.with_memory_space_constraint(w, pltpu.HBM) for w in weights])


def expert_kernel(wide, *refs):
    rows, refs = refs[:8], refs[8:]
    gate, up, down, own, low, far_side, far_across, gate_sum, up_sum = refs
    height, width = rows[0].shape
    half = 4 * height

    def span(k):
        return pl.ds(pl.multiple_of(k * wide, wide), wide)

    gate_sum[...] = jnp.zeros_like(gate_sum)
    up_sum[...] = jnp.zeros_like(up_sum)

    @pl.loop(0, width // wide)
    def _(k):
        piece = jnp.concatenate([ref[:, span(k)] for ref in rows], axis=0)
        gate_sum[...] += jnp.dot(piece, gate[0, span(k), :], preferred_element_type=jnp.float32)
        up_sum[...] += jnp.dot(piece, up[0, span(k), :], preferred_element_type=jnp.float32)

    total = gate_sum[...]
    hidden = (total / (1.0 + jnp.exp(-total)) * up_sum[...]).astype(jnp.bfloat16)

    @pl.loop(0, width // wide)
    def _(k):
        product = jnp.dot(hidden, down[0, :, span(k)], preferred_element_type=jnp.float32)
        product = product.astype(jnp.bfloat16)
        own[:, span(k)] = product[:half]
        low[:, span(k)] = product[half : half + 2 * height]
        far_side[:, span(k)] = product[half + 2 * height : half + 3 * height]
        far_across[:, span(k)] = product[half + 3 * height :]


def experts(rows, weights):
    height, width = rows[0].shape
    units = weights[0].shape[2]
    wide = max(w for w in (128, 256, 512, 1024) if width % w == 0)
    total = len(rows) * height
    whole = pl.BlockSpec(memory_space=pltpu.VMEM)
    inputs = [pltpu.with_memory_space_constraint(v, pltpu.VMEM) for v in (*rows, *weights)]
    return pl.pallas_call(
        lambda *refs: expert_kernel(wide, *refs),
        in_specs=[whole] * len(inputs),
        out_specs=[whole] * 4,
        out_shape=[pltpu.VMEM((count * height, width), jnp.bfloat16) for count in (4, 2, 1, 1)],
        scratch_shapes=[
            pltpu.VMEM((total, units), jnp.float32),
            pltpu.VMEM((total, units), jnp.float32),
        ],
        compiler_params=pltpu.CompilerParams(vmem_limit_bytes=28 * 2**20),
        cost_estimate=pl.CostEstimate(
            flops=6 * total * width * units,
            bytes_accessed=6 * width * units + 4 * total * width,
            transcendentals=total * units,
        ),
    )(*inputs)


def body(
    queries,
    latent_cache,
    new_latent,
    parents,
    lengths,
    expert_input,
    routed_experts,
    route_weights,
    gate_weight,
    up_weight,
    down_weight,
):
    beam_count, width = expert_input.shape
    devices = lax.axis_size("dp")
    slices = FF_E // gate_weight.shape[2]
    expert_count = devices // slices
    route_count = routed_experts.shape[1]
    capacity = min(beam_count, max(2, 2 * beam_count * route_count // expert_count))
    dense = capacity == beam_count
    assert slices == 8 and expert_count & (expert_count - 1) == 0

    mine = lax.axis_index("dp") // slices
    turns = jnp.arange(expert_count, dtype=jnp.int32)
    targets = mine ^ turns
    if dense:
        blocks = [expert_input] * expert_count
        mixing = [
            jnp.sum(jnp.where(routed_experts == targets[r], route_weights, 0.0), axis=1)
            for r in range(expert_count)
        ]
    else:
        slots = pair_slots(routed_experts, expert_count, capacity)
        wanted = targets[:, None] * capacity + jnp.arange(capacity, dtype=jnp.int32)
        matches = (slots[:, :, None] == wanted.reshape(-1)).astype(jnp.float32)
        mixing = jnp.sum(route_weights[:, :, None] * matches, axis=1)
        selector = jnp.sum(matches, axis=1).T.astype(jnp.bfloat16)
        chosen = jnp.dot(selector, expert_input, preferred_element_type=jnp.float32)
        blocks = list(chosen.astype(jnp.bfloat16).reshape(expert_count, capacity, width))

    def ahead(r):
        return lambda i: i ^ (r * slices)

    def twin(i):
        return i ^ 1

    def first(i):
        return i ^ (2 if i & 1 else 4)

    def second(i):
        return i ^ (4 if i & 1 else 2)

    spans, pieces = [], []

    def cache_rows(kind, begin, end, ready=None):
        moves = {"early": EARLY, "late": LATE}[kind]
        source = latent_cache[begin:end]
        if ready is not None:
            source, ready = tied(source, ready)
        spans.append((kind, begin, end))
        return neighbours(source, moves, slices), ready

    column = blocks[:1] + [swapped(blocks[r], ahead(r)) for r in range(1, expert_count)]
    early, _ = cache_rows("early", 0, beam_count)
    height = expert_count * capacity
    rows = jnp.pad(column[0], ((0, height - capacity), (0, 0)))
    rows, column, mixing = tied(rows, column, mixing)
    for r in range(1, expert_count):
        rows = lax.dynamic_update_slice(rows, column[r], (r * capacity, 0))
    column = rows
    near = swapped(column, first)
    again, near, early = tied(column, near, early)
    pieces.append(early)
    across = swapped(near, second)
    side = swapped(again, second)
    beside = swapped(latent_cache, twin)
    twin_column, twin_near = swapped(column, twin), swapped(near, twin)
    weights = fetched([gate_weight, up_weight, down_weight])
    across, twin_column, twin_near, weights, beside = tied(
        across, twin_column, twin_near, weights, beside
    )
    late, across = cache_rows("late", 0, beam_count, across)
    held = [column, near, side, across, twin_column, twin_near]
    held = held + [swapped(side, twin), swapped(across, twin)]
    own, low, far_side, far_across = experts(held, weights)
    far_across, late = tied(far_across, late)
    pieces.append(late)

    far_across, far_side = swapped(far_across, twin), swapped(far_side, twin)
    low = swapped(low, twin)
    height = expert_count * capacity

    cut = 128 * (5 * width // 1024)
    halves = [(0, cut), (cut, width)]

    def block(value, j, half):
        return value[j * height : (j + 1) * height, half[0] : half[1]]

    def to_second(half):
        return added([block(own, 3, half), block(far_across, 0, half)]).astype(jnp.bfloat16)

    def to_first(half, across):
        return added([block(own, 1, half), block(low, 1, half), across]).astype(jnp.bfloat16)

    def to_side(half):
        return added([block(own, 2, half), block(far_side, 0, half)]).astype(jnp.bfloat16)

    def shares(half, side, near):
        here = [block(own, 0, half), block(low, 0, half), side, near]
        return [
            added([v[r * capacity : (r + 1) * capacity] for v in here])
            for r in range(expert_count)
        ]

    def back(share):
        return [
            swapped(share[r].astype(jnp.bfloat16), ahead(r)) for r in range(1, expert_count)
        ]

    across, pieces[1] = tied(to_second(halves[0]), pieces[1])
    across = swapped(across, second)
    attention = attend(
        queries, latent_cache, beside, new_latent, spans, pieces, parents, lengths
    )
    across, attention = tied(across, attention)
    near, side = to_first(halves[0], across), to_side(halves[0])
    near, across = tied(near, to_second(halves[1]))
    near, side, across = swapped(near, first), swapped(side, second), swapped(across, second)
    share = shares(halves[0], side, near)
    share, across, far_side = tied(share, across, far_side)
    values = [[share[0]] + back(share)]
    near, side = to_first(halves[1], across), to_side(halves[1])
    near, side = swapped(near, first), swapped(side, second)
    share = shares(halves[1], side, near)
    values.append([share[0]] + back(share))

    def mixed(value):
        value = [v.astype(jnp.float32) for v in value]
        if dense:
            total = sum(mixing[r][:, None] * value[r] for r in range(expert_count))
        else:
            total = jnp.dot(
                mixing,
                jnp.concatenate(value),
                precision=lax.Precision.HIGHEST,
                preferred_element_type=jnp.float32,
            )
        return total.astype(jnp.bfloat16)

    expert_output = jnp.pad(mixed(values[0]), ((0, 0), (0, width - cut)))
    expert_output, values[1] = tied(expert_output, values[1])
    expert_output = lax.dynamic_update_slice(expert_output, mixed(values[1]), (0, cut))
    return (attention, expert_output)


def solution(mesh):
    in_specs = (
        P(("groups", "dp"), None, None),
        P(("groups", "dp"), None, None),
        P(("groups", "dp"), None),
        P(("groups", "dp")),
        P(("groups", "dp")),
        P(("groups", "dp"), None),
        P(("groups", "dp"), None),
        P(("groups", "dp"), None),
        P("dp", None, None),
        P("dp", None, None),
        P("dp", None, None),
    )
    out_specs = (P(("groups", "dp"), None, None), P(("groups", "dp"), None))
    return jax.shard_map(body, mesh=mesh, in_specs=in_specs, out_specs=out_specs, check_vma=False)
```

```python
import jax
import jax.numpy as jnp
from jax import lax
from jax.experimental import pallas as pl
from jax.experimental.pallas import tpu as pltpu
from jax.sharding import PartitionSpec as P

FF_E = 2048
KV = 512


score_scale = 192.0 ** (-0.5)


def pair_slots(route_rows, expert_count, capacity):
    flat_experts = route_rows.reshape(-1)
    onehot = (flat_experts[:, None] == jnp.arange(expert_count, dtype=jnp.int32)[None, :]).astype(
        jnp.int32
    )
    position = jnp.sum((jnp.cumsum(onehot, axis=0) - onehot) * onehot, axis=1)
    return (flat_experts * capacity + position).astype(jnp.int32).reshape(route_rows.shape)


def swapped(value, partner):
    peers = lax.axis_size("dp")
    return lax.ppermute(value, "dp", [(i, partner(i)) for i in range(peers)])


def tied(*values):
    return lax.optimization_barrier(values)


def added(values):
    total = values[0].astype(jnp.float32)
    for value in values[1:]:
        total = total + value.astype(jnp.float32)
    return total


EARLY = ((1, 2), (3, 4), (5, 6), (6, 5))
LATE = ((2, 1), (4, 3), (7, 8), (8, 7))


def neighbours(value, moves, slices):
    peers = lax.axis_size("dp")
    pairs = [(base + i, base + j) for base in range(0, peers, slices) for i, j in moves]
    return lax.ppermute(value, "dp", [p for p in pairs if max(p) < peers])


def attend_kernel(spans, parents, lengths, query, own, twin, newest, *refs):
    pieces, out = refs[:-1], refs[-1]
    beams = range(query.shape[0])
    rank = lax.axis_index("dp")
    place = rank % 8
    arrives_early = (place == 2) | (place == 4) | (place == 5) | (place == 6)
    latest = newest[...].astype(jnp.float32)
    at = lax.broadcasted_iota(jnp.int32, own.shape[1:], 0)
    rows, scores, probs = [], [], []
    for b in beams:
        slot, holder = parents[b] % len(beams), parents[b] // len(beams)
        value = own[slot]
        value = jnp.where(holder == (rank ^ 1), twin[slot], value)
        far = (holder != rank) & (holder != (rank ^ 1))
        for (kind, low, high), piece in zip(spans, pieces):
            here = far & (slot >= low) & (slot < high)
            if kind == "early":
                here = here & arrives_early
            if kind == "late":
                here = here & jnp.logical_not(arrives_early)
            value = jnp.where(here, piece[jnp.clip(slot - low, 0, high - low - 1)], value)
        value = jnp.where(at < lengths[b] - 1, value, jnp.zeros_like(value))
        row = jnp.broadcast_to(latest[b : b + 1], value.shape).astype(value.dtype)
        rows.append(jnp.where(at == lengths[b] - 1, row, value))
    for b in beams:
        product = lax.dot_general(
            query[b], rows[b], (((1,), (1,)), ((), ())), preferred_element_type=jnp.float32
        )
        scores.append(product * score_scale)
    at = lax.broadcasted_iota(jnp.int32, scores[0].shape, 1)
    for b in beams:
        value = jnp.where(at < lengths[b], scores[b], -jnp.inf)
        expons = jnp.exp(value - jnp.max(value, axis=1, keepdims=True))
        total = jnp.sum(expons, axis=1, keepdims=True)
        probs.append((expons / total).astype(jnp.bfloat16))
    for b in beams:
        mixed = jnp.dot(probs[b], rows[b][:, :KV], preferred_element_type=jnp.float32)
        out[b] = mixed.astype(out.dtype)


def attend(queries, own, twin, newest, spans, pieces, parents, lengths):
    beam_count, heads, width = queries.shape
    positions = own.shape[1]
    scalars = pl.BlockSpec(memory_space=pltpu.SMEM)
    whole = pl.BlockSpec(memory_space=pltpu.VMEM)
    arrays = [
        pltpu.with_memory_space_constraint(v, pltpu.VMEM)
        for v in (queries, own, twin, newest, *pieces)
    ]
    return pl.pallas_call(
        lambda *refs: attend_kernel(spans, *refs),
        in_specs=[scalars] * 2 + [whole] * len(arrays),
        out_specs=whole,
        out_shape=jax.ShapeDtypeStruct((beam_count, heads, KV), jnp.bfloat16),
        compiler_params=pltpu.CompilerParams(vmem_limit_bytes=16 * 2**20),
        cost_estimate=pl.CostEstimate(
            flops=2 * beam_count * heads * positions * (width + KV),
            bytes_accessed=2 * beam_count * (4 * positions * width + heads * (width + KV)),
            transcendentals=beam_count * heads * positions,
        ),
    )(parents, lengths, *arrays)


def fetch_kernel(*refs):
    count = len(refs) // 2
    sources, targets, sems = refs[:count], refs[count:-1], refs[-1]
    copies = [
        pltpu.make_async_copy(source, target, sems.at[i])
        for i, (source, target) in enumerate(zip(sources, targets))
    ]
    for copy in copies:
        copy.start()
    for copy in copies:
        copy.wait()


def fetched(weights):
    return pl.pallas_call(
        fetch_kernel,
        in_specs=[pl.BlockSpec(memory_space=pltpu.HBM)] * len(weights),
        out_specs=[pl.BlockSpec(memory_space=pltpu.VMEM)] * len(weights),
        out_shape=[pltpu.VMEM(w.shape, w.dtype) for w in weights],
        scratch_shapes=[pltpu.SemaphoreType.DMA((len(weights),))],
        compiler_params=pltpu.CompilerParams(vmem_limit_bytes=16 * 2**20),
        cost_estimate=pl.CostEstimate(
            flops=0,
            bytes_accessed=2 * sum(w.size * w.dtype.itemsize for w in weights),
            transcendentals=0,
        ),
    )(*[pltpu.with_memory_space_constraint(w, pltpu.HBM) for w in weights])


def expert_kernel(wide, *refs):
    rows, refs = refs[:8], refs[8:]
    gate, up, down, own, low, far_side, far_across, gate_sum, up_sum = refs
    height, width = rows[0].shape
    half = 4 * height

    def span(k):
        return pl.ds(pl.multiple_of(k * wide, wide), wide)

    gate_sum[...] = jnp.zeros_like(gate_sum)
    up_sum[...] = jnp.zeros_like(up_sum)

    @pl.loop(0, width // wide)
    def _(k):
        piece = jnp.concatenate([ref[:, span(k)] for ref in rows], axis=0)
        gate_sum[...] += jnp.dot(piece, gate[0, span(k), :], preferred_element_type=jnp.float32)
        up_sum[...] += jnp.dot(piece, up[0, span(k), :], preferred_element_type=jnp.float32)

    total = gate_sum[...]
    hidden = (total / (1.0 + jnp.exp(-total)) * up_sum[...]).astype(jnp.bfloat16)

    @pl.loop(0, width // wide)
    def _(k):
        product = jnp.dot(hidden, down[0, :, span(k)], preferred_element_type=jnp.float32)
        product = product.astype(jnp.bfloat16)
        own[:, span(k)] = product[:half]
        low[:, span(k)] = product[half : half + 2 * height]
        far_side[:, span(k)] = product[half + 2 * height : half + 3 * height]
        far_across[:, span(k)] = product[half + 3 * height :]


def experts(rows, weights):
    height, width = rows[0].shape
    units = weights[0].shape[2]
    wide = max(w for w in (128, 256, 512, 1024) if width % w == 0)
    total = len(rows) * height
    whole = pl.BlockSpec(memory_space=pltpu.VMEM)
    inputs = [pltpu.with_memory_space_constraint(v, pltpu.VMEM) for v in (*rows, *weights)]
    return pl.pallas_call(
        lambda *refs: expert_kernel(wide, *refs),
        in_specs=[whole] * len(inputs),
        out_specs=[whole] * 4,
        out_shape=[pltpu.VMEM((count * height, width), jnp.bfloat16) for count in (4, 2, 1, 1)],
        scratch_shapes=[
            pltpu.VMEM((total, units), jnp.float32),
            pltpu.VMEM((total, units), jnp.float32),
        ],
        compiler_params=pltpu.CompilerParams(vmem_limit_bytes=28 * 2**20),
        cost_estimate=pl.CostEstimate(
            flops=6 * total * width * units,
            bytes_accessed=6 * width * units + 4 * total * width,
            transcendentals=total * units,
        ),
    )(*inputs)


def body(
    queries,
    latent_cache,
    new_latent,
    parents,
    lengths,
    expert_input,
    routed_experts,
    route_weights,
    gate_weight,
    up_weight,
    down_weight,
):
    beam_count, width = expert_input.shape
    devices = lax.axis_size("dp")
    slices = FF_E // gate_weight.shape[2]
    expert_count = devices // slices
    route_count = routed_experts.shape[1]
    capacity = min(beam_count, max(2, 2 * beam_count * route_count // expert_count))
    dense = capacity == beam_count
    assert slices == 8 and expert_count & (expert_count - 1) == 0

    mine = lax.axis_index("dp") // slices
    turns = jnp.arange(expert_count, dtype=jnp.int32)
    targets = mine ^ turns
    if dense:
        blocks = [expert_input] * expert_count
        mixing = [
            jnp.sum(jnp.where(routed_experts == targets[r], route_weights, 0.0), axis=1)
            for r in range(expert_count)
        ]
    else:
        slots = pair_slots(routed_experts, expert_count, capacity)
        wanted = targets[:, None] * capacity + jnp.arange(capacity, dtype=jnp.int32)
        matches = (slots[:, :, None] == wanted.reshape(-1)).astype(jnp.float32)
        mixing = jnp.sum(route_weights[:, :, None] * matches, axis=1)
        selector = jnp.sum(matches, axis=1).T.astype(jnp.bfloat16)
        chosen = jnp.dot(selector, expert_input, preferred_element_type=jnp.float32)
        blocks = list(chosen.astype(jnp.bfloat16).reshape(expert_count, capacity, width))

    def ahead(r):
        return lambda i: i ^ (r * slices)

    def twin(i):
        return i ^ 1

    def first(i):
        return i ^ (2 if i & 1 else 4)

    def second(i):
        return i ^ (4 if i & 1 else 2)

    spans, pieces = [], []

    def cache_rows(kind, begin, end, ready=None):
        moves = {"early": EARLY, "late": LATE}[kind]
        source = latent_cache[begin:end]
        if ready is not None:
            source, ready = tied(source, ready)
        spans.append((kind, begin, end))
        return neighbours(source, moves, slices), ready

    column = blocks[:1] + [swapped(blocks[r], ahead(r)) for r in range(1, expert_count)]
    early, _ = cache_rows("early", 0, beam_count)
    height = expert_count * capacity
    rows = jnp.pad(column[0], ((0, height - capacity), (0, 0)))
    column = column[::-1]
    rows, column, early, mixing = tied(rows, column, early, mixing)
    column = column[::-1]
    pieces.append(early)
    for r in range(1, expert_count):
        rows = lax.dynamic_update_slice(rows, column[r], (r * capacity, 0))
    column = rows
    near = swapped(column, first)
    again, near = tied(column, near)
    across = swapped(near, second)
    side = swapped(again, second)
    beside = swapped(latent_cache, twin)
    twin_column, twin_near = swapped(column, twin), swapped(near, twin)
    weights = fetched([gate_weight, up_weight, down_weight])
    across, twin_column, twin_near, weights, beside = tied(
        across, twin_column, twin_near, weights, beside
    )
    late, across = cache_rows("late", 0, beam_count, across)
    held = [column, near, side, across, twin_column, twin_near]
    held = held + [swapped(side, twin), swapped(across, twin)]
    own, low, far_side, far_across = experts(held, weights)
    far_across, late = tied(far_across, late)
    pieces.append(late)

    far_across, far_side = swapped(far_across, twin), swapped(far_side, twin)
    low = swapped(low, twin)
    height = expert_count * capacity

    cut = 128 * (15 * width // 3584)
    halves = [(0, cut), (cut, width)]

    def block(value, j, half):
        return value[j * height : (j + 1) * height, half[0] : half[1]]

    def to_second(half):
        return added([block(own, 3, half), block(far_across, 0, half)]).astype(jnp.bfloat16)

    def to_first(half, across):
        return added([block(own, 1, half), block(low, 1, half), across]).astype(jnp.bfloat16)

    def to_side(half):
        return added([block(own, 2, half), block(far_side, 0, half)]).astype(jnp.bfloat16)

    def shares(half, side, near):
        here = [block(own, 0, half), block(low, 0, half), side, near]
        return [
            added([v[r * capacity : (r + 1) * capacity] for v in here])
            for r in range(expert_count)
        ]

    def back(share):
        sent = [
            swapped(share[r].astype(jnp.bfloat16), ahead(r))
            for r in reversed(range(1, expert_count))
        ]
        return sent[::-1]

    across, pieces[1] = tied(to_second(halves[0]), pieces[1])
    across = swapped(across, second)
    attention = attend(
        queries, latent_cache, beside, new_latent, spans, pieces, parents, lengths
    )
    across, attention = tied(across, attention)
    near, side = to_first(halves[0], across), to_side(halves[0])
    near, across = tied(near, to_second(halves[1]))
    near, side, across = swapped(near, first), swapped(side, second), swapped(across, second)
    share = shares(halves[0], side, near)
    share, across, far_side = tied(share, across, far_side)
    values = [[share[0]] + back(share)]
    near, side = to_first(halves[1], across), to_side(halves[1])
    near, side = swapped(near, first), swapped(side, second)
    share = shares(halves[1], side, near)
    values.append([share[0]] + back(share))
    totals = []
    for value in values:
        value = [v.astype(jnp.float32) for v in value]
        if dense:
            order = [0, *range(expert_count - 1, 0, -1)]
            total = sum(mixing[r][:, None] * value[r] for r in order)
        else:
            total = jnp.dot(
                mixing,
                jnp.concatenate(value),
                precision=lax.Precision.HIGHEST,
                preferred_element_type=jnp.float32,
            )
        totals.append(total.astype(jnp.bfloat16))
    expert_output = jnp.concatenate(totals, axis=1)
    return (attention, expert_output)


def solution(mesh):
    in_specs = (
        P(("groups", "dp"), None, None),
        P(("groups", "dp"), None, None),
        P(("groups", "dp"), None),
        P(("groups", "dp")),
        P(("groups", "dp")),
        P(("groups", "dp"), None),
        P(("groups", "dp"), None),
        P(("groups", "dp"), None),
        P("dp", None, None),
        P("dp", None, None),
        P("dp", None, None),
    )
    out_specs = (P(("groups", "dp"), None, None), P(("groups", "dp"), None))
    return jax.shard_map(body, mesh=mesh, in_specs=in_specs, out_specs=out_specs, check_vma=False)
```

```python
import jax
import jax.numpy as jnp
from jax import lax
from jax.experimental import pallas as pl
from jax.experimental.pallas import tpu as pltpu
from jax.sharding import PartitionSpec as P

FF_E = 2048
KV = 512


score_scale = 192.0 ** (-0.5)


def pair_slots(route_rows, expert_count, capacity):
    flat_experts = route_rows.reshape(-1)
    onehot = (flat_experts[:, None] == jnp.arange(expert_count, dtype=jnp.int32)[None, :]).astype(
        jnp.int32
    )
    position = jnp.sum((jnp.cumsum(onehot, axis=0) - onehot) * onehot, axis=1)
    return (flat_experts * capacity + position).astype(jnp.int32).reshape(route_rows.shape)


def swapped(value, partner):
    peers = lax.axis_size("dp")
    return lax.ppermute(value, "dp", [(i, partner(i)) for i in range(peers)])


def tied(*values):
    return lax.optimization_barrier(values)


def added(values):
    total = values[0].astype(jnp.float32)
    for value in values[1:]:
        total = total + value.astype(jnp.float32)
    return total


EARLY = ((1, 2), (3, 4), (5, 6), (6, 5))
LATE = ((2, 1), (4, 3), (7, 8), (8, 7))


def neighbours(value, moves, slices):
    peers = lax.axis_size("dp")
    pairs = [(base + i, base + j) for base in range(0, peers, slices) for i, j in moves]
    return lax.ppermute(value, "dp", [p for p in pairs if max(p) < peers])


def attend_kernel(spans, parents, lengths, query, own, twin, newest, *refs):
    pieces, out = refs[:-1], refs[-1]
    beams = range(query.shape[0])
    rank = lax.axis_index("dp")
    place = rank % 8
    arrives_early = (place == 2) | (place == 4) | (place == 5) | (place == 6)
    latest = newest[...].astype(jnp.float32)
    at = lax.broadcasted_iota(jnp.int32, own.shape[1:], 0)
    rows, scores, probs = [], [], []
    for b in beams:
        slot, holder = parents[b] % len(beams), parents[b] // len(beams)
        value = own[slot]
        value = jnp.where(holder == (rank ^ 1), twin[slot], value)
        far = (holder != rank) & (holder != (rank ^ 1))
        for (kind, low, high), piece in zip(spans, pieces):
            here = far & (slot >= low) & (slot < high)
            if kind == "early":
                here = here & arrives_early
            if kind == "late":
                here = here & jnp.logical_not(arrives_early)
            value = jnp.where(here, piece[jnp.clip(slot - low, 0, high - low - 1)], value)
        value = jnp.where(at < lengths[b] - 1, value, jnp.zeros_like(value))
        row = jnp.broadcast_to(latest[b : b + 1], value.shape).astype(value.dtype)
        rows.append(jnp.where(at == lengths[b] - 1, row, value))
    for b in beams:
        product = lax.dot_general(
            query[b], rows[b], (((1,), (1,)), ((), ())), preferred_element_type=jnp.float32
        )
        scores.append(product * score_scale)
    at = lax.broadcasted_iota(jnp.int32, scores[0].shape, 1)
    for b in beams:
        value = jnp.where(at < lengths[b], scores[b], -jnp.inf)
        expons = jnp.exp(value - jnp.max(value, axis=1, keepdims=True))
        total = jnp.sum(expons, axis=1, keepdims=True)
        probs.append((expons / total).astype(jnp.bfloat16))
    for b in beams:
        mixed = jnp.dot(probs[b], rows[b][:, :KV], preferred_element_type=jnp.float32)
        out[b] = mixed.astype(out.dtype)


def attend(queries, own, twin, newest, spans, pieces, parents, lengths):
    beam_count, heads, width = queries.shape
    positions = own.shape[1]
    scalars = pl.BlockSpec(memory_space=pltpu.SMEM)
    whole = pl.BlockSpec(memory_space=pltpu.VMEM)
    arrays = [
        pltpu.with_memory_space_constraint(v, pltpu.VMEM)
        for v in (queries, own, twin, newest, *pieces)
    ]
    return pl.pallas_call(
        lambda *refs: attend_kernel(spans, *refs),
        in_specs=[scalars] * 2 + [whole] * len(arrays),
        out_specs=whole,
        out_shape=jax.ShapeDtypeStruct((beam_count, heads, KV), jnp.bfloat16),
        compiler_params=pltpu.CompilerParams(vmem_limit_bytes=16 * 2**20),
        cost_estimate=pl.CostEstimate(
            flops=2 * beam_count * heads * positions * (width + KV),
            bytes_accessed=2 * beam_count * (4 * positions * width + heads * (width + KV)),
            transcendentals=beam_count * heads * positions,
        ),
    )(parents, lengths, *arrays)


def fetch_kernel(*refs):
    count = len(refs) // 2
    sources, targets, sems = refs[:count], refs[count:-1], refs[-1]
    copies = [
        pltpu.make_async_copy(source, target, sems.at[i])
        for i, (source, target) in enumerate(zip(sources, targets))
    ]
    for copy in copies:
        copy.start()
    for copy in copies:
        copy.wait()


def fetched(weights):
    return pl.pallas_call(
        fetch_kernel,
        in_specs=[pl.BlockSpec(memory_space=pltpu.HBM)] * len(weights),
        out_specs=[pl.BlockSpec(memory_space=pltpu.VMEM)] * len(weights),
        out_shape=[pltpu.VMEM(w.shape, w.dtype) for w in weights],
        scratch_shapes=[pltpu.SemaphoreType.DMA((len(weights),))],
        compiler_params=pltpu.CompilerParams(vmem_limit_bytes=16 * 2**20),
        cost_estimate=pl.CostEstimate(
            flops=0,
            bytes_accessed=2 * sum(w.size * w.dtype.itemsize for w in weights),
            transcendentals=0,
        ),
    )(*[pltpu.with_memory_space_constraint(w, pltpu.HBM) for w in weights])


def expert_kernel(wide, *refs):
    rows, refs = refs[:8], refs[8:]
    gate, up, down, own, low, far_side, *far_across, gate_sum, up_sum = refs
    height, width = rows[0].shape
    half = 4 * height

    def span(k):
        return pl.ds(pl.multiple_of(k * wide, wide), wide)

    gate_sum[...] = jnp.zeros_like(gate_sum)
    up_sum[...] = jnp.zeros_like(up_sum)

    @pl.loop(0, width // wide)
    def _(k):
        piece = jnp.concatenate([ref[:, span(k)] for ref in rows], axis=0)
        gate_sum[...] += jnp.dot(piece, gate[0, span(k), :], preferred_element_type=jnp.float32)
        up_sum[...] += jnp.dot(piece, up[0, span(k), :], preferred_element_type=jnp.float32)

    total = gate_sum[...]
    hidden = (total / (1.0 + jnp.exp(-total)) * up_sum[...]).astype(jnp.bfloat16)

    steps = far_across[0].shape[1] // wide

    def give(k, ref, first):
        product = jnp.dot(hidden, down[0, :, span(k)], preferred_element_type=jnp.float32)
        product = product.astype(jnp.bfloat16)
        own[:, span(k)] = product[:half]
        low[:, span(k)] = product[half : half + 2 * height]
        far_side[:, span(k)] = product[half + 2 * height : half + 3 * height]
        ref[:, span(k - first)] = product[half + 3 * height :]

    @pl.loop(0, steps)
    def _(k):
        give(k, far_across[0], 0)

    @pl.loop(steps, width // wide)
    def _(k):
        give(k, far_across[1], steps)


def step_width(width):
    return max(w for w in (128, 256, 512, 1024) if width % w == 0)


def experts(rows, weights, cut):
    height, width = rows[0].shape
    units = weights[0].shape[2]
    wide = step_width(width)
    total = len(rows) * height
    whole = pl.BlockSpec(memory_space=pltpu.VMEM)
    inputs = [pltpu.with_memory_space_constraint(v, pltpu.VMEM) for v in (*rows, *weights)]
    return pl.pallas_call(
        lambda *refs: expert_kernel(wide, *refs),
        in_specs=[whole] * len(inputs),
        out_specs=[whole] * 5,
        out_shape=[pltpu.VMEM((count * height, width), jnp.bfloat16) for count in (4, 2, 1)]
        + [pltpu.VMEM((height, part), jnp.bfloat16) for part in (cut, width - cut)],
        scratch_shapes=[
            pltpu.VMEM((total, units), jnp.float32),
            pltpu.VMEM((total, units), jnp.float32),
        ],
        compiler_params=pltpu.CompilerParams(vmem_limit_bytes=28 * 2**20),
        cost_estimate=pl.CostEstimate(
            flops=0,
            bytes_accessed=0,
            transcendentals=0,
        ),
    )(*inputs)


def body(
    queries,
    latent_cache,
    new_latent,
    parents,
    lengths,
    expert_input,
    routed_experts,
    route_weights,
    gate_weight,
    up_weight,
    down_weight,
):
    beam_count, width = expert_input.shape
    devices = lax.axis_size("dp")
    slices = FF_E // gate_weight.shape[2]
    expert_count = devices // slices
    route_count = routed_experts.shape[1]
    capacity = min(beam_count, max(2, 2 * beam_count * route_count // expert_count))
    dense = capacity == beam_count
    assert slices == 8 and expert_count & (expert_count - 1) == 0

    mine = lax.axis_index("dp") // slices
    turns = jnp.arange(expert_count, dtype=jnp.int32)
    targets = mine ^ turns
    if dense:
        blocks = [expert_input] * expert_count
        mixing = [
            jnp.sum(jnp.where(routed_experts == targets[r], route_weights, 0.0), axis=1)
            for r in range(expert_count)
        ]
    else:
        slots = pair_slots(routed_experts, expert_count, capacity)
        wanted = targets[:, None] * capacity + jnp.arange(capacity, dtype=jnp.int32)
        matches = (slots[:, :, None] == wanted.reshape(-1)).astype(jnp.float32)
        mixing = jnp.sum(route_weights[:, :, None] * matches, axis=1)
        selector = jnp.sum(matches, axis=1).T.astype(jnp.bfloat16)
        chosen = jnp.dot(selector, expert_input, preferred_element_type=jnp.float32)
        blocks = list(chosen.astype(jnp.bfloat16).reshape(expert_count, capacity, width))

    def ahead(r):
        return lambda i: i ^ (r * slices)

    def twin(i):
        return i ^ 1

    def first(i):
        return i ^ (2 if i & 1 else 4)

    def second(i):
        return i ^ (4 if i & 1 else 2)

    spans, pieces = [], []

    def cache_rows(kind, begin, end, ready=None):
        moves = {"early": EARLY, "late": LATE}[kind]
        source = latent_cache[begin:end]
        if ready is not None:
            source, ready = tied(source, ready)
        spans.append((kind, begin, end))
        return neighbours(source, moves, slices), ready

    column = blocks[:1] + [swapped(blocks[r], ahead(r)) for r in range(1, expert_count)]
    early, _ = cache_rows("early", 0, beam_count)
    height = expert_count * capacity
    rows = jnp.pad(column[0], ((0, height - capacity), (0, 0)))
    column = column[::-1]
    rows, column, early, mixing = tied(rows, column, early, mixing)
    column = column[::-1]
    pieces.append(early)
    for r in range(1, expert_count):
        rows = lax.dynamic_update_slice(rows, column[r], (r * capacity, 0))
    column = rows
    near = swapped(column, first)
    again, near = tied(column, near)
    across = swapped(near, second)
    side = swapped(again, second)
    beside = swapped(latent_cache, twin)
    twin_column, twin_near = swapped(column, twin), swapped(near, twin)
    weights = fetched([gate_weight, up_weight, down_weight])
    across, twin_column, twin_near, weights, beside = tied(
        across, twin_column, twin_near, weights, beside
    )
    late, across = cache_rows("late", 0, beam_count, across)
    held = [column, near, side, across, twin_column, twin_near]
    held = held + [swapped(side, twin), swapped(across, twin)]
    wide = step_width(width)
    cut = wide * max(1, 4 * (width // wide) // 7)
    own, low, far_side, *far_across = experts(held, weights, cut)
    far_across[1], far_side, low, late = tied(far_across[1], far_side, low, late)
    pieces.append(late)

    far_across = [swapped(value, twin) for value in far_across]
    far_side = swapped(far_side, twin)
    low = swapped(low, twin)
    height = expert_count * capacity

    halves = [(0, cut), (cut, width)]

    def block(value, j, half):
        return value[j * height : (j + 1) * height, half[0] : half[1]]

    def to_second(half):
        return added([block(own, 3, half), far_across[half[0] > 0]]).astype(jnp.bfloat16)

    def to_first(half, across):
        return added([block(own, 1, half), block(low, 1, half), across]).astype(jnp.bfloat16)

    def to_side(half):
        return added([block(own, 2, half), block(far_side, 0, half)]).astype(jnp.bfloat16)

    def shares(half, side, near):
        here = [block(own, 0, half), block(low, 0, half), side, near]
        return [
            added([v[r * capacity : (r + 1) * capacity] for v in here])
            for r in range(expert_count)
        ]

    def back(share):
        sent = [
            swapped(share[r].astype(jnp.bfloat16), ahead(r))
            for r in reversed(range(1, expert_count))
        ]
        return sent[::-1]

    across, pieces[1] = tied(to_second(halves[0]), pieces[1])
    across = swapped(across, second)
    attention = attend(
        queries, latent_cache, beside, new_latent, spans, pieces, parents, lengths
    )
    across, attention = tied(across, attention)
    near, side = to_first(halves[0], across), to_side(halves[0])
    near, across = tied(near, to_second(halves[1]))
    near, side, across = swapped(near, first), swapped(side, second), swapped(across, second)
    share = shares(halves[0], side, near)
    share, across, far_side = tied(share, across, far_side)
    values = [[share[0]] + back(share)]
    near, side = to_first(halves[1], across), to_side(halves[1])
    near, side = swapped(near, first), swapped(side, second)
    share = shares(halves[1], side, near)
    values.append([share[0]] + back(share))
    totals = []
    for value in values:
        value = [v.astype(jnp.float32) for v in value]
        if dense:
            order = [0, *range(expert_count - 1, 0, -1)]
            total = sum(mixing[r][:, None] * value[r] for r in order)
        else:
            total = jnp.dot(
                mixing,
                jnp.concatenate(value),
                precision=lax.Precision.HIGHEST,
                preferred_element_type=jnp.float32,
            )
        totals.append(total.astype(jnp.bfloat16))
    expert_output = jnp.concatenate(totals, axis=1)
    return (attention, expert_output)


def solution(mesh):
    in_specs = (
        P(("groups", "dp"), None, None),
        P(("groups", "dp"), None, None),
        P(("groups", "dp"), None),
        P(("groups", "dp")),
        P(("groups", "dp")),
        P(("groups", "dp"), None),
        P(("groups", "dp"), None),
        P(("groups", "dp"), None),
        P("dp", None, None),
        P("dp", None, None),
        P("dp", None, None),
    )
    out_specs = (P(("groups", "dp"), None, None), P(("groups", "dp"), None))
    return jax.shard_map(body, mesh=mesh, in_specs=in_specs, out_specs=out_specs, check_vma=False)
```

```python
import jax
import jax.numpy as jnp
from jax import lax
from jax.experimental import pallas as pl
from jax.experimental.pallas import tpu as pltpu
from jax.sharding import PartitionSpec as P

FF_E = 2048
KV = 512


score_scale = 192.0 ** (-0.5)


def pair_slots(route_rows, expert_count, capacity):
    flat_experts = route_rows.reshape(-1)
    onehot = (flat_experts[:, None] == jnp.arange(expert_count, dtype=jnp.int32)[None, :]).astype(
        jnp.int32
    )
    position = jnp.sum((jnp.cumsum(onehot, axis=0) - onehot) * onehot, axis=1)
    return (flat_experts * capacity + position).astype(jnp.int32).reshape(route_rows.shape)


def swapped(value, partner):
    peers = lax.axis_size("dp")
    return lax.ppermute(value, "dp", [(i, partner(i)) for i in range(peers)])


def tied(*values):
    return lax.optimization_barrier(values)


def added(values):
    total = values[0].astype(jnp.float32)
    for value in values[1:]:
        total = total + value.astype(jnp.float32)
    return total


EARLY = ((1, 2), (3, 4), (5, 6), (6, 5))
LATE = ((2, 1), (4, 3), (7, 8), (8, 7))


def neighbours(value, moves, slices):
    peers = lax.axis_size("dp")
    pairs = [(base + i, base + j) for base in range(0, peers, slices) for i, j in moves]
    return lax.ppermute(value, "dp", [p for p in pairs if max(p) < peers])


def attend_kernel(spans, parents, lengths, query, own, twin, newest, *refs):
    pieces, out = refs[:-1], refs[-1]
    beams = range(query.shape[0])
    rank = lax.axis_index("dp")
    place = rank % 8
    arrives_early = (place == 2) | (place == 4) | (place == 5) | (place == 6)
    latest = newest[...].astype(jnp.float32)
    at = lax.broadcasted_iota(jnp.int32, own.shape[1:], 0)
    rows, scores, probs = [], [], []
    for b in beams:
        slot, holder = parents[b] % len(beams), parents[b] // len(beams)
        value = own[slot]
        value = jnp.where(holder == (rank ^ 1), twin[slot], value)
        far = (holder != rank) & (holder != (rank ^ 1))
        for (kind, low, high), piece in zip(spans, pieces):
            here = far & (slot >= low) & (slot < high)
            if kind == "early":
                here = here & arrives_early
            if kind == "late":
                here = here & jnp.logical_not(arrives_early)
            value = jnp.where(here, piece[jnp.clip(slot - low, 0, high - low - 1)], value)
        value = jnp.where(at < lengths[b] - 1, value, jnp.zeros_like(value))
        row = jnp.broadcast_to(latest[b : b + 1], value.shape).astype(value.dtype)
        rows.append(jnp.where(at == lengths[b] - 1, row, value))
    for b in beams:
        product = lax.dot_general(
            query[b], rows[b], (((1,), (1,)), ((), ())), preferred_element_type=jnp.float32
        )
        scores.append(product * score_scale)
    at = lax.broadcasted_iota(jnp.int32, scores[0].shape, 1)
    for b in beams:
        value = jnp.where(at < lengths[b], scores[b], -jnp.inf)
        expons = jnp.exp(value - jnp.max(value, axis=1, keepdims=True))
        total = jnp.sum(expons, axis=1, keepdims=True)
        probs.append((expons / total).astype(jnp.bfloat16))
    for b in beams:
        mixed = jnp.dot(probs[b], rows[b][:, :KV], preferred_element_type=jnp.float32)
        out[b] = mixed.astype(out.dtype)


def attend(queries, own, twin, newest, spans, pieces, parents, lengths):
    beam_count, heads, width = queries.shape
    positions = own.shape[1]
    scalars = pl.BlockSpec(memory_space=pltpu.SMEM)
    whole = pl.BlockSpec(memory_space=pltpu.VMEM)
    arrays = [
        pltpu.with_memory_space_constraint(v, pltpu.VMEM)
        for v in (queries, own, twin, newest, *pieces)
    ]
    return pl.pallas_call(
        lambda *refs: attend_kernel(spans, *refs),
        in_specs=[scalars] * 2 + [whole] * len(arrays),
        out_specs=whole,
        out_shape=jax.ShapeDtypeStruct((beam_count, heads, KV), jnp.bfloat16),
        compiler_params=pltpu.CompilerParams(vmem_limit_bytes=16 * 2**20),
        cost_estimate=pl.CostEstimate(
            flops=2 * beam_count * heads * positions * (width + KV),
            bytes_accessed=2 * beam_count * (4 * positions * width + heads * (width + KV)),
            transcendentals=beam_count * heads * positions,
        ),
    )(parents, lengths, *arrays)


def fetch_kernel(*refs):
    count = len(refs) // 2
    sources, targets, sems = refs[:count], refs[count:-1], refs[-1]
    copies = [
        pltpu.make_async_copy(source, target, sems.at[i])
        for i, (source, target) in enumerate(zip(sources, targets))
    ]
    for copy in copies:
        copy.start()
    for copy in copies:
        copy.wait()


def fetched(weights):
    return pl.pallas_call(
        fetch_kernel,
        in_specs=[pl.BlockSpec(memory_space=pltpu.HBM)] * len(weights),
        out_specs=[pl.BlockSpec(memory_space=pltpu.VMEM)] * len(weights),
        out_shape=[pltpu.VMEM(w.shape, w.dtype) for w in weights],
        scratch_shapes=[pltpu.SemaphoreType.DMA((len(weights),))],
        compiler_params=pltpu.CompilerParams(vmem_limit_bytes=16 * 2**20),
        cost_estimate=pl.CostEstimate(
            flops=0,
            bytes_accessed=2 * sum(w.size * w.dtype.itemsize for w in weights),
            transcendentals=0,
        ),
    )(*[pltpu.with_memory_space_constraint(w, pltpu.HBM) for w in weights])


def expert_kernel(wide, *refs):
    rows, refs = refs[:8], refs[8:]
    gate, up, down, own, low, far_side, *far_across, gate_sum, up_sum = refs
    height, width = rows[0].shape
    half = 4 * height

    def span(k):
        return pl.ds(pl.multiple_of(k * wide, wide), wide)

    gate_sum[...] = jnp.zeros_like(gate_sum)
    up_sum[...] = jnp.zeros_like(up_sum)

    @pl.loop(0, width // wide)
    def _(k):
        piece = jnp.concatenate([ref[:, span(k)] for ref in rows], axis=0)
        gate_sum[...] += jnp.dot(piece, gate[0, span(k), :], preferred_element_type=jnp.float32)
        up_sum[...] += jnp.dot(piece, up[0, span(k), :], preferred_element_type=jnp.float32)

    total = gate_sum[...]
    hidden = (total / (1.0 + jnp.exp(-total)) * up_sum[...]).astype(jnp.bfloat16)

    steps = far_across[0].shape[1] // wide

    def give(k, ref, first):
        product = jnp.dot(hidden, down[0, :, span(k)], preferred_element_type=jnp.float32)
        product = product.astype(jnp.bfloat16)
        own[:, span(k)] = product[:half]
        low[:, span(k)] = product[half : half + 2 * height]
        far_side[:, span(k)] = product[half + 2 * height : half + 3 * height]
        ref[:, span(k - first)] = product[half + 3 * height :]

    @pl.loop(0, steps)
    def _(k):
        give(k, far_across[0], 0)

    @pl.loop(steps, width // wide)
    def _(k):
        give(k, far_across[1], steps)


def step_width(width):
    return max(w for w in (128, 256, 512, 1024) if width % w == 0)


def experts(rows, weights, cut):
    height, width = rows[0].shape
    units = weights[0].shape[2]
    wide = step_width(width)
    total = len(rows) * height
    whole = pl.BlockSpec(memory_space=pltpu.VMEM)
    inputs = [pltpu.with_memory_space_constraint(v, pltpu.VMEM) for v in (*rows, *weights)]
    return pl.pallas_call(
        lambda *refs: expert_kernel(wide, *refs),
        in_specs=[whole] * len(inputs),
        out_specs=[whole] * 5,
        out_shape=[pltpu.VMEM((count * height, width), jnp.bfloat16) for count in (4, 2, 1)]
        + [pltpu.VMEM((height, part), jnp.bfloat16) for part in (cut, width - cut)],
        scratch_shapes=[
            pltpu.VMEM((total, units), jnp.float32),
            pltpu.VMEM((total, units), jnp.float32),
        ],
        compiler_params=pltpu.CompilerParams(vmem_limit_bytes=28 * 2**20),
        cost_estimate=pl.CostEstimate(
            flops=0,
            bytes_accessed=0,
            transcendentals=0,
        ),
    )(*inputs)


def body(
    queries,
    latent_cache,
    new_latent,
    parents,
    lengths,
    expert_input,
    routed_experts,
    route_weights,
    gate_weight,
    up_weight,
    down_weight,
):
    beam_count, width = expert_input.shape
    devices = lax.axis_size("dp")
    slices = FF_E // gate_weight.shape[2]
    expert_count = devices // slices
    route_count = routed_experts.shape[1]
    capacity = min(beam_count, max(2, 2 * beam_count * route_count // expert_count))
    dense = capacity == beam_count
    assert slices == 8 and expert_count & (expert_count - 1) == 0

    mine = lax.axis_index("dp") // slices
    turns = jnp.arange(expert_count, dtype=jnp.int32)
    targets = mine ^ turns
    if dense:
        blocks = [expert_input] * expert_count
        mixing = [
            jnp.sum(jnp.where(routed_experts == targets[r], route_weights, 0.0), axis=1)
            for r in range(expert_count)
        ]
    else:
        slots = pair_slots(routed_experts, expert_count, capacity)
        wanted = targets[:, None] * capacity + jnp.arange(capacity, dtype=jnp.int32)
        matches = (slots[:, :, None] == wanted.reshape(-1)).astype(jnp.float32)
        mixing = jnp.sum(route_weights[:, :, None] * matches, axis=1)
        selector = jnp.sum(matches, axis=1).T.astype(jnp.bfloat16)
        chosen = jnp.dot(selector, expert_input, preferred_element_type=jnp.float32)
        blocks = list(chosen.astype(jnp.bfloat16).reshape(expert_count, capacity, width))

    def ahead(r):
        return lambda i: i ^ (r * slices)

    def twin(i):
        return i ^ 1

    def first(i):
        return i ^ (2 if i & 1 else 4)

    def second(i):
        return i ^ (4 if i & 1 else 2)

    spans, pieces = [], []

    def cache_rows(kind, begin, end, ready=None):
        moves = {"early": EARLY, "late": LATE}[kind]
        source = latent_cache[begin:end]
        if ready is not None:
            source, ready = tied(source, ready)
        spans.append((kind, begin, end))
        return neighbours(source, moves, slices), ready

    column = blocks[:1] + [swapped(blocks[r], ahead(r)) for r in range(1, expert_count)]
    early, _ = cache_rows("early", 0, beam_count)
    height = expert_count * capacity
    rows = jnp.pad(column[0], ((0, height - capacity), (0, 0)))
    column = column[::-1]
    rows, column, early, mixing = tied(rows, column, early, mixing)
    column = column[::-1]
    pieces.append(early)
    for r in range(1, expert_count):
        rows = lax.dynamic_update_slice(rows, column[r], (r * capacity, 0))
    column = rows
    near = swapped(column, first)
    again, near = tied(column, near)
    across = swapped(near, second)
    side = swapped(again, second)
    beside = swapped(latent_cache, twin)
    twin_column, twin_near = swapped(column, twin), swapped(near, twin)
    weights = fetched([gate_weight, up_weight, down_weight])
    across, twin_column, twin_near, weights, beside = tied(
        across, twin_column, twin_near, weights, beside
    )
    late, across = cache_rows("late", 0, beam_count, across)
    held = [column, near, side, across, twin_column, twin_near]
    held = held + [swapped(side, twin), swapped(across, twin)]
    wide = step_width(width)
    cut = wide * max(1, 4 * (width // wide) // 7)
    own, low, far_side, *far_across = experts(held, weights, cut)
    far_side, low, late = tied(far_side, low, late)
    pieces.append(late)

    far_across = [swapped(value, twin) for value in far_across]
    far_side = swapped(far_side, twin)
    low = swapped(low, twin)
    height = expert_count * capacity

    halves = [(0, cut), (cut, width)]

    def block(value, j, half):
        return value[j * height : (j + 1) * height, half[0] : half[1]]

    def to_second(half):
        return added([block(own, 3, half), far_across[half[0] > 0]]).astype(jnp.bfloat16)

    def to_first(half, across):
        return added([block(own, 1, half), block(low, 1, half), across]).astype(jnp.bfloat16)

    def to_side(half):
        return added([block(own, 2, half), block(far_side, 0, half)]).astype(jnp.bfloat16)

    def shares(half, side, near):
        here = [block(own, 0, half), block(low, 0, half), side, near]
        return [
            added([v[r * capacity : (r + 1) * capacity] for v in here])
            for r in range(expert_count)
        ]

    def back(share):
        sent = [
            swapped(share[r].astype(jnp.bfloat16), ahead(r))
            for r in reversed(range(1, expert_count))
        ]
        return sent[::-1]

    across, pieces[1] = tied(to_second(halves[0]), pieces[1])
    across = swapped(across, second)
    attention = attend(
        queries, latent_cache, beside, new_latent, spans, pieces, parents, lengths
    )
    across, attention = tied(across, attention)
    near, side = to_first(halves[0], across), to_side(halves[0])
    near, across = tied(near, to_second(halves[1]))
    near, side, across = swapped(near, first), swapped(side, second), swapped(across, second)
    share = shares(halves[0], side, near)
    share, across, far_side = tied(share, across, far_side)
    values = [[share[0]] + back(share)]
    near, side = to_first(halves[1], across), to_side(halves[1])
    near, side = swapped(near, first), swapped(side, second)
    share = shares(halves[1], side, near)
    values.append([share[0]] + back(share))
    totals = []
    for value in values:
        value = [v.astype(jnp.float32) for v in value]
        if dense:
            order = [0, *range(expert_count - 1, 0, -1)]
            total = sum(mixing[r][:, None] * value[r] for r in order)
        else:
            total = jnp.dot(
                mixing,
                jnp.concatenate(value),
                precision=lax.Precision.HIGHEST,
                preferred_element_type=jnp.float32,
            )
        totals.append(total.astype(jnp.bfloat16))
    expert_output = jnp.concatenate(totals, axis=1)
    return (attention, expert_output)


def solution(mesh):
    in_specs = (
        P(("groups", "dp"), None, None),
        P(("groups", "dp"), None, None),
        P(("groups", "dp"), None),
        P(("groups", "dp")),
        P(("groups", "dp")),
        P(("groups", "dp"), None),
        P(("groups", "dp"), None),
        P(("groups", "dp"), None),
        P("dp", None, None),
        P("dp", None, None),
        P("dp", None, None),
    )
    out_specs = (P(("groups", "dp"), None, None), P(("groups", "dp"), None))
    return jax.shard_map(body, mesh=mesh, in_specs=in_specs, out_specs=out_specs, check_vma=False)
```

```python
import jax
import jax.numpy as jnp
from jax import lax
from jax.experimental import pallas as pl
from jax.experimental.pallas import tpu as pltpu
from jax.sharding import PartitionSpec as P

FF_E = 2048
KV = 512


score_scale = 192.0 ** (-0.5)


def pair_slots(route_rows, expert_count, capacity):
    flat_experts = route_rows.reshape(-1)
    onehot = (flat_experts[:, None] == jnp.arange(expert_count, dtype=jnp.int32)[None, :]).astype(
        jnp.int32
    )
    position = jnp.sum((jnp.cumsum(onehot, axis=0) - onehot) * onehot, axis=1)
    return (flat_experts * capacity + position).astype(jnp.int32).reshape(route_rows.shape)


def swapped(value, partner):
    peers = lax.axis_size("dp")
    return lax.ppermute(value, "dp", [(i, partner(i)) for i in range(peers)])


def tied(*values):
    return lax.optimization_barrier(values)


def added(values):
    total = values[0].astype(jnp.float32)
    for value in values[1:]:
        total = total + value.astype(jnp.float32)
    return total


EARLY = ((1, 2), (3, 4), (5, 6), (6, 5))
LATE = ((2, 1), (4, 3), (7, 8), (8, 7))


def neighbours(value, moves, slices):
    peers = lax.axis_size("dp")
    pairs = [(base + i, base + j) for base in range(0, peers, slices) for i, j in moves]
    return lax.ppermute(value, "dp", [p for p in pairs if max(p) < peers])


def attend_kernel(spans, parents, lengths, query, own, twin, newest, *refs):
    pieces, out = refs[:-1], refs[-1]
    beams = range(query.shape[0])
    rank = lax.axis_index("dp")
    place = rank % 8
    arrives_early = (place == 2) | (place == 4) | (place == 5) | (place == 6)
    latest = newest[...].astype(jnp.float32)
    at = lax.broadcasted_iota(jnp.int32, own.shape[1:], 0)
    rows, scores, probs = [], [], []
    for b in beams:
        slot, holder = parents[b] % len(beams), parents[b] // len(beams)
        value = own[slot]
        value = jnp.where(holder == (rank ^ 1), twin[slot], value)
        far = (holder != rank) & (holder != (rank ^ 1))
        for (kind, low, high), piece in zip(spans, pieces):
            here = far & (slot >= low) & (slot < high)
            if kind == "early":
                here = here & arrives_early
            if kind == "late":
                here = here & jnp.logical_not(arrives_early)
            value = jnp.where(here, piece[jnp.clip(slot - low, 0, high - low - 1)], value)
        value = jnp.where(at < lengths[b] - 1, value, jnp.zeros_like(value))
        row = jnp.broadcast_to(latest[b : b + 1], value.shape).astype(value.dtype)
        rows.append(jnp.where(at == lengths[b] - 1, row, value))
    for b in beams:
        product = lax.dot_general(
            query[b], rows[b], (((1,), (1,)), ((), ())), preferred_element_type=jnp.float32
        )
        scores.append(product * score_scale)
    at = lax.broadcasted_iota(jnp.int32, scores[0].shape, 1)
    for b in beams:
        value = jnp.where(at < lengths[b], scores[b], -jnp.inf)
        expons = jnp.exp(value - jnp.max(value, axis=1, keepdims=True))
        total = jnp.sum(expons, axis=1, keepdims=True)
        probs.append((expons / total).astype(jnp.bfloat16))
    for b in beams:
        mixed = jnp.dot(probs[b], rows[b][:, :KV], preferred_element_type=jnp.float32)
        out[b] = mixed.astype(out.dtype)


def attend(queries, own, twin, newest, spans, pieces, parents, lengths):
    beam_count, heads, width = queries.shape
    positions = own.shape[1]
    scalars = pl.BlockSpec(memory_space=pltpu.SMEM)
    whole = pl.BlockSpec(memory_space=pltpu.VMEM)
    arrays = [
        pltpu.with_memory_space_constraint(v, pltpu.VMEM)
        for v in (queries, own, twin, newest, *pieces)
    ]
    return pl.pallas_call(
        lambda *refs: attend_kernel(spans, *refs),
        in_specs=[scalars] * 2 + [whole] * len(arrays),
        out_specs=whole,
        out_shape=jax.ShapeDtypeStruct((beam_count, heads, KV), jnp.bfloat16),
        compiler_params=pltpu.CompilerParams(vmem_limit_bytes=16 * 2**20),
        cost_estimate=pl.CostEstimate(
            flops=2 * beam_count * heads * positions * (width + KV),
            bytes_accessed=2 * beam_count * (4 * positions * width + heads * (width + KV)),
            transcendentals=beam_count * heads * positions,
        ),
    )(parents, lengths, *arrays)


def fetch_kernel(*refs):
    count = len(refs) // 2
    sources, targets, sems = refs[:count], refs[count:-1], refs[-1]
    copies = [
        pltpu.make_async_copy(source, target, sems.at[i])
        for i, (source, target) in enumerate(zip(sources, targets))
    ]
    for copy in copies:
        copy.start()
    for copy in copies:
        copy.wait()


def fetched(weights):
    return pl.pallas_call(
        fetch_kernel,
        in_specs=[pl.BlockSpec(memory_space=pltpu.HBM)] * len(weights),
        out_specs=[pl.BlockSpec(memory_space=pltpu.VMEM)] * len(weights),
        out_shape=[pltpu.VMEM(w.shape, w.dtype) for w in weights],
        scratch_shapes=[pltpu.SemaphoreType.DMA((len(weights),))],
        compiler_params=pltpu.CompilerParams(vmem_limit_bytes=16 * 2**20),
        cost_estimate=pl.CostEstimate(
            flops=0,
            bytes_accessed=2 * sum(w.size * w.dtype.itemsize for w in weights),
            transcendentals=0,
        ),
    )(*[pltpu.with_memory_space_constraint(w, pltpu.HBM) for w in weights])


def expert_kernel(wide, *refs):
    rows, refs = refs[:8], refs[8:]
    gate, up, down, own, low, far_side, *far_across, gate_sum, up_sum = refs
    height, width = rows[0].shape
    half = 4 * height

    def span(k):
        return pl.ds(pl.multiple_of(k * wide, wide), wide)

    gate_sum[...] = jnp.zeros_like(gate_sum)
    up_sum[...] = jnp.zeros_like(up_sum)

    @pl.loop(0, width // wide, unroll=True)
    def _(k):
        piece = jnp.concatenate([ref[:, span(k)] for ref in rows], axis=0)
        gate_sum[...] += jnp.dot(piece, gate[0, span(k), :], preferred_element_type=jnp.float32)
        up_sum[...] += jnp.dot(piece, up[0, span(k), :], preferred_element_type=jnp.float32)

    total = gate_sum[...]
    hidden = (total / (1.0 + jnp.exp(-total)) * up_sum[...]).astype(jnp.bfloat16)

    steps = far_across[0].shape[1] // wide

    def give(k, ref, first):
        product = jnp.dot(hidden, down[0, :, span(k)], preferred_element_type=jnp.float32)
        product = product.astype(jnp.bfloat16)
        own[:, span(k)] = product[:half]
        low[:, span(k)] = product[half : half + 2 * height]
        far_side[:, span(k)] = product[half + 2 * height : half + 3 * height]
        ref[:, span(k - first)] = product[half + 3 * height :]

    @pl.loop(0, steps, unroll=True)
    def _(k):
        give(k, far_across[0], 0)

    @pl.loop(steps, width // wide, unroll=True)
    def _(k):
        give(k, far_across[1], steps)


def step_width(width):
    return max(w for w in (128, 256, 512, 1024) if width % w == 0)


def experts(rows, weights, cut):
    height, width = rows[0].shape
    units = weights[0].shape[2]
    wide = step_width(width)
    total = len(rows) * height
    whole = pl.BlockSpec(memory_space=pltpu.VMEM)
    inputs = [pltpu.with_memory_space_constraint(v, pltpu.VMEM) for v in (*rows, *weights)]
    return pl.pallas_call(
        lambda *refs: expert_kernel(wide, *refs),
        in_specs=[whole] * len(inputs),
        out_specs=[whole] * 5,
        out_shape=[pltpu.VMEM((count * height, width), jnp.bfloat16) for count in (4, 2, 1)]
        + [pltpu.VMEM((height, part), jnp.bfloat16) for part in (cut, width - cut)],
        scratch_shapes=[
            pltpu.VMEM((total, units), jnp.float32),
            pltpu.VMEM((total, units), jnp.float32),
        ],
        compiler_params=pltpu.CompilerParams(vmem_limit_bytes=28 * 2**20),
        cost_estimate=pl.CostEstimate(
            flops=0,
            bytes_accessed=0,
            transcendentals=0,
        ),
    )(*inputs)


def body(
    queries,
    latent_cache,
    new_latent,
    parents,
    lengths,
    expert_input,
    routed_experts,
    route_weights,
    gate_weight,
    up_weight,
    down_weight,
):
    beam_count, width = expert_input.shape
    devices = lax.axis_size("dp")
    slices = FF_E // gate_weight.shape[2]
    expert_count = devices // slices
    route_count = routed_experts.shape[1]
    capacity = min(beam_count, max(2, 2 * beam_count * route_count // expert_count))
    dense = capacity == beam_count
    assert slices == 8 and expert_count & (expert_count - 1) == 0

    mine = lax.axis_index("dp") // slices
    turns = jnp.arange(expert_count, dtype=jnp.int32)
    targets = mine ^ turns
    if dense:
        blocks = [expert_input] * expert_count
        mixing = [
            jnp.sum(jnp.where(routed_experts == targets[r], route_weights, 0.0), axis=1)
            for r in range(expert_count)
        ]
    else:
        slots = pair_slots(routed_experts, expert_count, capacity)
        wanted = targets[:, None] * capacity + jnp.arange(capacity, dtype=jnp.int32)
        matches = (slots[:, :, None] == wanted.reshape(-1)).astype(jnp.float32)
        mixing = jnp.sum(route_weights[:, :, None] * matches, axis=1)
        selector = jnp.sum(matches, axis=1).T.astype(jnp.bfloat16)
        chosen = jnp.dot(selector, expert_input, preferred_element_type=jnp.float32)
        blocks = list(chosen.astype(jnp.bfloat16).reshape(expert_count, capacity, width))

    def ahead(r):
        return lambda i: i ^ (r * slices)

    def twin(i):
        return i ^ 1

    def first(i):
        return i ^ (2 if i & 1 else 4)

    def second(i):
        return i ^ (4 if i & 1 else 2)

    spans, pieces = [], []

    def cache_rows(kind, begin, end, ready=None):
        moves = {"early": EARLY, "late": LATE}[kind]
        source = latent_cache[begin:end]
        if ready is not None:
            source, ready = tied(source, ready)
        spans.append((kind, begin, end))
        return neighbours(source, moves, slices), ready

    column = blocks[:1] + [swapped(blocks[r], ahead(r)) for r in range(1, expert_count)]
    early, _ = cache_rows("early", 0, beam_count)
    height = expert_count * capacity
    rows = jnp.pad(column[0], ((0, height - capacity), (0, 0)))
    column = column[::-1]
    rows, column, early, mixing = tied(rows, column, early, mixing)
    column = column[::-1]
    pieces.append(early)
    for r in range(1, expert_count):
        rows = lax.dynamic_update_slice(rows, column[r], (r * capacity, 0))
    column = rows
    near = swapped(column, first)
    again, near = tied(column, near)
    across = swapped(near, second)
    side = swapped(again, second)
    beside = swapped(latent_cache, twin)
    twin_column, twin_near = swapped(column, twin), swapped(near, twin)
    weights = fetched([gate_weight, up_weight, down_weight])
    across, twin_column, twin_near, weights, beside = tied(
        across, twin_column, twin_near, weights, beside
    )
    late, across = cache_rows("late", 0, beam_count, across)
    held = [column, near, side, across, twin_column, twin_near]
    held = held + [swapped(side, twin), swapped(across, twin)]
    wide = step_width(width)
    cut = wide * max(1, 4 * (width // wide) // 7)
    own, low, far_side, *far_across = experts(held, weights, cut)
    far_across[1], far_side, low, late = tied(far_across[1], far_side, low, late)
    pieces.append(late)

    far_across = [swapped(value, twin) for value in far_across]
    far_side = swapped(far_side, twin)
    low = swapped(low, twin)
    height = expert_count * capacity

    halves = [(0, cut), (cut, width)]

    def block(value, j, half):
        return value[j * height : (j + 1) * height, half[0] : half[1]]

    def to_second(half):
        return added([block(own, 3, half), far_across[half[0] > 0]]).astype(jnp.bfloat16)

    def to_first(half, across):
        return added([block(own, 1, half), block(low, 1, half), across]).astype(jnp.bfloat16)

    def to_side(half):
        return added([block(own, 2, half), block(far_side, 0, half)]).astype(jnp.bfloat16)

    def shares(half, side, near):
        here = [block(own, 0, half), block(low, 0, half), side, near]
        return [
            added([v[r * capacity : (r + 1) * capacity] for v in here])
            for r in range(expert_count)
        ]

    def back(share):
        sent = [
            swapped(share[r].astype(jnp.bfloat16), ahead(r))
            for r in reversed(range(1, expert_count))
        ]
        return sent[::-1]

    across, pieces[1] = tied(to_second(halves[0]), pieces[1])
    across = swapped(across, second)
    attention = attend(
        queries, latent_cache, beside, new_latent, spans, pieces, parents, lengths
    )
    across, attention = tied(across, attention)
    near, side = to_first(halves[0], across), to_side(halves[0])
    near, across = tied(near, to_second(halves[1]))
    near, side, across = swapped(near, first), swapped(side, second), swapped(across, second)
    share = shares(halves[0], side, near)
    share, across, far_side = tied(share, across, far_side)
    values = [[share[0]] + back(share)]
    near, side = to_first(halves[1], across), to_side(halves[1])
    near, side = swapped(near, first), swapped(side, second)
    share = shares(halves[1], side, near)
    values.append([share[0]] + back(share))
    totals = []
    for value in values:
        value = [v.astype(jnp.float32) for v in value]
        if dense:
            order = [0, *range(expert_count - 1, 0, -1)]
            total = sum(mixing[r][:, None] * value[r] for r in order)
        else:
            total = jnp.dot(
                mixing,
                jnp.concatenate(value),
                precision=lax.Precision.HIGHEST,
                preferred_element_type=jnp.float32,
            )
        totals.append(total.astype(jnp.bfloat16))
    expert_output = jnp.concatenate(totals, axis=1)
    return (attention, expert_output)


def solution(mesh):
    in_specs = (
        P(("groups", "dp"), None, None),
        P(("groups", "dp"), None, None),
        P(("groups", "dp"), None),
        P(("groups", "dp")),
        P(("groups", "dp")),
        P(("groups", "dp"), None),
        P(("groups", "dp"), None),
        P(("groups", "dp"), None),
        P("dp", None, None),
        P("dp", None, None),
        P("dp", None, None),
    )
    out_specs = (P(("groups", "dp"), None, None), P(("groups", "dp"), None))
    return jax.shard_map(body, mesh=mesh, in_specs=in_specs, out_specs=out_specs, check_vma=False)
```
